32 devices in a mesh: gx: 8 (over z, x), gy: 4 (over y, core).
Axes of the slice: x: 2, y: 2, z: 4, core: 2. Of those that a mesh axis runs over, the one named last changes fastest.
Arguments:
- field: bfloat16 [20, 64, 64, 256], P(None, 'gx', 'gy'), may hold values from -6 to 6
- cotangent: bfloat16 [20, 64, 64, 256], P(None, 'gx', 'gy'), may hold values from -6 to 6
- spectral_weight: bfloat16 [2, 20, 20, 24, 2304], P(None, None, None, 'gy', 'gx'), may hold values from -6 to 6
- pointwise_weight: bfloat16 [20, 20], replicated, may hold values from -1.25 to 1.25
- bias: float32 [20], replicated, may hold values from -1 to 1
Outputs:
- output: bfloat16 [20, 64, 64, 256], P(None, 'gx', 'gy')
- grad_field: bfloat16 [20, 64, 64, 256], P(None, 'gx', 'gy')
- grad_spectral: float32 [2, 20, 20, 24, 2304], P(None, None, None, 'gy', 'gx')
- grad_pointwise: float32 [20, 20], replicated
- grad_bias: float32 [20], replicated
The draws below stay inside these ranges and needn't reach their ends.
All inputs are finite; a program needn't handle non-finite values.
Results may differ from the reference program's by a relative error of at most 0.0013.
Values sent between devices are 32-bit elements; how exact they have to be, the bound alone decides.
No kernel may reach another device: no remote copies, remote signals or barrier semaphores. Data moves between devices by JAX's collectives and lax.ppermute only.
A program may use at most 128 MiB of HBM per device.

```python
import math
import jax
import jax.numpy as jnp
from jax import lax

C = 20
MX = 24
MY = 24
MZ = 24
NZ = 256
CX = 8
NX = 64
NY = 64
PAIRS = 2304


def levels(rng, shape, pieces, smallest, high):
    factor_of, own = 1.0, jax.random.fold_in(rng, 6)
    for axis_at, blocks in pieces:
        heights = jnp.exp(jax.random.uniform(jax.random.fold_in(own, axis_at), (blocks,), jnp.float32, smallest / len(pieces), high / len(pieces)))
        factor_of = factor_of * jnp.repeat(heights, shape[axis_at] // blocks).reshape([-1 if axis == axis_at else 1 for axis in range(len(shape))])
    return factor_of


def scatter_about(key, shape, scale, most, cuts=(), kind=jnp.bfloat16):
    array = jax.random.normal(key, shape, jnp.float32) * scale
    if len(cuts) > 0:
        array = levels(key, shape, cuts, -0.22, 0.18) * array
    return jnp.clip(array, min=-most, max=most).astype(kind)


def setup_inputs(seed: int = 0) -> dict:
    key_of = jax.random.split(jax.random.key(seed), 6)
    field = scatter_about(key_of[0], (C, NX, NY, NZ), 1.0, 6.0, ((1, 8), (2, 4)))
    cotangent = scatter_about(key_of[1], (C, NX, NY, NZ), 1.0, 6.0, ((1, 8), (2, 4)))
    spectral_weight = scatter_about(key_of[2], (2, C, C, MZ, PAIRS), 1.0, 6.0, ((3, 4), (4, 8)))
    pointwise_weight = scatter_about(key_of[3], (C, C), C ** -0.5, 1.25)
    bias = jnp.clip(jax.random.uniform(key_of[4], (C,), jnp.float32, -1.0, 1.0), -1.0, 1.0)
    return dict(field=field, cotangent=cotangent, spectral_weight=spectral_weight, pointwise_weight=pointwise_weight, bias=bias)


PRECISE = lax.Precision.HIGHEST
TWO_PI = 2.0 * math.pi

def angles(frequencies, places, length):
    product = places[:, None] * frequencies[None, :] % length
    return product.astype(jnp.float32) * (TWO_PI / length)

def frequency(position, kept_modes, length):
    return jnp.where(position < kept_modes, position, position - 2 * kept_modes + length).astype(jnp.int32)

def forward_y(values, phases):
    cosine_table = jnp.cos(phases)
    sine_table = jnp.sin(phases)
    with_cos = jnp.einsum('cxymr,yj->cxjmr', values, cosine_table, precision=PRECISE)
    with_sin = jnp.einsum('cxymr,yj->cxjmr', values, sine_table, precision=PRECISE)
    real_part = with_cos[..., 0] + with_sin[..., 1]
    imag_part = with_cos[..., 1] - with_sin[..., 0]
    return jnp.stack([real_part, imag_part], axis=-1)

def inverse_y(values, phases):
    cosine_table = jnp.cos(phases)
    sine_table = jnp.sin(phases)
    with_cos = jnp.einsum('cxjmr,yj->cxymr', values, cosine_table, precision=PRECISE)
    with_sin = jnp.einsum('cxjmr,yj->cxymr', values, sine_table, precision=PRECISE)
    real_part = with_cos[..., 0] - with_sin[..., 1]
    imag_part = with_sin[..., 0] + with_cos[..., 1]
    return jnp.stack([real_part, imag_part], axis=-1)

def forward_x(values, phases):
    cosine_table = jnp.cos(phases)
    sine_table = jnp.sin(phases)
    real_part = jnp.einsum('cxjm,xi->cijm', values[..., 0], cosine_table, precision=PRECISE) + jnp.einsum('cxjm,xi->cijm', values[..., 1], sine_table, precision=PRECISE)
    imag_part = jnp.einsum('cxjm,xi->cijm', values[..., 1], cosine_table, precision=PRECISE) - jnp.einsum('cxjm,xi->cijm', values[..., 0], sine_table, precision=PRECISE)
    return jnp.stack([real_part, imag_part], axis=-1)

def inverse_x(values, phases):
    cosine_table = jnp.cos(phases)
    sine_table = jnp.sin(phases)
    real_part = jnp.einsum('cijm,xi->cxjm', values[..., 0], cosine_table, precision=PRECISE) - jnp.einsum('cijm,xi->cxjm', values[..., 1], sine_table, precision=PRECISE)
    imag_part = jnp.einsum('cijm,xi->cxjm', values[..., 0], sine_table, precision=PRECISE) + jnp.einsum('cijm,xi->cxjm', values[..., 1], cosine_table, precision=PRECISE)
    return jnp.stack([real_part, imag_part], axis=-1)

def reference(field, cotangent, spectral_weight, pointwise_weight, bias):
    width_x = 2 * MX
    width_y = 2 * MY
    cell_count = float(NX * NY * NZ)
    freq_x = frequency(jnp.arange(width_x, dtype=jnp.int32), MX, NX)
    freq_y = frequency(jnp.arange(width_y, dtype=jnp.int32), MY, NY)
    phases_y = angles(freq_y, jnp.arange(NY, dtype=jnp.int32), NY)
    z_phases = angles(jnp.arange(MZ, dtype=jnp.int32), jnp.arange(NZ, dtype=jnp.int32), NZ)
    table_z = jnp.stack([jnp.cos(z_phases), -jnp.sin(z_phases)], axis=2).reshape(NZ, 2 * MZ)
    weight_z = (jnp.where(jnp.arange(MZ, dtype=jnp.int32) == 0, 1.0, 2.0).astype(jnp.float32) / cell_count)[:, None]
    block_count = NX // CX
    block_ids = jnp.arange(block_count, dtype=jnp.int32)

    def block_of(source, block_id):
        return lax.dynamic_slice_in_dim(source, (block_id * CX).astype(jnp.int32), CX, 1)

    def positions(block_id):
        return (block_id * CX + jnp.arange(CX, dtype=jnp.int32)).astype(jnp.int32)

    def analyze_block(block, places):
        spectra = jnp.dot(block.reshape(-1, NZ), table_z, precision=PRECISE).reshape(C, CX, NY, MZ, 2)
        return forward_x(forward_y(spectra, phases_y), angles(freq_x, places, NX))

    def synthesize_block(spectrum, places):
        rows = inverse_y(inverse_x(spectrum, angles(freq_x, places, NX)), phases_y)
        return jnp.dot(rows.reshape(-1, 2 * MZ), table_z.T, precision=PRECISE).reshape(C, CX, NY, NZ)

    def spectrum_step(running, block_id):
        block = block_of(field, block_id).astype(jnp.float32)
        return (running + analyze_block(block, positions(block_id)), None)
    zero_spec = jnp.zeros((C, width_x, width_y, MZ, 2), jnp.float32)
    spec_u, _ = lax.scan(spectrum_step, zero_spec, block_ids)
    weights = spectral_weight.astype(jnp.float32).reshape(2, C, C, MZ, width_x, width_y).transpose(1, 2, 4, 5, 3, 0)
    mixed_re = jnp.einsum('coijm,cijm->oijm', weights[..., 0], spec_u[..., 0], precision=PRECISE) - jnp.einsum('coijm,cijm->oijm', weights[..., 1], spec_u[..., 1], precision=PRECISE)
    mixed_im = jnp.einsum('coijm,cijm->oijm', weights[..., 0], spec_u[..., 1], precision=PRECISE) + jnp.einsum('coijm,cijm->oijm', weights[..., 1], spec_u[..., 0], precision=PRECISE)
    mixed_modes = jnp.stack([mixed_re, mixed_im], axis=-1) * weight_z

    def local_pre(block_id):
        block = block_of(field, block_id)
        conv = synthesize_block(mixed_modes, positions(block_id))
        pointwise = jnp.dot(pointwise_weight.T, block.reshape(C, -1), preferred_element_type=jnp.float32).reshape(C, CX, NY, NZ)
        preact = pointwise + bias[:, None, None, None] + conv
        activated, pullback = jax.vjp(jax.nn.gelu, preact)
        gradient = pullback(block_of(cotangent, block_id).astype(jnp.float32))[0]
        return (block, activated, gradient)

    def first_step(running, block_id):
        spec_d, sum_w, sum_b = running
        block, activated, gradient = local_pre(block_id)
        spec_d = spec_d + analyze_block(gradient, positions(block_id))
        grad_flat = gradient.reshape(C, -1)
        sum_w = sum_w + jnp.dot(block.astype(jnp.float32).reshape(C, -1), grad_flat.T, precision=PRECISE)
        sum_b = sum_b + lax.optimization_barrier(jnp.sum(grad_flat, axis=1))
        return ((spec_d, sum_w, sum_b), activated.astype(jnp.bfloat16))
    start_state = (zero_spec, jnp.zeros((C, C), jnp.float32), jnp.zeros((C,), jnp.float32))
    (spec_d, sum_w, sum_b), outputs = lax.scan(first_step, start_state, block_ids)
    output = outputs.transpose(1, 0, 2, 3, 4).reshape(C, NX, NY, NZ)
    grad_mix = spec_d * weight_z
    spec_re = jnp.einsum('coijm,oijm->cijm', weights[..., 0], grad_mix[..., 0], precision=PRECISE) + jnp.einsum('coijm,oijm->cijm', weights[..., 1], grad_mix[..., 1], precision=PRECISE)
    spec_im = jnp.einsum('coijm,oijm->cijm', weights[..., 0], grad_mix[..., 1], precision=PRECISE) - jnp.einsum('coijm,oijm->cijm', weights[..., 1], grad_mix[..., 0], precision=PRECISE)
    grad_spec = jnp.stack([spec_re, spec_im], axis=-1)
    weight_re = jnp.einsum('cijm,oijm->coijm', spec_u[..., 0], grad_mix[..., 0], precision=PRECISE) + jnp.einsum('cijm,oijm->coijm', spec_u[..., 1], grad_mix[..., 1], precision=PRECISE)
    weight_im = jnp.einsum('cijm,oijm->coijm', spec_u[..., 0], grad_mix[..., 1], precision=PRECISE) - jnp.einsum('cijm,oijm->coijm', spec_u[..., 1], grad_mix[..., 0], precision=PRECISE)
    grad_spectral = jnp.stack([weight_re, weight_im], axis=-1).transpose(5, 0, 1, 4, 2, 3).reshape(2, C, C, MZ, width_x * width_y)

    def second_step(block_id):
        block, activated, gradient = local_pre(block_id)
        returned = synthesize_block(grad_spec, positions(block_id))
        pointwise = jnp.dot(pointwise_weight.astype(jnp.float32), gradient.reshape(C, -1), precision=PRECISE).reshape(C, CX, NY, NZ)
        return (pointwise + returned).astype(jnp.bfloat16)
    grad_blocks = lax.map(second_step, block_ids)
    grad_field = grad_blocks.transpose(1, 0, 2, 3, 4).reshape(C, NX, NY, NZ)
    shrink = cell_count ** (-0.5)
    return (output, grad_field, grad_spectral, sum_w * shrink, sum_b * shrink)
```

```python
import functools
import math

import jax
import jax.numpy as jnp
from jax import lax
import numpy as np
from jax.experimental import pallas as pl
from jax.experimental.pallas import tpu as pltpu
from jax.sharding import PartitionSpec as P

MX = 24
MY = 24
MZ = 24


PRECISE = lax.Precision.HIGHEST
TWO_PI = 2.0 * math.pi


def angles(frequencies, places, length):
    product = places[:, None] * frequencies[None, :] % length
    return product.astype(jnp.float32) * (TWO_PI / length)


def frequency(position, kept_modes, length):
    return jnp.where(position < kept_modes, position, position - 2 * kept_modes + length)


def forward_y(values, phases):
    cosine_table = jnp.cos(phases)
    sine_table = jnp.sin(phases)
    with_cos = jnp.einsum("brcxy,yj->brcxj", values, cosine_table, precision=PRECISE)
    with_sin = jnp.einsum("brcxy,yj->brcxj", values, sine_table, precision=PRECISE)
    real_part = with_cos[:, 0] + with_sin[:, 1]
    imag_part = with_cos[:, 1] - with_sin[:, 0]
    return jnp.stack([real_part, imag_part], axis=1)


def inverse_y(values, phases):
    cosine_table = jnp.cos(phases)
    sine_table = jnp.sin(phases)
    with_cos = jnp.einsum("brcxj,yj->brcxy", values, cosine_table, precision=PRECISE)
    with_sin = jnp.einsum("brcxj,yj->brcxy", values, sine_table, precision=PRECISE)
    real_part = with_cos[:, 0] - with_sin[:, 1]
    imag_part = with_sin[:, 0] + with_cos[:, 1]
    return jnp.stack([real_part, imag_part], axis=1)


def local(field, cotangent, spectral_weight, pointwise_weight, bias):
    channels, rows_x, rows_y, depth_cells = field.shape
    blocks_z = spectral_weight.shape[3]
    pair_rows = spectral_weight.shape[4]
    width_x = 2 * MX
    width_y = 2 * MY
    full_x = rows_x * lax.axis_size("gx")
    full_y = rows_y * lax.axis_size("gy")
    cell_count = float(full_x * full_y * depth_cells)
    place_x = lax.axis_index("gx")
    place_y = lax.axis_index("gy")
    own_x = place_x * rows_x + jnp.arange(rows_x, dtype=jnp.int32)
    freq_x = frequency(jnp.arange(width_x, dtype=jnp.int32), MX, full_x)
    freq_y = frequency(jnp.arange(width_y, dtype=jnp.int32), MY, full_y)
    phases_full_y = angles(freq_y, jnp.arange(full_y, dtype=jnp.int32), full_y)
    z_phases = angles(
        jnp.arange(MZ, dtype=jnp.int32), jnp.arange(depth_cells, dtype=jnp.int32), depth_cells
    )
    table_z = jnp.stack([jnp.cos(z_phases), -jnp.sin(z_phases)], axis=2).reshape(
        depth_cells, 2 * MZ
    )
    kz_own = place_y * blocks_z + jnp.arange(blocks_z, dtype=jnp.int32)
    weight_z = (jnp.where(kz_own == 0, 1.0, 2.0).astype(jnp.float32) / cell_count)[None, :, None]
    own_first = place_x * pair_rows
    flat_width = blocks_z * 2 * channels

    def kx_terms(values, places, first_pair, count):
        kx_count = min(count // width_y + 2, width_x)
        kx_first = jnp.minimum(first_pair // width_y, width_x - kx_count)
        kx_ids = kx_first + jnp.arange(kx_count, dtype=jnp.int32)
        phases = angles(frequency(kx_ids, MX, full_x), places, full_x)
        cosine_table = jnp.cos(phases)
        sine_table = jnp.sin(phases)
        real_part = jnp.einsum(
            "bcxj,xi->ijbc", values[:, 0], cosine_table, precision=PRECISE
        ) + jnp.einsum("bcxj,xi->ijbc", values[:, 1], sine_table, precision=PRECISE)
        imag_part = jnp.einsum(
            "bcxj,xi->ijbc", values[:, 1], cosine_table, precision=PRECISE
        ) - jnp.einsum("bcxj,xi->ijbc", values[:, 0], sine_table, precision=PRECISE)
        terms = jnp.stack([real_part, imag_part], axis=3).reshape(kx_count * width_y, flat_width)
        offset = first_pair - kx_first * width_y
        return lax.dynamic_slice_in_dim(terms, offset, count, 0)

    def analyze(values):
        flat = values.reshape(-1, depth_cells)
        spectra = jnp.einsum("zk,mz->km", table_z, flat, precision=PRECISE).reshape(
            2 * MZ, channels, rows_x, rows_y
        )
        columns = lax.all_to_all(spectra, "gy", split_axis=0, concat_axis=3, tiled=True)
        mode_data = forward_y(columns.reshape(blocks_z, 2, channels, rows_x, full_y), phases_full_y)
        portion = lax.all_gather(mode_data, "gx", axis=3, tiled=True)
        places = jnp.arange(portion.shape[3], dtype=jnp.int32)
        owned = kx_terms(portion, places, own_first, pair_rows)
        return jnp.transpose(owned.reshape(pair_rows, blocks_z, 2, channels), (2, 3, 1, 0))

    def synthesize(spectrum):
        portion = lax.all_gather(spectrum, "gx", axis=3, tiled=True)
        blocks = portion.reshape(2, channels, blocks_z, width_x, width_y)
        phases = angles(freq_x, own_x, full_x)
        cosine_table = jnp.cos(phases)
        sine_table = jnp.sin(phases)
        real_part = jnp.einsum(
            "cbij,xi->bcxj", blocks[0], cosine_table, precision=PRECISE
        ) - jnp.einsum("cbij,xi->bcxj", blocks[1], sine_table, precision=PRECISE)
        imag_part = jnp.einsum(
            "cbij,xi->bcxj", blocks[0], sine_table, precision=PRECISE
        ) + jnp.einsum("cbij,xi->bcxj", blocks[1], cosine_table, precision=PRECISE)
        mode_data = jnp.stack([real_part, imag_part], axis=1)
        fields = inverse_y(mode_data, phases_full_y)
        columns = lax.all_to_all(fields, "gy", split_axis=4, concat_axis=0, tiled=True)
        flat = columns.reshape(2 * MZ, -1)
        return jnp.einsum("km,zk->mz", flat, table_z, precision=PRECISE).reshape(
            channels, rows_x, rows_y, depth_cells
        )

    weights = spectral_weight.astype(jnp.float32)
    widened = field.astype(jnp.float32)
    spec_u = analyze(widened)
    mixed_re = jnp.einsum("cobp,cbp->obp", weights[0], spec_u[0], precision=PRECISE) - jnp.einsum(
        "cobp,cbp->obp", weights[1], spec_u[1], precision=PRECISE
    )
    mixed_im = jnp.einsum("cobp,cbp->obp", weights[0], spec_u[1], precision=PRECISE) + jnp.einsum(
        "cobp,cbp->obp", weights[1], spec_u[0], precision=PRECISE
    )
    mixed_modes = jnp.stack([mixed_re, mixed_im]) * weight_z
    conv = synthesize(mixed_modes)
    pointwise = jnp.dot(
        pointwise_weight.T, field.reshape(channels, -1), preferred_element_type=jnp.float32
    ).reshape(field.shape)
    preact = pointwise + bias[:, None, None, None] + conv
    activated, pullback = jax.vjp(jax.nn.gelu, preact)
    gradient = pullback(cotangent.astype(jnp.float32))[0]
    grad_mix = analyze(gradient) * weight_z
    spec_re = jnp.einsum("cobp,obp->cbp", weights[0], grad_mix[0], precision=PRECISE) + jnp.einsum(
        "cobp,obp->cbp", weights[1], grad_mix[1], precision=PRECISE
    )
    spec_im = jnp.einsum("cobp,obp->cbp", weights[0], grad_mix[1], precision=PRECISE) - jnp.einsum(
        "cobp,obp->cbp", weights[1], grad_mix[0], precision=PRECISE
    )
    grad_spec = jnp.stack([spec_re, spec_im])
    weight_re = jnp.einsum("cbp,obp->cobp", spec_u[0], grad_mix[0], precision=PRECISE) + jnp.einsum(
        "cbp,obp->cobp", spec_u[1], grad_mix[1], precision=PRECISE
    )
    weight_im = jnp.einsum("cbp,obp->cobp", spec_u[0], grad_mix[1], precision=PRECISE) - jnp.einsum(
        "cbp,obp->cobp", spec_u[1], grad_mix[0], precision=PRECISE
    )
    grad_spectral = jnp.stack([weight_re, weight_im])
    returned = synthesize(grad_spec)
    grad_flat = gradient.reshape(channels, -1)
    back_point = jnp.dot(
        pointwise_weight.astype(jnp.float32), grad_flat, precision=PRECISE
    ).reshape(field.shape)
    grad_field = (back_point + returned).astype(jnp.bfloat16)
    local_weight = jnp.dot(widened.reshape(channels, -1), grad_flat.T, precision=PRECISE)
    local_bias = jnp.sum(grad_flat, axis=1)
    summed_weight, summed_bias = lax.psum((local_weight, local_bias), ("gx", "gy"))
    shrink = cell_count ** (-0.5)
    return (
        activated.astype(jnp.bfloat16),
        grad_field,
        grad_spectral,
        summed_weight * shrink,
        summed_bias * shrink,
    )


LANES = 128
HALF = 64
VMEM_BYTES = 48 * 1024 * 1024


def split_table(table):
    high = table.astype(jnp.bfloat16)
    low = (table - high.astype(np.float64)).astype(jnp.bfloat16)
    return high, low


def frequency_table(kept_modes, length):
    position = np.arange(2 * kept_modes)
    return np.where(position < kept_modes, position, position - 2 * kept_modes + length)


def phase_table(frequencies, places, length):
    product = places[:, None] * frequencies[None, :] % length
    return product.astype(np.float64) * (TWO_PI / length)


def split(values):
    high = values.astype(jnp.bfloat16)
    low = (values - high.astype(jnp.float32)).astype(jnp.bfloat16)
    return high, low


def product(left, right, contract=((1,), (0,)), precision=None):
    return lax.dot_general(
        left, right, (contract, ((), ())), preferred_element_type=jnp.float32, precision=precision
    )


NT = ((1,), (1,))
TN = ((0,), (0,))


def lane_ids(rows):
    return lax.broadcasted_iota(jnp.int32, (rows, LANES), 1)


def roll_lanes(values, shift):
    shift = shift % LANES
    if shift == 0:
        return values
    return pltpu.roll(values, shift, 1)


class Plan:
    def __init__(self, field_shape, weight_shape, size_x, size_y):
        self.channels, self.rows_x, self.rows_y, self.depth = field_shape
        self.size_x, self.size_y = size_x, size_y
        self.blocks_z = weight_shape[3]
        self.pair_rows = weight_shape[4]
        self.full_x = self.rows_x * size_x
        self.full_y = self.rows_y * size_y
        self.width_x, self.width_y = 2 * MX, 2 * MY
        self.cells = self.rows_x * self.rows_y
        self.part_c, self.part_z = 0, 0
        for part_z in range(1, self.blocks_z + 1):
            part_c = size_x // part_z
            if size_x % part_z or self.blocks_z % part_z or self.channels % part_c:
                continue
            self.part_c, self.part_z = part_c, part_z
        self.fits = False
        if self.part_c == 0:
            return
        self.own_c = self.channels // self.part_c
        self.own_z = self.blocks_z // self.part_z
        self.planes = self.own_c * self.own_z
        self.plane_rows = 16
        self.own_kx = self.pair_rows // self.width_y
        self.devices = size_x * size_y
        self.fits = (
            self.cells == LANES
            and self.rows_y == 16
            and self.depth % LANES == 0
            and self.planes < self.plane_rows
            and self.pair_rows % self.width_y == 0
            and self.pair_rows == 2 * LANES + 32
            and self.width_y <= HALF
            and self.channels + 1 <= min(self.devices, 24)
            and self.own_z * 2 * self.part_z * size_y == 2 * MZ
        )

    def z_table(self, scaled):
        kz = np.arange(MZ)
        phases = phase_table(kz, np.arange(self.depth), self.depth)
        both = np.stack([np.cos(phases), -np.sin(phases)])
        if scaled:
            cells = float(self.full_x * self.full_y * self.depth)
            both = both * (np.where(kz == 0, 1.0, 2.0) / cells)
        both = both.reshape(2, self.depth, self.size_y, self.part_z, self.own_z)
        return both.transpose(2, 3, 0, 4, 1).reshape(2 * MZ, self.depth)

    def y_table(self):
        freq = frequency_table(MY, self.full_y)
        phases = phase_table(freq, np.arange(self.full_y), self.full_y)
        cosine, sine = np.cos(phases), np.sin(phases)
        one = np.zeros((self.size_y, 2, self.rows_y, 2, HALF))
        by_block = (self.size_y, self.rows_y, self.width_y)
        one[:, 0, :, 0, : self.width_y] = cosine.reshape(by_block)
        one[:, 1, :, 0, : self.width_y] = sine.reshape(by_block)
        one[:, 0, :, 1, : self.width_y] = -sine.reshape(by_block)
        one[:, 1, :, 1, : self.width_y] = cosine.reshape(by_block)
        full = np.zeros((self.size_y, 2, self.rows_x, self.rows_y, self.rows_x, LANES))
        for row in range(self.rows_x):
            full[:, :, row, :, row, :] = one.reshape(self.size_y, 2, self.rows_y, LANES)
        return full.reshape(self.size_y * 2 * LANES, self.rows_x * LANES)

    def x_tables(self):
        freq = frequency_table(MX, self.full_x)
        phases = phase_table(freq, np.arange(self.full_x), self.full_x)
        cosine, sine = np.cos(phases), np.sin(phases)
        forward = np.concatenate([cosine.T, sine.T], axis=0)
        inverse = np.concatenate([cosine, sine], axis=0)
        tables = []
        for table in (forward, inverse):
            high, low = split_table(table)
            tables.append(np.concatenate([high, low, high], axis=1))
        return tables


def call(kernel, out_shape, scratch, *operands, smem=(), **more):
    specs = [
        pl.BlockSpec(memory_space=pltpu.SMEM if at in smem else pltpu.VMEM)
        for at in range(len(operands))
    ]
    single = not isinstance(out_shape, (tuple, list))
    outs = pl.BlockSpec(memory_space=pltpu.VMEM)
    return pl.pallas_call(
        kernel,
        out_shape=out_shape,
        in_specs=specs,
        out_specs=outs if single else [outs] * len(out_shape),
        scratch_shapes=scratch,
        compiler_params=pltpu.CompilerParams(vmem_limit_bytes=VMEM_BYTES),
        **more,
    )(*operands)


def put_spectrum(plan, out_ref, channel, rows):
    block, inner = divmod(channel, plan.own_c)
    size = plan.own_z
    at = 0
    for place_y in range(plan.size_y):
        for part in range(plan.part_z):
            place_x = block * plan.part_z + part
            for which in range(2):
                out_ref[place_x, place_y, which, inner * size : (inner + 1) * size, :] = rows[
                    at : at + size
                ]
                at += size


def take_spectrum(plan, in_ref, rows_ref, channel):
    block, inner = divmod(channel, plan.own_c)
    size = plan.own_z
    at = 0
    for place_y in range(plan.size_y):
        for part in range(plan.part_z):
            place_x = block * plan.part_z + part
            for which in range(2):
                rows_ref[at : at + size, :] = in_ref[
                    place_x, place_y, which, inner * size : (inner + 1) * size, :
                ]
                at += size
    return rows_ref[...]


def clear_spare(plan, out_ref):
    zeros = jnp.zeros((plan.plane_rows - plan.planes, LANES), jnp.float32)
    for place_x in range(plan.size_x):
        for place_y in range(plan.size_y):
            for which in range(2):
                out_ref[place_x, place_y, which, plan.planes :, :] = zeros


def depth_analysis_kernel(plan, field_ref, table_ref, out_ref):
    clear_spare(plan, out_ref)
    table = table_ref[...]
    for channel in range(plan.channels):
        block = field_ref[channel].reshape(plan.cells, plan.depth)
        both = product(table, block, NT)
        put_spectrum(plan, out_ref, channel, both[: 2 * MZ] + both[2 * MZ :])


def plane_analysis_kernel(
    plan, in_ref, y_high_ref, y_low_ref, x_ref, out_ref, sums_ref, rows_ref, modes_ref, rest_ref
):
    pad = plan.plane_rows
    spare = jnp.zeros((1, LANES), jnp.float32)
    for place_x in range(plan.size_x):
        for place_y in range(plan.size_y):
            spare = spare + in_ref[place_x, place_y, 0, plan.planes : plan.planes + 1, :]
    sums_ref[...] = jnp.broadcast_to(spare, (8, LANES))
    left = jnp.concatenate(
        [
            in_ref[:, place_y, which].reshape(plan.size_x * pad, LANES)
            for place_y in range(plan.size_y)
            for which in range(2)
        ],
        axis=1,
    )
    high, low = split(left)
    y_high = y_high_ref[...]
    along_y = product(high, y_high) + product(low, y_high) + product(high, y_low_ref[...])
    for place_x in range(plan.size_x):
        for row in range(plan.rows_x):
            at = (place_x * plan.rows_x + row) * pad
            rows_ref[at : at + pad, :] = along_y[
                place_x * pad : (place_x + 1) * pad, row * LANES : (row + 1) * LANES
            ]
    right = jnp.concatenate(
        [rows_ref[pl.ds(plane, plan.full_x, stride=pad), :] for plane in range(plan.planes)], axis=1
    )
    high, low = split(right)
    both = product(x_ref[...], jnp.concatenate([high, high, low], axis=0))
    sign = jnp.where(lane_ids(plan.width_x) < HALF, 1.0, -1.0)
    for plane in range(plan.planes):
        mine = slice(plane * LANES, (plane + 1) * LANES)
        turned = roll_lanes(both[plan.width_x :, mine], HALF)
        modes_ref[pl.ds(plane, plan.width_x, stride=pad), :] = (
            both[: plan.width_x, mine] + sign * turned
        )
    modes_ref[pl.ds(plan.planes, plan.width_x, stride=pad), :] = jnp.zeros(
        (plan.width_x, LANES), jnp.float32
    )
    lanes = lane_ids(pad)
    width = plan.width_y
    for place_x in range(plan.size_x):
        for which in range(2):
            tiles = [None, None, None]
            for inner in range(plan.own_kx):
                kx = place_x * plan.own_kx + inner
                first = inner * width
                turned = roll_lanes(modes_ref[kx * pad : (kx + 1) * pad, :], first - which * HALF)
                tile, offset = divmod(first, LANES)
                for at in (tile, tile + 1):
                    begin = first - at * LANES
                    if begin >= LANES or begin + width <= 0:
                        continue
                    if tiles[at] is None:
                        tiles[at] = turned
                    else:
                        tiles[at] = jnp.where(lanes < begin, tiles[at], turned)
            for at in range(2):
                row = at * 2 * pad + which * pad
                out_ref[place_x, row : row + pad, :] = tiles[at]
            rest_ref[which * pad : (which + 1) * pad, :] = tiles[2]
        out_ref[place_x, 4 * pad : 4 * pad + 8, :] = pack_rest(rest_ref)


def pack_rest(rest_ref):
    lanes = lane_ids(8)
    packed = rest_ref[0:8, :]
    for group in range(1, 4):
        turned = roll_lanes(rest_ref[group * 8 : (group + 1) * 8, :], group * 32)
        packed = jnp.where(lanes < group * 32, packed, turned)
    return packed


def unpack_rest(packed, rest_ref):
    for group in range(4):
        rest_ref[group * 8 : (group + 1) * 8, :] = roll_lanes(packed, -group * 32)


def take_modes(plan, in_ref, modes_ref, rest_ref):
    pad, size = plan.plane_rows, plan.own_z
    for place_x in range(plan.size_x):
        block, part = divmod(place_x, plan.part_z)
        unpack_rest(in_ref[place_x, 4 * pad : 4 * pad + 8, :], rest_ref)
        for which in range(2):
            for inner in range(plan.own_c):
                channel = block * plan.own_c + inner
                row = which * pad + inner * size
                kz = slice(part * size, (part + 1) * size)
                for at in range(2):
                    begin = at * 2 * pad + row
                    modes_ref[channel, which, kz, at * LANES : (at + 1) * LANES] = in_ref[
                        place_x, begin : begin + size, :
                    ]
                modes_ref[channel, which, kz, 2 * LANES :] = rest_ref[row : row + size, 0:32]


def put_modes(plan, modes_ref, out_ref, rest_ref):
    pad, size = plan.plane_rows, plan.own_z
    zeros = jnp.zeros((pad - plan.planes, LANES), jnp.float32)
    rest_ref[...] = jnp.zeros((2 * pad, LANES), jnp.float32)
    for place_x in range(plan.size_x):
        block, part = divmod(place_x, plan.part_z)
        for which in range(2):
            for inner in range(plan.own_c):
                channel = block * plan.own_c + inner
                row = which * pad + inner * size
                kz = slice(part * size, (part + 1) * size)
                for at in range(2):
                    begin = at * 2 * pad + row
                    out_ref[place_x, begin : begin + size, :] = modes_ref[
                        channel, which, kz, at * LANES : (at + 1) * LANES
                    ]
                rest_ref[row : row + size, 0:32] = modes_ref[channel, which, kz, 2 * LANES :]
            for at in range(2):
                begin = at * 2 * pad + which * pad + plan.planes
                out_ref[place_x, begin : begin + pad - plan.planes, :] = zeros
        out_ref[place_x, 4 * pad : 4 * pad + 8, :] = pack_rest(rest_ref)


def mix_kernel(plan, in_ref, weight_ref, out_ref, spectrum_ref, mixed_ref, rest_ref):
    take_modes(plan, in_ref, spectrum_ref, rest_ref)
    shape = (plan.blocks_z, plan.pair_rows)

    def one(out_channel, carry):
        real_part = jnp.zeros(shape, jnp.float32)
        imag_part = jnp.zeros(shape, jnp.float32)
        for channel in range(plan.channels):
            weight_re = weight_ref[0, channel, out_channel].astype(jnp.float32)
            weight_im = weight_ref[1, channel, out_channel].astype(jnp.float32)
            value_re = spectrum_ref[channel, 0]
            value_im = spectrum_ref[channel, 1]
            real_part += weight_re * value_re - weight_im * value_im
            imag_part += weight_re * value_im + weight_im * value_re
        mixed_ref[out_channel, 0] = real_part
        mixed_ref[out_channel, 1] = imag_part
        return carry

    lax.fori_loop(0, plan.channels, one, 0)
    put_modes(plan, mixed_ref, out_ref, rest_ref)


def mix_back_kernel(plan, in_ref, weight_ref, out_ref, grad_ref, mixed_ref, rest_ref):
    take_modes(plan, in_ref, grad_ref, rest_ref)
    shape = (plan.blocks_z, plan.pair_rows)

    def one(channel, carry):
        real_part = jnp.zeros(shape, jnp.float32)
        imag_part = jnp.zeros(shape, jnp.float32)
        for out_channel in range(plan.channels):
            weight_re = weight_ref[0, channel, out_channel].astype(jnp.float32)
            weight_im = weight_ref[1, channel, out_channel].astype(jnp.float32)
            value_re = grad_ref[out_channel, 0]
            value_im = grad_ref[out_channel, 1]
            real_part += weight_re * value_re + weight_im * value_im
            imag_part += weight_re * value_im - weight_im * value_re
        mixed_ref[channel, 0] = real_part
        mixed_ref[channel, 1] = imag_part
        return carry

    lax.fori_loop(0, plan.channels, one, 0)
    put_modes(plan, mixed_ref, out_ref, rest_ref)


def weight_grad_kernel(plan, spectrum_ref, grad_ref, out_ref):
    value_re = spectrum_ref[0, 0]
    value_im = spectrum_ref[0, 1]
    for out_channel in range(plan.channels):
        grad_re = grad_ref[out_channel, 0]
        grad_im = grad_ref[out_channel, 1]
        out_ref[0, 0, out_channel] = value_re * grad_re + value_im * grad_im
        out_ref[1, 0, out_channel] = value_re * grad_im - value_im * grad_re


def weight_grad(plan, spectrum, grad):
    modes = (plan.blocks_z, plan.pair_rows)
    return pl.pallas_call(
        functools.partial(weight_grad_kernel, plan),
        grid=(plan.channels,),
        out_shape=jax.ShapeDtypeStruct((2, plan.channels, plan.channels) + modes, jnp.float32),
        in_specs=[
            pl.BlockSpec((1, 2) + modes, lambda channel: (channel, 0, 0, 0)),
            pl.BlockSpec((plan.channels, 2) + modes, lambda channel: (0, 0, 0, 0)),
        ],
        out_specs=pl.BlockSpec(
            (2, 1, plan.channels) + modes, lambda channel: (0, channel, 0, 0, 0)
        ),
        compiler_params=pltpu.CompilerParams(vmem_limit_bytes=VMEM_BYTES),
    )(spectrum, grad)


def plane_synthesis_kernel(
    plan, in_ref, sums_ref, y_high_ref, y_low_ref, x_ref, out_ref, rows_ref, modes_ref, rest_ref
):
    pad, width = plan.plane_rows, plan.width_y
    lanes = lane_ids(pad)
    for place_x in range(plan.size_x):
        unpack_rest(in_ref[place_x, 4 * pad : 4 * pad + 8, :], rest_ref)
        tiles = []
        for which in range(2):
            row = which * pad
            tiles.append(
                [
                    in_ref[place_x, row : row + pad, :],
                    in_ref[place_x, 2 * pad + row : 3 * pad + row, :],
                    rest_ref[row : row + pad, :],
                ]
            )
        for inner in range(plan.own_kx):
            first = inner * width
            tile, offset = divmod(first, LANES)
            pieces = []
            for which in range(2):
                piece = roll_lanes(tiles[which][tile], which * HALF - offset)
                if offset + width > LANES:
                    later = roll_lanes(tiles[which][tile + 1], which * HALF - offset)
                    piece = jnp.where(lanes < which * HALF + LANES - offset, piece, later)
                pieces.append(piece)
            merged = jnp.where(lanes < HALF, pieces[0], pieces[1])
            used = jnp.bitwise_and(lanes, HALF - 1) < width
            at = (place_x * plan.own_kx + inner) * pad
            modes_ref[at : at + pad, :] = jnp.where(used, merged, 0.0)
    right = jnp.concatenate(
        [modes_ref[pl.ds(plane, plan.width_x, stride=pad), :] for plane in range(plan.planes)],
        axis=1,
    )
    high, low = split(right)
    both = product(x_ref[...], jnp.concatenate([high, high, low], axis=0))
    sign = jnp.where(lane_ids(plan.full_x) < HALF, -1.0, 1.0)
    for plane in range(plan.planes):
        mine = slice(plane * LANES, (plane + 1) * LANES)
        turned = roll_lanes(both[plan.full_x :, mine], HALF)
        rows_ref[pl.ds(plane, plan.full_x, stride=pad), :] = (
            both[: plan.full_x, mine] + sign * turned
        )
    rows_ref[pl.ds(plan.planes, plan.full_x, stride=pad), :] = jnp.zeros(
        (plan.full_x, LANES), jnp.float32
    )
    columns = []
    for row in range(plan.rows_x):
        starts = [(place_x * plan.rows_x + row) * pad for place_x in range(plan.size_x)]
        columns.append(jnp.concatenate([rows_ref[at : at + pad, :] for at in starts], axis=0))
    high, low = split(jnp.concatenate(columns, axis=1))
    y_high = y_high_ref[...]
    along_y = (
        product(high, y_high, NT) + product(low, y_high, NT) + product(high, y_low_ref[...], NT)
    )
    spare = sums_ref[0:1, :]
    for place_y in range(plan.size_y):
        for which in range(2):
            at = (place_y * 2 + which) * LANES
            out_ref[:, place_y, which] = along_y[:, at : at + LANES].reshape(
                plan.size_x, pad, LANES
            )
    for place_x in range(plan.size_x):
        for place_y in range(plan.size_y):
            out_ref[place_x, place_y, 0, plan.planes : plan.planes + 1, :] = spare


def widen_map(plan, small, transposed):
    rows = plan.channels * plan.rows_y
    row_ids = lax.broadcasted_iota(jnp.int32, (rows, plan.channels), 0)
    column_ids = lax.broadcasted_iota(jnp.int32, (rows, plan.channels), 1)
    spread = jnp.where(row_ids // plan.rows_y == column_ids, 1.0, 0.0).astype(jnp.bfloat16)
    wide = product(spread, small, ((1,), (0,)) if transposed else ((1,), (1,)))
    wide = product(wide.astype(jnp.bfloat16), spread, NT)
    return jnp.where(same_cell(plan), wide, 0.0).astype(jnp.bfloat16)


def same_cell(plan):
    rows = plan.channels * plan.rows_y
    row_ids = lax.broadcasted_iota(jnp.int32, (rows, rows), 0)
    column_ids = lax.broadcasted_iota(jnp.int32, (rows, rows), 1)
    return jnp.bitwise_and(row_ids, plan.rows_y - 1) == jnp.bitwise_and(
        column_ids, plan.rows_y - 1
    )


def synthesize_depth(plan, in_ref, rows_ref, table, channel):
    rows = take_spectrum(plan, in_ref, rows_ref, channel)
    high, low = split(rows)
    return product(jnp.concatenate([high, high, low], axis=0), table, TN)


def middle_kernel(
    plan,
    in_ref,
    field_ref,
    cotangent_ref,
    map_ref,
    bias_ref,
    inverse_ref,
    forward_ref,
    output_ref,
    spectrum_ref,
    high_ref,
    low_ref,
    conv_ref,
    rows_ref,
    cross_ref,
    total_ref,
):
    clear_spare(plan, spectrum_ref)
    block = (plan.rows_x, plan.rows_y, plan.depth)
    rows = plan.channels * plan.rows_y
    inverse = inverse_ref[...]
    for channel in range(plan.channels):
        conv = synthesize_depth(plan, in_ref, rows_ref, inverse, channel) + bias_ref[channel]
        conv_ref[channel] = conv.reshape(block)
    wide = widen_map(plan, map_ref[...], False)
    cross_ref[...] = jnp.zeros((rows, rows), jnp.float32)
    total_ref[...] = jnp.zeros((rows, plan.depth), jnp.float32)
    scale = math.sqrt(2.0 / math.pi)
    slab = (plan.channels, 1, plan.rows_y, plan.depth)

    def one(row, carry):
        here = pl.ds(row, 1)
        values = field_ref[:, here].reshape(rows, plan.depth)
        preact = conv_ref[:, here].reshape(rows, plan.depth) + product(wide, values)
        square = preact * preact
        bend = jnp.tanh(scale * preact * (1.0 + 0.044715 * square))
        half = 0.5 * (1.0 + bend)
        output_ref[:, here] = (preact * half).astype(jnp.bfloat16).reshape(slab)
        slope = half + (0.5 * scale) * preact * (1.0 - bend * bend) * (
            1.0 + (3.0 * 0.044715) * square
        )
        grad = cotangent_ref[:, here].reshape(rows, plan.depth).astype(jnp.float32) * slope
        high, low = split(grad)
        high_ref[:, here] = high.reshape(slab)
        low_ref[:, here] = low.reshape(slab)
        cross_ref[...] += product(values, high, NT) + product(values, low, NT)
        total_ref[...] += grad
        return carry

    lax.fori_loop(0, plan.rows_x, one, 0)
    forward = forward_ref[...]
    for channel in range(plan.channels):
        high = high_ref[channel].reshape(plan.cells, plan.depth)
        low = low_ref[channel].reshape(plan.cells, plan.depth)
        both = product(forward, high, NT)
        more = product(forward[: 2 * MZ], low, NT)
        put_spectrum(plan, spectrum_ref, channel, both[: 2 * MZ] + both[2 * MZ :] + more)
    row_ids = lax.broadcasted_iota(jnp.int32, (rows, LANES), 0)
    gather = jnp.where(row_ids // plan.rows_y == lane_ids(rows), 1.0, 0.0)
    exact = lax.Precision.HIGHEST
    cross = jnp.where(same_cell(plan), cross_ref[...], 0.0)
    by_out = product(cross, gather, precision=exact)
    sums = product(gather, by_out, TN, precision=exact)
    ones = jnp.ones((8, plan.depth), jnp.float32)
    bias_sums = product(
        product(ones, total_ref[...], NT, precision=exact), gather, precision=exact
    )
    for row in range(plan.channels + 1):
        place_x, place_y = divmod(row, plan.size_y)
        spare = sums[row : row + 1] if row < plan.channels else bias_sums[0:1]
        spectrum_ref[place_x, place_y, 0, plan.planes : plan.planes + 1, :] = spare


def last_kernel(
    plan,
    in_ref,
    high_ref,
    low_ref,
    map_ref,
    inverse_ref,
    grad_ref,
    sums_ref,
    conv_ref,
    rows_ref,
):
    block = (plan.rows_x, plan.rows_y, plan.depth)
    rows = plan.channels * plan.rows_y
    inverse = inverse_ref[...]
    for channel in range(plan.channels):
        conv_ref[channel] = synthesize_depth(plan, in_ref, rows_ref, inverse, channel).reshape(
            block
        )
    wide = widen_map(plan, map_ref[...], True)
    slab = (plan.channels, 1, plan.rows_y, plan.depth)

    def one(row, carry):
        here = pl.ds(row, 1)
        high = high_ref[:, here].reshape(rows, plan.depth)
        low = low_ref[:, here].reshape(rows, plan.depth)
        total = (
            conv_ref[:, here].reshape(rows, plan.depth) + product(wide, high) + product(wide, low)
        )
        grad_ref[:, here] = total.astype(jnp.bfloat16).reshape(slab)
        return carry

    lax.fori_loop(0, plan.rows_x, one, 0)
    sums_ref[...] = jnp.zeros((24, LANES), jnp.float32)
    shrink = float(plan.full_x * plan.full_y * plan.depth) ** (-0.5)
    for row in range(plan.channels + 1):
        place_x, place_y = divmod(row, plan.size_y)
        sums_ref[row : row + 1, :] = shrink * (
            in_ref[place_x, place_y, 0, plan.planes : plan.planes + 1, :]
        )


def by_planes(plan, field, cotangent, spectral_weight, pointwise_weight, bias):
    pad = plan.plane_rows
    f32 = jnp.float32
    cell_shape = (plan.size_x, plan.size_y, 2, pad, LANES)
    mode_shape = (plan.size_x, 4 * pad + 8, LANES)
    own_shape = (plan.channels, 2, plan.blocks_z, plan.pair_rows)
    grid_shape = field.shape

    def shape(dims, kind=f32):
        return jax.ShapeDtypeStruct(dims, kind)

    def cell_exchange(values):
        flat = values.reshape(plan.devices, 2 * pad, LANES)
        return lax.all_to_all(flat, ("gx", "gy"), 0, 0, tiled=True).reshape(cell_shape)

    def mode_exchange(values):
        return lax.all_to_all(values, "gx", 0, 0, tiled=True)

    z_high, z_low = split_table(plan.z_table(False))
    scaled_high, scaled_low = split_table(plan.z_table(True))
    z_forward = jnp.asarray(np.concatenate([z_high, z_low]))
    z_inverse = jnp.asarray(np.concatenate([z_high, z_low, z_high]))
    scaled_forward = jnp.asarray(np.concatenate([scaled_high, scaled_low]))
    scaled_inverse = jnp.asarray(np.concatenate([scaled_high, scaled_low, scaled_high]))
    y_high, y_low = (jnp.asarray(table) for table in split_table(plan.y_table()))
    x_forward, x_inverse = (jnp.asarray(table) for table in plan.x_tables())

    lane_rows = pltpu.VMEM((plan.full_x * pad, LANES), f32)
    lane_modes = pltpu.VMEM((plan.width_x * pad, LANES), f32)
    rest = pltpu.VMEM((2 * pad, LANES), f32)
    own = pltpu.VMEM(own_shape, f32)
    grid = pltpu.VMEM(grid_shape, f32)
    lines = pltpu.VMEM((2 * MZ, LANES), f32)
    wide = plan.channels * plan.rows_y

    def with_plan(kernel):
        return functools.partial(kernel, plan)

    def plane_analysis(cells):
        return call(
            with_plan(plane_analysis_kernel),
            [shape(mode_shape), shape((8, LANES))],
            [lane_rows, lane_modes, rest],
            cells,
            y_high,
            y_low,
            x_forward,
        )

    def plane_synthesis(modes, sums):
        return call(
            with_plan(plane_synthesis_kernel),
            shape(cell_shape),
            [lane_rows, lane_modes, rest],
            modes,
            sums,
            y_high,
            y_low,
            x_inverse,
        )

    with jax.named_scope("depth_analysis"):
        cells = call(with_plan(depth_analysis_kernel), shape(cell_shape), [], field, z_forward)
    with jax.named_scope("cells_to_planes"):
        cells = cell_exchange(cells)
    with jax.named_scope("plane_analysis"):
        modes, no_sums = plane_analysis(cells)
    with jax.named_scope("planes_to_modes"):
        modes = mode_exchange(modes)
    with jax.named_scope("mix"):
        modes, spectrum = call(
            with_plan(mix_kernel),
            [shape(mode_shape), shape(own_shape)],
            [own, rest],
            modes,
            spectral_weight,
        )
    with jax.named_scope("modes_to_planes"):
        modes = mode_exchange(modes)
    with jax.named_scope("plane_synthesis"):
        cells = plane_synthesis(modes, no_sums)
    with jax.named_scope("planes_to_cells"):
        cells = cell_exchange(cells)
    with jax.named_scope("activation"):
        output, cells, grad_high, grad_low = call(
            with_plan(middle_kernel),
            [
                shape(grid_shape, jnp.bfloat16),
                shape(cell_shape),
                shape(grid_shape, jnp.bfloat16),
                shape(grid_shape, jnp.bfloat16),
            ],
            [grid, lines, pltpu.VMEM((wide, wide), f32), pltpu.VMEM((wide, plan.depth), f32)],
            cells,
            field,
            cotangent,
            pointwise_weight,
            bias,
            scaled_inverse,
            scaled_forward,
            smem=(4,),
        )
    with jax.named_scope("grad_cells_to_planes"):
        cells = cell_exchange(cells)
    with jax.named_scope("grad_plane_analysis"):
        modes, sums = plane_analysis(cells)
    with jax.named_scope("grad_planes_to_modes"):
        modes = mode_exchange(modes)
    with jax.named_scope("grad_mix"):
        modes, grad_mix = call(
            with_plan(mix_back_kernel),
            [shape(mode_shape), shape(own_shape)],
            [own, rest],
            modes,
            spectral_weight,
        )
    with jax.named_scope("grad_modes_to_planes"):
        modes = mode_exchange(modes)
    with jax.named_scope("grad_spectral"):
        grad_spectral = weight_grad(plan, spectrum, grad_mix)
    with jax.named_scope("grad_plane_synthesis"):
        cells = plane_synthesis(modes, sums)
    with jax.named_scope("grad_planes_to_cells"):
        cells = cell_exchange(cells)
    with jax.named_scope("grad_field"):
        grad_field, sums = call(
            with_plan(last_kernel),
            [shape(grid_shape, jnp.bfloat16), shape((24, LANES))],
            [grid, lines],
            cells,
            grad_high,
            grad_low,
            pointwise_weight,
            z_inverse,
        )
    channels = plan.channels
    return output, grad_field, grad_spectral, sums[:channels, :channels], sums[channels, :channels]


def layer(field, cotangent, spectral_weight, pointwise_weight, bias):
    plan = Plan(
        field.shape, spectral_weight.shape, lax.axis_size("gx"), lax.axis_size("gy")
    )
    if plan.fits:
        return by_planes(plan, field, cotangent, spectral_weight, pointwise_weight, bias)
    return local(field, cotangent, spectral_weight, pointwise_weight, bias)


def solution(mesh):
    placed = (
        P(None, "gx", "gy", None),
        P(None, "gx", "gy", None),
        P(None, None, None, "gy", "gx"),
        P(),
        P(),
    )
    return jax.shard_map(
        layer,
        mesh=mesh,
        in_specs=placed,
        out_specs=(
            P(None, "gx", "gy", None),
            P(None, "gx", "gy", None),
            P(None, None, None, "gy", "gx"),
            P(),
            P(),
        ),
        check_vma=False,
    )
```

```python
import functools
import math

import jax
import jax.numpy as jnp
from jax import lax
import numpy as np
from jax.experimental import pallas as pl
from jax.experimental.layout import Layout, with_layout_constraint
from jax.experimental.pallas import tpu as pltpu
from jax.sharding import PartitionSpec as P

MX = 24
MY = 24
MZ = 24


PRECISE = lax.Precision.HIGHEST
TWO_PI = 2.0 * math.pi


def angles(frequencies, places, length):
    product = places[:, None] * frequencies[None, :] % length
    return product.astype(jnp.float32) * (TWO_PI / length)


def frequency(position, kept_modes, length):
    return jnp.where(position < kept_modes, position, position - 2 * kept_modes + length)


def forward_y(values, phases):
    cosine_table = jnp.cos(phases)
    sine_table = jnp.sin(phases)
    with_cos = jnp.einsum("brcxy,yj->brcxj", values, cosine_table, precision=PRECISE)
    with_sin = jnp.einsum("brcxy,yj->brcxj", values, sine_table, precision=PRECISE)
    real_part = with_cos[:, 0] + with_sin[:, 1]
    imag_part = with_cos[:, 1] - with_sin[:, 0]
    return jnp.stack([real_part, imag_part], axis=1)


def inverse_y(values, phases):
    cosine_table = jnp.cos(phases)
    sine_table = jnp.sin(phases)
    with_cos = jnp.einsum("brcxj,yj->brcxy", values, cosine_table, precision=PRECISE)
    with_sin = jnp.einsum("brcxj,yj->brcxy", values, sine_table, precision=PRECISE)
    real_part = with_cos[:, 0] - with_sin[:, 1]
    imag_part = with_sin[:, 0] + with_cos[:, 1]
    return jnp.stack([real_part, imag_part], axis=1)


def local(field, cotangent, spectral_weight, pointwise_weight, bias):
    channels, rows_x, rows_y, depth_cells = field.shape
    blocks_z = spectral_weight.shape[3]
    pair_rows = spectral_weight.shape[4]
    width_x = 2 * MX
    width_y = 2 * MY
    full_x = rows_x * lax.axis_size("gx")
    full_y = rows_y * lax.axis_size("gy")
    cell_count = float(full_x * full_y * depth_cells)
    place_x = lax.axis_index("gx")
    place_y = lax.axis_index("gy")
    own_x = place_x * rows_x + jnp.arange(rows_x, dtype=jnp.int32)
    freq_x = frequency(jnp.arange(width_x, dtype=jnp.int32), MX, full_x)
    freq_y = frequency(jnp.arange(width_y, dtype=jnp.int32), MY, full_y)
    phases_full_y = angles(freq_y, jnp.arange(full_y, dtype=jnp.int32), full_y)
    z_phases = angles(
        jnp.arange(MZ, dtype=jnp.int32), jnp.arange(depth_cells, dtype=jnp.int32), depth_cells
    )
    table_z = jnp.stack([jnp.cos(z_phases), -jnp.sin(z_phases)], axis=2).reshape(
        depth_cells, 2 * MZ
    )
    kz_own = place_y * blocks_z + jnp.arange(blocks_z, dtype=jnp.int32)
    weight_z = (jnp.where(kz_own == 0, 1.0, 2.0).astype(jnp.float32) / cell_count)[None, :, None]
    own_first = place_x * pair_rows
    flat_width = blocks_z * 2 * channels

    def kx_terms(values, places, first_pair, count):
        kx_count = min(count // width_y + 2, width_x)
        kx_first = jnp.minimum(first_pair // width_y, width_x - kx_count)
        kx_ids = kx_first + jnp.arange(kx_count, dtype=jnp.int32)
        phases = angles(frequency(kx_ids, MX, full_x), places, full_x)
        cosine_table = jnp.cos(phases)
        sine_table = jnp.sin(phases)
        real_part = jnp.einsum(
            "bcxj,xi->ijbc", values[:, 0], cosine_table, precision=PRECISE
        ) + jnp.einsum("bcxj,xi->ijbc", values[:, 1], sine_table, precision=PRECISE)
        imag_part = jnp.einsum(
            "bcxj,xi->ijbc", values[:, 1], cosine_table, precision=PRECISE
        ) - jnp.einsum("bcxj,xi->ijbc", values[:, 0], sine_table, precision=PRECISE)
        terms = jnp.stack([real_part, imag_part], axis=3).reshape(kx_count * width_y, flat_width)
        offset = first_pair - kx_first * width_y
        return lax.dynamic_slice_in_dim(terms, offset, count, 0)

    def analyze(values):
        flat = values.reshape(-1, depth_cells)
        spectra = jnp.einsum("zk,mz->km", table_z, flat, precision=PRECISE).reshape(
            2 * MZ, channels, rows_x, rows_y
        )
        columns = lax.all_to_all(spectra, "gy", split_axis=0, concat_axis=3, tiled=True)
        mode_data = forward_y(columns.reshape(blocks_z, 2, channels, rows_x, full_y), phases_full_y)
        portion = lax.all_gather(mode_data, "gx", axis=3, tiled=True)
        places = jnp.arange(portion.shape[3], dtype=jnp.int32)
        owned = kx_terms(portion, places, own_first, pair_rows)
        return jnp.transpose(owned.reshape(pair_rows, blocks_z, 2, channels), (2, 3, 1, 0))

    def synthesize(spectrum):
        portion = lax.all_gather(spectrum, "gx", axis=3, tiled=True)
        blocks = portion.reshape(2, channels, blocks_z, width_x, width_y)
        phases = angles(freq_x, own_x, full_x)
        cosine_table = jnp.cos(phases)
        sine_table = jnp.sin(phases)
        real_part = jnp.einsum(
            "cbij,xi->bcxj", blocks[0], cosine_table, precision=PRECISE
        ) - jnp.einsum("cbij,xi->bcxj", blocks[1], sine_table, precision=PRECISE)
        imag_part = jnp.einsum(
            "cbij,xi->bcxj", blocks[0], sine_table, precision=PRECISE
        ) + jnp.einsum("cbij,xi->bcxj", blocks[1], cosine_table, precision=PRECISE)
        mode_data = jnp.stack([real_part, imag_part], axis=1)
        fields = inverse_y(mode_data, phases_full_y)
        columns = lax.all_to_all(fields, "gy", split_axis=4, concat_axis=0, tiled=True)
        flat = columns.reshape(2 * MZ, -1)
        return jnp.einsum("km,zk->mz", flat, table_z, precision=PRECISE).reshape(
            channels, rows_x, rows_y, depth_cells
        )

    weights = spectral_weight.astype(jnp.float32)
    widened = field.astype(jnp.float32)
    spec_u = analyze(widened)
    mixed_re = jnp.einsum("cobp,cbp->obp", weights[0], spec_u[0], precision=PRECISE) - jnp.einsum(
        "cobp,cbp->obp", weights[1], spec_u[1], precision=PRECISE
    )
    mixed_im = jnp.einsum("cobp,cbp->obp", weights[0], spec_u[1], precision=PRECISE) + jnp.einsum(
        "cobp,cbp->obp", weights[1], spec_u[0], precision=PRECISE
    )
    mixed_modes = jnp.stack([mixed_re, mixed_im]) * weight_z
    conv = synthesize(mixed_modes)
    pointwise = jnp.dot(
        pointwise_weight.T, field.reshape(channels, -1), preferred_element_type=jnp.float32
    ).reshape(field.shape)
    preact = pointwise + bias[:, None, None, None] + conv
    activated, pullback = jax.vjp(jax.nn.gelu, preact)
    gradient = pullback(cotangent.astype(jnp.float32))[0]
    grad_mix = analyze(gradient) * weight_z
    spec_re = jnp.einsum("cobp,obp->cbp", weights[0], grad_mix[0], precision=PRECISE) + jnp.einsum(
        "cobp,obp->cbp", weights[1], grad_mix[1], precision=PRECISE
    )
    spec_im = jnp.einsum("cobp,obp->cbp", weights[0], grad_mix[1], precision=PRECISE) - jnp.einsum(
        "cobp,obp->cbp", weights[1], grad_mix[0], precision=PRECISE
    )
    grad_spec = jnp.stack([spec_re, spec_im])
    weight_re = jnp.einsum("cbp,obp->cobp", spec_u[0], grad_mix[0], precision=PRECISE) + jnp.einsum(
        "cbp,obp->cobp", spec_u[1], grad_mix[1], precision=PRECISE
    )
    weight_im = jnp.einsum("cbp,obp->cobp", spec_u[0], grad_mix[1], precision=PRECISE) - jnp.einsum(
        "cbp,obp->cobp", spec_u[1], grad_mix[0], precision=PRECISE
    )
    grad_spectral = jnp.stack([weight_re, weight_im])
    returned = synthesize(grad_spec)
    grad_flat = gradient.reshape(channels, -1)
    back_point = jnp.dot(
        pointwise_weight.astype(jnp.float32), grad_flat, precision=PRECISE
    ).reshape(field.shape)
    grad_field = (back_point + returned).astype(jnp.bfloat16)
    local_weight = jnp.dot(widened.reshape(channels, -1), grad_flat.T, precision=PRECISE)
    local_bias = jnp.sum(grad_flat, axis=1)
    summed_weight, summed_bias = lax.psum((local_weight, local_bias), ("gx", "gy"))
    shrink = cell_count ** (-0.5)
    return (
        activated.astype(jnp.bfloat16),
        grad_field,
        grad_spectral,
        summed_weight * shrink,
        summed_bias * shrink,
    )


LANES = 128
HALF = 64
SLOT = 32
VMEM_BYTES = 40 * 1024 * 1024


def split_table(table):
    high = table.astype(jnp.bfloat16)
    low = (table - high.astype(np.float64)).astype(jnp.bfloat16)
    return high, low


def frequency_table(kept_modes, length):
    position = np.arange(2 * kept_modes)
    return np.where(position < kept_modes, position, position - 2 * kept_modes + length)


def phase_table(frequencies, places, length):
    product = places[:, None] * frequencies[None, :] % length
    return product.astype(np.float64) * (TWO_PI / length)


def split(values):
    high = values.astype(jnp.bfloat16)
    low = (values - high.astype(jnp.float32)).astype(jnp.bfloat16)
    return high, low


def product(left, right, contract=((1,), (0,)), precision=None):
    return lax.dot_general(
        left, right, (contract, ((), ())), preferred_element_type=jnp.float32, precision=precision
    )


NT = ((1,), (1,))
TN = ((0,), (0,))


def lane_ids(rows):
    return lax.broadcasted_iota(jnp.int32, (rows, LANES), 1)


def roll_lanes(values, shift):
    shift = shift % LANES
    if shift == 0:
        return values
    return pltpu.roll(values, shift, 1)


class Plan:
    def __init__(self, field_shape, weight_shape, size_x, size_y):
        self.channels, self.rows_x, self.rows_y, self.depth = field_shape
        self.size_x, self.size_y = size_x, size_y
        self.blocks_z = weight_shape[3]
        self.pair_rows = weight_shape[4]
        self.full_x = self.rows_x * size_x
        self.full_y = self.rows_y * size_y
        self.width_x, self.width_y = 2 * MX, 2 * MY
        self.cells = self.rows_x * self.rows_y
        self.part_c, self.part_z = 0, 0
        for part_z in range(1, self.blocks_z + 1):
            part_c = size_x // part_z
            if size_x % part_z or self.blocks_z % part_z or self.channels % part_c:
                continue
            self.part_c, self.part_z = part_c, part_z
        self.fits = False
        if self.part_c == 0:
            return
        self.own_c = self.channels // self.part_c
        self.own_z = self.blocks_z // self.part_z
        self.planes = self.own_c * self.own_z
        self.plane_rows = 16
        self.own_kx = self.pair_rows // self.width_y
        self.devices = size_x * size_y
        self.fits = (
            self.cells == LANES
            and self.rows_y == 16
            and self.size_y * 2 == self.rows_x
            and self.depth % LANES == 0
            and self.planes < self.plane_rows
            and self.pair_rows % self.width_y == 0
            and self.pair_rows == 2 * LANES + 32
            and self.width_y <= HALF
            and size_x == 8
            and self.channels <= SLOT
            and self.channels < size_x * (LANES // SLOT)
            and self.own_z * 2 * self.part_z * size_y == 2 * MZ
        )

    def z_table(self, scaled):
        kz = np.arange(MZ)
        phases = phase_table(kz, np.arange(self.depth), self.depth)
        both = np.stack([np.cos(phases), -np.sin(phases)])
        if scaled:
            cells = float(self.full_x * self.full_y * self.depth)
            both = both * (np.where(kz == 0, 1.0, 2.0) / cells)
        both = both.reshape(2, self.depth, self.size_y, self.part_z, self.own_z)
        return both.transpose(2, 3, 0, 4, 1).reshape(2 * MZ, self.depth)

    def y_tables(self):
        freq = frequency_table(MY, self.full_y)
        phases = phase_table(freq, np.arange(self.full_y), self.full_y)
        cosine, sine = np.cos(phases), np.sin(phases)
        one = np.zeros((self.size_y, 2, self.rows_y, 2, HALF))
        by_block = (self.size_y, self.rows_y, self.width_y)
        one[:, 0, :, 0, : self.width_y] = cosine.reshape(by_block)
        one[:, 1, :, 0, : self.width_y] = sine.reshape(by_block)
        one[:, 0, :, 1, : self.width_y] = -sine.reshape(by_block)
        one[:, 1, :, 1, : self.width_y] = cosine.reshape(by_block)
        one = one.reshape(LANES, LANES)
        tables = []
        for table in (one, one.T):
            high, low = split_table(table)
            top = np.concatenate([high, low], axis=1)
            bottom = np.concatenate([high, np.zeros_like(low)], axis=1)
            tables.append(np.concatenate([top, bottom], axis=0))
        return tables

    def x_tables(self):
        freq = frequency_table(MX, self.full_x)
        phases = phase_table(freq, np.arange(self.full_x), self.full_x)
        phases = phases.reshape(self.size_x, self.rows_x, self.width_x).transpose(1, 0, 2)
        phases = phases.reshape(self.full_x, self.width_x)
        cosine, sine = np.cos(phases), np.sin(phases)
        forward = np.concatenate([cosine.T, sine.T], axis=0)
        inverse = np.concatenate([cosine, sine], axis=0)
        tables = []
        for table in (forward, inverse):
            high, low = split_table(table)
            tables.append(np.concatenate([high, low, high], axis=1))
        return tables


def call(kernel, out_shape, scratch, *operands, smem=(), **more):
    specs = [
        pl.BlockSpec(memory_space=pltpu.SMEM if at in smem else pltpu.VMEM)
        for at in range(len(operands))
    ]
    single = not isinstance(out_shape, (tuple, list))
    outs = pl.BlockSpec(memory_space=pltpu.VMEM)
    return pl.pallas_call(
        kernel,
        out_shape=out_shape,
        in_specs=specs,
        out_specs=outs if single else [outs] * len(out_shape),
        scratch_shapes=scratch,
        compiler_params=pltpu.CompilerParams(vmem_limit_bytes=VMEM_BYTES),
        **more,
    )(*operands)


def put_spectrum(plan, out_ref, channel, rows):
    block, inner = divmod(channel, plan.own_c)
    size = plan.own_z
    at = 0
    for place_y in range(plan.size_y):
        for part in range(plan.part_z):
            place_x = block * plan.part_z + part
            for which in range(2):
                out_ref[place_x, place_y, which, inner * size : (inner + 1) * size, :] = rows[
                    at : at + size
                ]
                at += size


def take_spectrum(plan, in_ref, rows_ref, channel):
    block, inner = divmod(channel, plan.own_c)
    size = plan.own_z
    at = 0
    for place_y in range(plan.size_y):
        for part in range(plan.part_z):
            place_x = block * plan.part_z + part
            for which in range(2):
                rows_ref[at : at + size, :] = in_ref[
                    place_x, place_y, which, inner * size : (inner + 1) * size, :
                ]
                at += size
    return rows_ref[...]


def clear_spare(plan, out_ref):
    zeros = jnp.zeros((plan.plane_rows - plan.planes, LANES), jnp.float32)
    for place_x in range(plan.size_x):
        for place_y in range(plan.size_y):
            for which in range(2):
                out_ref[place_x, place_y, which, plan.planes :, :] = zeros


def depth_analysis_kernel(plan, field_ref, table_ref, out_ref):
    clear_spare(plan, out_ref)
    table = table_ref[...]
    for channel in range(plan.channels):
        block = field_ref[channel].reshape(plan.cells, plan.depth)
        both = product(table, block, NT)
        put_spectrum(plan, out_ref, channel, both[: 2 * MZ] + both[2 * MZ :])


def swap_blocks(values, block):
    values = list(values)
    lanes = lane_ids(values[0].shape[0])
    step = 1
    while step < len(values):
        low = jnp.bitwise_and(lanes, step * block) == 0
        for at in range(len(values)):
            if at & step:
                continue
            first, second = values[at], values[at + step]
            values[at] = jnp.where(low, first, roll_lanes(second, step * block))
            values[at + step] = jnp.where(low, roll_lanes(first, -step * block), second)
        step *= 2
    return values


def along_y(values, table):
    high, low = split(values)
    both = product(jnp.concatenate([high, low], axis=1), table)
    return both[:, :LANES] + both[:, LANES:]


def plane_analysis_kernel(
    plan, in_ref, extra_ref, y_ref, x_ref, out_ref, rows_ref, modes_ref, rest_ref
):
    pad = plan.plane_rows
    left = [
        in_ref[:, place_y, which].reshape(plan.size_x * pad, LANES)
        for place_y in range(plan.size_y)
        for which in range(2)
    ]
    rows_ref[...] = along_y(
        jnp.concatenate(swap_blocks(left, plan.rows_y), axis=0), y_ref[...]
    )
    right = jnp.concatenate(
        [rows_ref[pl.ds(plane, plan.full_x, stride=pad), :] for plane in range(plan.planes)], axis=1
    )
    high, low = split(right)
    both = product(x_ref[...], jnp.concatenate([high, high, low], axis=0))
    sign = jnp.where(lane_ids(plan.width_x) < HALF, 1.0, -1.0)
    for plane in range(plan.planes):
        mine = slice(plane * LANES, (plane + 1) * LANES)
        turned = roll_lanes(both[plan.width_x :, mine], HALF)
        modes_ref[pl.ds(plane, plan.width_x, stride=pad), :] = (
            both[: plan.width_x, mine] + sign * turned
        )
    modes_ref[pl.ds(plan.planes, plan.width_x, stride=pad), :] = jnp.zeros(
        (plan.width_x, LANES), jnp.float32
    )
    lanes = lane_ids(pad)
    width = plan.width_y
    for place_x in range(plan.size_x):
        for which in range(2):
            tiles = [None, None, None]
            for inner in range(plan.own_kx):
                kx = place_x * plan.own_kx + inner
                first = inner * width
                turned = roll_lanes(modes_ref[kx * pad : (kx + 1) * pad, :], first - which * HALF)
                tile, offset = divmod(first, LANES)
                for at in (tile, tile + 1):
                    begin = first - at * LANES
                    if begin >= LANES or begin + width <= 0:
                        continue
                    if tiles[at] is None:
                        tiles[at] = turned
                    else:
                        tiles[at] = jnp.where(lanes < begin, tiles[at], turned)
            for at in range(2):
                row = at * 2 * pad + which * pad
                out_ref[place_x, row : row + pad, :] = tiles[at]
            rest_ref[which * pad : (which + 1) * pad, :] = tiles[2]
        out_ref[place_x, 4 * pad : 4 * pad + 8, :] = pack_rest(rest_ref)
        out_ref[place_x, plan.planes : plan.planes + 1, :] = extra_ref[place_x : place_x + 1, :]


def pack_rest(rest_ref):
    lanes = lane_ids(8)
    packed = rest_ref[0:8, :]
    for group in range(1, 4):
        turned = roll_lanes(rest_ref[group * 8 : (group + 1) * 8, :], group * 32)
        packed = jnp.where(lanes < group * 32, packed, turned)
    return packed


def unpack_rest(packed, rest_ref):
    for group in range(4):
        rest_ref[group * 8 : (group + 1) * 8, :] = roll_lanes(packed, -group * 32)


def take_modes(plan, in_ref, modes_ref, rest_ref):
    pad, size = plan.plane_rows, plan.own_z
    for place_x in range(plan.size_x):
        block, part = divmod(place_x, plan.part_z)
        unpack_rest(in_ref[place_x, 4 * pad : 4 * pad + 8, :], rest_ref)
        for which in range(2):
            for inner in range(plan.own_c):
                channel = block * plan.own_c + inner
                row = which * pad + inner * size
                kz = slice(part * size, (part + 1) * size)
                for at in range(2):
                    begin = at * 2 * pad + row
                    modes_ref[channel, which, kz, at * LANES : (at + 1) * LANES] = in_ref[
                        place_x, begin : begin + size, :
                    ]
                modes_ref[channel, which, kz, 2 * LANES :] = rest_ref[row : row + size, 0:32]


def put_modes(plan, modes_ref, out_ref, rest_ref):
    pad, size = plan.plane_rows, plan.own_z
    zeros = jnp.zeros((pad - plan.planes, LANES), jnp.float32)
    rest_ref[...] = jnp.zeros((2 * pad, LANES), jnp.float32)
    for place_x in range(plan.size_x):
        block, part = divmod(place_x, plan.part_z)
        for which in range(2):
            for inner in range(plan.own_c):
                channel = block * plan.own_c + inner
                row = which * pad + inner * size
                kz = slice(part * size, (part + 1) * size)
                for at in range(2):
                    begin = at * 2 * pad + row
                    out_ref[place_x, begin : begin + size, :] = modes_ref[
                        channel, which, kz, at * LANES : (at + 1) * LANES
                    ]
                rest_ref[row : row + size, 0:32] = modes_ref[channel, which, kz, 2 * LANES :]
            for at in range(2):
                begin = at * 2 * pad + which * pad + plan.planes
                out_ref[place_x, begin : begin + pad - plan.planes, :] = zeros
        out_ref[place_x, 4 * pad : 4 * pad + 8, :] = pack_rest(rest_ref)


def mix_kernel(plan, in_ref, weight_ref, out_ref, spectrum_ref, mixed_ref, rest_ref):
    take_modes(plan, in_ref, spectrum_ref, rest_ref)
    shape = (plan.blocks_z, plan.pair_rows)

    def one(out_channel, carry):
        real_part = jnp.zeros(shape, jnp.float32)
        imag_part = jnp.zeros(shape, jnp.float32)
        for channel in range(plan.channels):
            weight_re = weight_ref[0, channel, out_channel].astype(jnp.float32)
            weight_im = weight_ref[1, channel, out_channel].astype(jnp.float32)
            value_re = spectrum_ref[channel, 0]
            value_im = spectrum_ref[channel, 1]
            real_part += weight_re * value_re - weight_im * value_im
            imag_part += weight_re * value_im + weight_im * value_re
        mixed_ref[out_channel, 0] = real_part
        mixed_ref[out_channel, 1] = imag_part
        return carry

    lax.fori_loop(0, plan.channels, one, 0)
    put_modes(plan, mixed_ref, out_ref, rest_ref)


def mix_back_kernel(plan, in_ref, weight_ref, out_ref, grad_ref, sums_ref, mixed_ref, rest_ref):
    spare = jnp.zeros((1, LANES), jnp.float32)
    for place_x in range(plan.size_x):
        spare = spare + in_ref[place_x, plan.planes : plan.planes + 1, :]
    sums_ref[...] = jnp.broadcast_to(spare, (8, LANES))
    take_modes(plan, in_ref, grad_ref, rest_ref)
    shape = (plan.blocks_z, plan.pair_rows)

    def one(channel, carry):
        real_part = jnp.zeros(shape, jnp.float32)
        imag_part = jnp.zeros(shape, jnp.float32)
        for out_channel in range(plan.channels):
            weight_re = weight_ref[0, channel, out_channel].astype(jnp.float32)
            weight_im = weight_ref[1, channel, out_channel].astype(jnp.float32)
            value_re = grad_ref[out_channel, 0]
            value_im = grad_ref[out_channel, 1]
            real_part += weight_re * value_re + weight_im * value_im
            imag_part += weight_re * value_im - weight_im * value_re
        mixed_ref[channel, 0] = real_part
        mixed_ref[channel, 1] = imag_part
        return carry

    lax.fori_loop(0, plan.channels, one, 0)
    put_modes(plan, mixed_ref, out_ref, rest_ref)


def weight_grad_kernel(plan, spectrum_ref, grad_ref, out_ref):
    value_re = spectrum_ref[0, 0]
    value_im = spectrum_ref[0, 1]
    for out_channel in range(plan.channels):
        grad_re = grad_ref[out_channel, 0]
        grad_im = grad_ref[out_channel, 1]
        out_ref[0, 0, out_channel] = value_re * grad_re + value_im * grad_im
        out_ref[1, 0, out_channel] = value_re * grad_im - value_im * grad_re


def weight_grad(plan, spectrum, grad):
    modes = (plan.blocks_z, plan.pair_rows)
    return pl.pallas_call(
        functools.partial(weight_grad_kernel, plan),
        grid=(plan.channels,),
        out_shape=jax.ShapeDtypeStruct((2, plan.channels, plan.channels) + modes, jnp.float32),
        in_specs=[
            pl.BlockSpec((1, 2) + modes, lambda channel: (channel, 0, 0, 0)),
            pl.BlockSpec((plan.channels, 2) + modes, lambda channel: (0, 0, 0, 0)),
        ],
        out_specs=pl.BlockSpec(
            (2, 1, plan.channels) + modes, lambda channel: (0, channel, 0, 0, 0)
        ),
        compiler_params=pltpu.CompilerParams(vmem_limit_bytes=VMEM_BYTES),
    )(spectrum, grad)


def plane_synthesis_kernel(
    plan, in_ref, extra_ref, y_ref, x_ref, out_ref, rows_ref, modes_ref, rest_ref
):
    pad, width = plan.plane_rows, plan.width_y
    lanes = lane_ids(pad)
    for place_x in range(plan.size_x):
        unpack_rest(in_ref[place_x, 4 * pad : 4 * pad + 8, :], rest_ref)
        tiles = []
        for which in range(2):
            row = which * pad
            tiles.append(
                [
                    in_ref[place_x, row : row + pad, :],
                    in_ref[place_x, 2 * pad + row : 3 * pad + row, :],
                    rest_ref[row : row + pad, :],
                ]
            )
        for inner in range(plan.own_kx):
            first = inner * width
            tile, offset = divmod(first, LANES)
            pieces = []
            for which in range(2):
                piece = roll_lanes(tiles[which][tile], which * HALF - offset)
                if offset + width > LANES:
                    later = roll_lanes(tiles[which][tile + 1], which * HALF - offset)
                    piece = jnp.where(lanes < which * HALF + LANES - offset, piece, later)
                pieces.append(piece)
            merged = jnp.where(lanes < HALF, pieces[0], pieces[1])
            used = jnp.bitwise_and(lanes, HALF - 1) < width
            at = (place_x * plan.own_kx + inner) * pad
            modes_ref[at : at + pad, :] = jnp.where(used, merged, 0.0)
    right = jnp.concatenate(
        [modes_ref[pl.ds(plane, plan.width_x, stride=pad), :] for plane in range(plan.planes)],
        axis=1,
    )
    high, low = split(right)
    both = product(x_ref[...], jnp.concatenate([high, high, low], axis=0))
    sign = jnp.where(lane_ids(plan.full_x) < HALF, -1.0, 1.0)
    for plane in range(plan.planes):
        mine = slice(plane * LANES, (plane + 1) * LANES)
        turned = roll_lanes(both[plan.full_x :, mine], HALF)
        rows_ref[pl.ds(plane, plan.full_x, stride=pad), :] = (
            both[: plan.full_x, mine] + sign * turned
        )
    rows_ref[pl.ds(plan.planes, plan.full_x, stride=pad), :] = jnp.zeros(
        (plan.full_x, LANES), jnp.float32
    )
    cells = along_y(rows_ref[...], y_ref[...])
    size = plan.size_x * pad
    cells = swap_blocks(
        [cells[row * size : (row + 1) * size] for row in range(plan.rows_x)], plan.rows_y
    )
    for place_y in range(plan.size_y):
        for which in range(2):
            out_ref[:, place_y, which] = cells[place_y * 2 + which].reshape(
                plan.size_x, pad, LANES
            )
    spare = extra_ref[0:1, :]
    for place_x in range(plan.size_x):
        for place_y in range(plan.size_y):
            out_ref[place_x, place_y, 0, plan.planes : plan.planes + 1, :] = spare


def widen_map(plan, small, transposed):
    rows = plan.channels * plan.rows_y
    row_ids = lax.broadcasted_iota(jnp.int32, (rows, plan.channels), 0)
    column_ids = lax.broadcasted_iota(jnp.int32, (rows, plan.channels), 1)
    spread = jnp.where(row_ids // plan.rows_y == column_ids, 1.0, 0.0).astype(jnp.bfloat16)
    wide = product(spread, small, ((1,), (0,)) if transposed else ((1,), (1,)))
    wide = product(wide.astype(jnp.bfloat16), spread, NT)
    return jnp.where(same_cell(plan), wide, 0.0).astype(jnp.bfloat16)


def same_cell(plan):
    rows = plan.channels * plan.rows_y
    row_ids = lax.broadcasted_iota(jnp.int32, (rows, rows), 0)
    column_ids = lax.broadcasted_iota(jnp.int32, (rows, rows), 1)
    return jnp.bitwise_and(row_ids, plan.rows_y - 1) == jnp.bitwise_and(
        column_ids, plan.rows_y - 1
    )


def synthesize_depth(plan, in_ref, rows_ref, table, channel):
    rows = take_spectrum(plan, in_ref, rows_ref, channel)
    high, low = split(rows)
    return product(jnp.concatenate([high, high, low], axis=0), table, TN)


def pointwise_kernel(plan, field_ref, map_ref, bias_ref, out_ref):
    rows, size = plan.channels * plan.rows_y, plan.rows_y
    wide = widen_map(plan, map_ref[...], False)

    def one(row, carry):
        here = pl.ds(row, 1)
        mapped = product(wide, field_ref[:, here].reshape(rows, plan.depth))
        for channel in range(plan.channels):
            part = mapped[channel * size : (channel + 1) * size] + bias_ref[channel]
            out_ref[channel, here] = part.reshape(1, size, plan.depth)
        return carry

    lax.fori_loop(0, plan.rows_x, one, 0)


def activation_kernel(
    plan,
    in_ref,
    pointwise_ref,
    cotangent_ref,
    inverse_ref,
    forward_ref,
    output_ref,
    spectrum_ref,
    high_ref,
    low_ref,
    rows_ref,
):
    clear_spare(plan, spectrum_ref)
    flat = (plan.cells, plan.depth)
    block = (plan.rows_x, plan.rows_y, plan.depth)
    inverse = inverse_ref[...]
    forward = forward_ref[...]
    scale = math.sqrt(2.0 / math.pi)
    for channel in range(plan.channels):
        preact = synthesize_depth(plan, in_ref, rows_ref, inverse, channel)
        preact = preact + pointwise_ref[channel].reshape(flat)
        square = preact * preact
        bend = jnp.tanh(scale * preact * (1.0 + 0.044715 * square))
        half = 0.5 * (1.0 + bend)
        output_ref[channel] = (preact * half).astype(jnp.bfloat16).reshape(block)
        slope = half + (0.5 * scale) * preact * (1.0 - bend * bend) * (
            1.0 + (3.0 * 0.044715) * square
        )
        grad = cotangent_ref[channel].reshape(flat).astype(jnp.float32) * slope
        high, low = split(grad)
        high_ref[channel] = high.reshape(block)
        low_ref[channel] = low.reshape(block)
        both = product(forward, high, NT)
        more = product(forward[: 2 * MZ], low, NT)
        put_spectrum(plan, spectrum_ref, channel, both[: 2 * MZ] + both[2 * MZ :] + more)


def pointwise_grad_kernel(
    plan, field_ref, high_ref, low_ref, map_ref, back_ref, sums_ref, cross_ref
):
    rows = plan.channels * plan.rows_y
    wide = widen_map(plan, map_ref[...], True)
    cross_ref[...] = jnp.zeros((rows + 16, rows), jnp.float32)
    ones = jnp.ones((16, plan.depth), jnp.bfloat16)
    slab = (plan.channels, 1, plan.rows_y, plan.depth)

    def one(row, carry):
        here = pl.ds(row, 1)
        values = field_ref[:, here].reshape(rows, plan.depth)
        values = jnp.concatenate([values, ones], axis=0)
        high = high_ref[:, here].reshape(rows, plan.depth)
        low = low_ref[:, here].reshape(rows, plan.depth)
        back_ref[:, here] = (product(wide, high) + product(wide, low)).reshape(slab)
        cross_ref[...] += product(values, high, NT) + product(values, low, NT)
        return carry

    lax.fori_loop(0, plan.rows_x, one, 0)
    row_ids = lax.broadcasted_iota(jnp.int32, (rows, LANES), 0)
    gather = jnp.where(row_ids // plan.rows_y == lane_ids(rows), 1.0, 0.0)
    exact = lax.Precision.HIGHEST
    cross = jnp.where(same_cell(plan), cross_ref[:rows], 0.0)
    by_out = product(cross, gather, precision=exact)
    sums = product(gather, by_out, TN, precision=exact)
    bias_sums = product(cross_ref[rows : rows + 8], gather, precision=exact)
    lanes = lane_ids(1)
    per_row = LANES // SLOT
    for at in range(8):
        packed = jnp.zeros((1, LANES), jnp.float32)
        for slot in range(per_row):
            row = at * per_row + slot
            if row > plan.channels:
                continue
            line = sums[row : row + 1] if row < plan.channels else bias_sums[0:1]
            packed = jnp.where(lanes // SLOT == slot, roll_lanes(line, slot * SLOT), packed)
        sums_ref[at : at + 1, :] = packed


def last_kernel(
    plan, in_ref, back_ref, inverse_ref, grad_ref, map_grad_ref, bias_grad_ref, rows_ref
):
    block = (plan.rows_x, plan.rows_y, plan.depth)
    flat = (plan.cells, plan.depth)
    inverse = inverse_ref[...]
    for channel in range(plan.channels):
        total = synthesize_depth(plan, in_ref, rows_ref, inverse, channel)
        total = total + back_ref[channel].reshape(flat)
        grad_ref[channel] = total.astype(jnp.bfloat16).reshape(block)
    shrink = float(plan.full_x * plan.full_y * plan.depth) ** (-0.5)
    per_row = LANES // SLOT
    for at in range(plan.size_x):
        line = jnp.zeros((1, LANES), jnp.float32)
        for place_y in range(plan.size_y):
            line = line + in_ref[at, place_y, 0, plan.planes : plan.planes + 1, :]
        for slot in range(per_row):
            row = at * per_row + slot
            mine = shrink * roll_lanes(line, -slot * SLOT)[:, : plan.channels]
            if row < plan.channels:
                map_grad_ref[row : row + 1, :] = mine
            elif row == plan.channels:
                bias_grad_ref[...] = mine


def by_planes(plan, field, cotangent, spectral_weight, pointwise_weight, bias):
    pad = plan.plane_rows
    f32 = jnp.float32
    cell_shape = (plan.size_x, plan.size_y, 2, pad, LANES)
    mode_shape = (plan.size_x, 4 * pad + 8, LANES)
    own_shape = (plan.channels, 2, plan.blocks_z, plan.pair_rows)
    grid_shape = field.shape

    def shape(dims, kind=f32):
        return jax.ShapeDtypeStruct(dims, kind)

    def cell_exchange(values):
        flat = values.reshape(plan.devices, 2 * pad, LANES)
        return lax.all_to_all(flat, ("gx", "gy"), 0, 0, tiled=True).reshape(cell_shape)

    def mode_exchange(values):
        return lax.all_to_all(values, "gx", 0, 0, tiled=True)

    z_high, z_low = split_table(plan.z_table(False))
    scaled_high, scaled_low = split_table(plan.z_table(True))
    z_forward = jnp.asarray(np.concatenate([z_high, z_low]))
    z_inverse = jnp.asarray(np.concatenate([z_high, z_low, z_high]))
    scaled_forward = jnp.asarray(np.concatenate([scaled_high, scaled_low]))
    scaled_inverse = jnp.asarray(np.concatenate([scaled_high, scaled_low, scaled_high]))
    y_forward, y_inverse = (jnp.asarray(table) for table in plan.y_tables())
    x_forward, x_inverse = (jnp.asarray(table) for table in plan.x_tables())

    lane_rows = pltpu.VMEM((plan.full_x * pad, LANES), f32)
    lane_modes = pltpu.VMEM((plan.width_x * pad, LANES), f32)
    rest = pltpu.VMEM((2 * pad, LANES), f32)
    own = pltpu.VMEM(own_shape, f32)
    lines = pltpu.VMEM((2 * MZ, LANES), f32)
    wide = plan.channels * plan.rows_y
    row_shape = shape((8, LANES))

    def with_plan(kernel):
        return functools.partial(kernel, plan)

    def plane_analysis(cells, extra):
        return call(
            with_plan(plane_analysis_kernel),
            shape(mode_shape),
            [lane_rows, lane_modes, rest],
            cells,
            extra,
            y_forward,
            x_forward,
        )

    def plane_synthesis(modes, extra):
        return call(
            with_plan(plane_synthesis_kernel),
            shape(cell_shape),
            [lane_rows, lane_modes, rest],
            modes,
            extra,
            y_inverse,
            x_inverse,
        )

    nothing = jnp.zeros((8, LANES), f32)
    with jax.named_scope("depth_analysis"):
        cells = call(with_plan(depth_analysis_kernel), shape(cell_shape), [], field, z_forward)
    with jax.named_scope("cells_to_planes"):
        cells = cell_exchange(cells)
    with jax.named_scope("pointwise"):
        pointwise = call(
            with_plan(pointwise_kernel),
            shape(grid_shape),
            [],
            field,
            pointwise_weight,
            bias,
            smem=(2,),
        )
        weights = with_layout_constraint(spectral_weight, Layout((0, 1, 2, 3, 4)))
        cells, pointwise, weights = lax.optimization_barrier((cells, pointwise, weights))
    with jax.named_scope("plane_analysis"):
        modes = plane_analysis(cells, nothing)
    with jax.named_scope("planes_to_modes"):
        modes = mode_exchange(modes)
    with jax.named_scope("mix"):
        modes, spectrum = call(
            with_plan(mix_kernel),
            [shape(mode_shape), shape(own_shape)],
            [own, rest],
            modes,
            weights,
        )
    with jax.named_scope("modes_to_planes"):
        modes = mode_exchange(modes)
    with jax.named_scope("plane_synthesis"):
        cells = plane_synthesis(modes, nothing)
    with jax.named_scope("planes_to_cells"):
        cells = cell_exchange(cells)
    with jax.named_scope("activation"):
        half_grid = shape(grid_shape, jnp.bfloat16)
        output, cells, grad_high, grad_low = call(
            with_plan(activation_kernel),
            [half_grid, shape(cell_shape), half_grid, half_grid],
            [lines],
            cells,
            pointwise,
            cotangent,
            scaled_inverse,
            scaled_forward,
        )
    with jax.named_scope("grad_cells_to_planes"):
        cells = cell_exchange(cells)
    with jax.named_scope("pointwise_grad"):
        back, sums = call(
            with_plan(pointwise_grad_kernel),
            [shape(grid_shape), row_shape],
            [pltpu.VMEM((wide + 16, wide), f32)],
            field,
            grad_high,
            grad_low,
            pointwise_weight,
        )
        cells, back, sums = lax.optimization_barrier((cells, back, sums))
    with jax.named_scope("grad_plane_analysis"):
        modes = plane_analysis(cells, sums)
    with jax.named_scope("grad_planes_to_modes"):
        modes = mode_exchange(modes)
    with jax.named_scope("grad_mix"):
        modes, grad_mix, sums = call(
            with_plan(mix_back_kernel),
            [shape(mode_shape), shape(own_shape), row_shape],
            [own, rest],
            modes,
            weights,
        )
    with jax.named_scope("grad_modes_to_planes"):
        modes = mode_exchange(modes)
    with jax.named_scope("grad_spectral"):
        grad_spectral = weight_grad(plan, spectrum, grad_mix)
        modes, grad_spectral = lax.optimization_barrier((modes, grad_spectral))
    with jax.named_scope("grad_plane_synthesis"):
        cells = plane_synthesis(modes, sums)
    with jax.named_scope("grad_planes_to_cells"):
        cells = cell_exchange(cells)
    with jax.named_scope("grad_field"):
        channels = plan.channels
        grad_field, map_grad, bias_grad = call(
            with_plan(last_kernel),
            [half_grid, shape((channels, channels)), shape((1, channels))],
            [lines],
            cells,
            back,
            z_inverse,
        )
    return output, grad_field, grad_spectral, map_grad, bias_grad.reshape(channels)


def layer(field, cotangent, spectral_weight, pointwise_weight, bias):
    plan = Plan(
        field.shape, spectral_weight.shape, lax.axis_size("gx"), lax.axis_size("gy")
    )
    if plan.fits:
        return by_planes(plan, field, cotangent, spectral_weight, pointwise_weight, bias)
    return local(field, cotangent, spectral_weight, pointwise_weight, bias)


def solution(mesh):
    placed = (
        P(None, "gx", "gy", None),
        P(None, "gx", "gy", None),
        P(None, None, None, "gy", "gx"),
        P(),
        P(),
    )
    return jax.shard_map(
        layer,
        mesh=mesh,
        in_specs=placed,
        out_specs=(
            P(None, "gx", "gy", None),
            P(None, "gx", "gy", None),
            P(None, None, None, "gy", "gx"),
            P(),
            P(),
        ),
        check_vma=False,
    )
```

```python
import functools
import math

import jax
import jax.numpy as jnp
from jax import lax
import numpy as np
from jax.experimental import pallas as pl
from jax.experimental.layout import Layout, with_layout_constraint
from jax.experimental.pallas import tpu as pltpu
from jax.sharding import PartitionSpec as P

MX = 24
MY = 24
MZ = 24


PRECISE = lax.Precision.HIGHEST
TWO_PI = 2.0 * math.pi


def angles(frequencies, places, length):
    product = places[:, None] * frequencies[None, :] % length
    return product.astype(jnp.float32) * (TWO_PI / length)


def frequency(position, kept_modes, length):
    return jnp.where(position < kept_modes, position, position - 2 * kept_modes + length)


def forward_y(values, phases):
    cosine_table = jnp.cos(phases)
    sine_table = jnp.sin(phases)
    with_cos = jnp.einsum("brcxy,yj->brcxj", values, cosine_table, precision=PRECISE)
    with_sin = jnp.einsum("brcxy,yj->brcxj", values, sine_table, precision=PRECISE)
    real_part = with_cos[:, 0] + with_sin[:, 1]
    imag_part = with_cos[:, 1] - with_sin[:, 0]
    return jnp.stack([real_part, imag_part], axis=1)


def inverse_y(values, phases):
    cosine_table = jnp.cos(phases)
    sine_table = jnp.sin(phases)
    with_cos = jnp.einsum("brcxj,yj->brcxy", values, cosine_table, precision=PRECISE)
    with_sin = jnp.einsum("brcxj,yj->brcxy", values, sine_table, precision=PRECISE)
    real_part = with_cos[:, 0] - with_sin[:, 1]
    imag_part = with_sin[:, 0] + with_cos[:, 1]
    return jnp.stack([real_part, imag_part], axis=1)


def local(field, cotangent, spectral_weight, pointwise_weight, bias):
    channels, rows_x, rows_y, depth_cells = field.shape
    blocks_z = spectral_weight.shape[3]
    pair_rows = spectral_weight.shape[4]
    width_x = 2 * MX
    width_y = 2 * MY
    full_x = rows_x * lax.axis_size("gx")
    full_y = rows_y * lax.axis_size("gy")
    cell_count = float(full_x * full_y * depth_cells)
    place_x = lax.axis_index("gx")
    place_y = lax.axis_index("gy")
    own_x = place_x * rows_x + jnp.arange(rows_x, dtype=jnp.int32)
    freq_x = frequency(jnp.arange(width_x, dtype=jnp.int32), MX, full_x)
    freq_y = frequency(jnp.arange(width_y, dtype=jnp.int32), MY, full_y)
    phases_full_y = angles(freq_y, jnp.arange(full_y, dtype=jnp.int32), full_y)
    z_phases = angles(
        jnp.arange(MZ, dtype=jnp.int32), jnp.arange(depth_cells, dtype=jnp.int32), depth_cells
    )
    table_z = jnp.stack([jnp.cos(z_phases), -jnp.sin(z_phases)], axis=2).reshape(
        depth_cells, 2 * MZ
    )
    kz_own = place_y * blocks_z + jnp.arange(blocks_z, dtype=jnp.int32)
    weight_z = (jnp.where(kz_own == 0, 1.0, 2.0).astype(jnp.float32) / cell_count)[None, :, None]
    own_first = place_x * pair_rows
    flat_width = blocks_z * 2 * channels

    def kx_terms(values, places, first_pair, count):
        kx_count = min(count // width_y + 2, width_x)
        kx_first = jnp.minimum(first_pair // width_y, width_x - kx_count)
        kx_ids = kx_first + jnp.arange(kx_count, dtype=jnp.int32)
        phases = angles(frequency(kx_ids, MX, full_x), places, full_x)
        cosine_table = jnp.cos(phases)
        sine_table = jnp.sin(phases)
        real_part = jnp.einsum(
            "bcxj,xi->ijbc", values[:, 0], cosine_table, precision=PRECISE
        ) + jnp.einsum("bcxj,xi->ijbc", values[:, 1], sine_table, precision=PRECISE)
        imag_part = jnp.einsum(
            "bcxj,xi->ijbc", values[:, 1], cosine_table, precision=PRECISE
        ) - jnp.einsum("bcxj,xi->ijbc", values[:, 0], sine_table, precision=PRECISE)
        terms = jnp.stack([real_part, imag_part], axis=3).reshape(kx_count * width_y, flat_width)
        offset = first_pair - kx_first * width_y
        return lax.dynamic_slice_in_dim(terms, offset, count, 0)

    def analyze(values):
        flat = values.reshape(-1, depth_cells)
        spectra = jnp.einsum("zk,mz->km", table_z, flat, precision=PRECISE).reshape(
            2 * MZ, channels, rows_x, rows_y
        )
        columns = lax.all_to_all(spectra, "gy", split_axis=0, concat_axis=3, tiled=True)
        mode_data = forward_y(columns.reshape(blocks_z, 2, channels, rows_x, full_y), phases_full_y)
        portion = lax.all_gather(mode_data, "gx", axis=3, tiled=True)
        places = jnp.arange(portion.shape[3], dtype=jnp.int32)
        owned = kx_terms(portion, places, own_first, pair_rows)
        return jnp.transpose(owned.reshape(pair_rows, blocks_z, 2, channels), (2, 3, 1, 0))

    def synthesize(spectrum):
        portion = lax.all_gather(spectrum, "gx", axis=3, tiled=True)
        blocks = portion.reshape(2, channels, blocks_z, width_x, width_y)
        phases = angles(freq_x, own_x, full_x)
        cosine_table = jnp.cos(phases)
        sine_table = jnp.sin(phases)
        real_part = jnp.einsum(
            "cbij,xi->bcxj", blocks[0], cosine_table, precision=PRECISE
        ) - jnp.einsum("cbij,xi->bcxj", blocks[1], sine_table, precision=PRECISE)
        imag_part = jnp.einsum(
            "cbij,xi->bcxj", blocks[0], sine_table, precision=PRECISE
        ) + jnp.einsum("cbij,xi->bcxj", blocks[1], cosine_table, precision=PRECISE)
        mode_data = jnp.stack([real_part, imag_part], axis=1)
        fields = inverse_y(mode_data, phases_full_y)
        columns = lax.all_to_all(fields, "gy", split_axis=4, concat_axis=0, tiled=True)
        flat = columns.reshape(2 * MZ, -1)
        return jnp.einsum("km,zk->mz", flat, table_z, precision=PRECISE).reshape(
            channels, rows_x, rows_y, depth_cells
        )

    weights = spectral_weight.astype(jnp.float32)
    widened = field.astype(jnp.float32)
    spec_u = analyze(widened)
    mixed_re = jnp.einsum("cobp,cbp->obp", weights[0], spec_u[0], precision=PRECISE) - jnp.einsum(
        "cobp,cbp->obp", weights[1], spec_u[1], precision=PRECISE
    )
    mixed_im = jnp.einsum("cobp,cbp->obp", weights[0], spec_u[1], precision=PRECISE) + jnp.einsum(
        "cobp,cbp->obp", weights[1], spec_u[0], precision=PRECISE
    )
    mixed_modes = jnp.stack([mixed_re, mixed_im]) * weight_z
    conv = synthesize(mixed_modes)
    pointwise = jnp.dot(
        pointwise_weight.T, field.reshape(channels, -1), preferred_element_type=jnp.float32
    ).reshape(field.shape)
    preact = pointwise + bias[:, None, None, None] + conv
    activated, pullback = jax.vjp(jax.nn.gelu, preact)
    gradient = pullback(cotangent.astype(jnp.float32))[0]
    grad_mix = analyze(gradient) * weight_z
    spec_re = jnp.einsum("cobp,obp->cbp", weights[0], grad_mix[0], precision=PRECISE) + jnp.einsum(
        "cobp,obp->cbp", weights[1], grad_mix[1], precision=PRECISE
    )
    spec_im = jnp.einsum("cobp,obp->cbp", weights[0], grad_mix[1], precision=PRECISE) - jnp.einsum(
        "cobp,obp->cbp", weights[1], grad_mix[0], precision=PRECISE
    )
    grad_spec = jnp.stack([spec_re, spec_im])
    weight_re = jnp.einsum("cbp,obp->cobp", spec_u[0], grad_mix[0], precision=PRECISE) + jnp.einsum(
        "cbp,obp->cobp", spec_u[1], grad_mix[1], precision=PRECISE
    )
    weight_im = jnp.einsum("cbp,obp->cobp", spec_u[0], grad_mix[1], precision=PRECISE) - jnp.einsum(
        "cbp,obp->cobp", spec_u[1], grad_mix[0], precision=PRECISE
    )
    grad_spectral = jnp.stack([weight_re, weight_im])
    returned = synthesize(grad_spec)
    grad_flat = gradient.reshape(channels, -1)
    back_point = jnp.dot(
        pointwise_weight.astype(jnp.float32), grad_flat, precision=PRECISE
    ).reshape(field.shape)
    grad_field = (back_point + returned).astype(jnp.bfloat16)
    local_weight = jnp.dot(widened.reshape(channels, -1), grad_flat.T, precision=PRECISE)
    local_bias = jnp.sum(grad_flat, axis=1)
    summed_weight, summed_bias = lax.psum((local_weight, local_bias), ("gx", "gy"))
    shrink = cell_count ** (-0.5)
    return (
        activated.astype(jnp.bfloat16),
        grad_field,
        grad_spectral,
        summed_weight * shrink,
        summed_bias * shrink,
    )


LANES = 128
HALF = 64
SLOT = 32
CHUNKS = 4
VMEM_BYTES = 20 * 1024 * 1024


def split_table(table):
    high = table.astype(jnp.bfloat16)
    low = (table - high.astype(np.float64)).astype(jnp.bfloat16)
    return high, low


def frequency_table(kept_modes, length):
    position = np.arange(2 * kept_modes)
    return np.where(position < kept_modes, position, position - 2 * kept_modes + length)


def phase_table(frequencies, places, length):
    product = places[:, None] * frequencies[None, :] % length
    return product.astype(np.float64) * (TWO_PI / length)


def split(values):
    high = values.astype(jnp.bfloat16)
    low = (values - high.astype(jnp.float32)).astype(jnp.bfloat16)
    return high, low


def product(left, right, contract=((1,), (0,)), precision=None):
    return lax.dot_general(
        left, right, (contract, ((), ())), preferred_element_type=jnp.float32, precision=precision
    )


NT = ((1,), (1,))
TN = ((0,), (0,))


def lane_ids(rows):
    return lax.broadcasted_iota(jnp.int32, (rows, LANES), 1)


def roll_lanes(values, shift):
    shift = shift % LANES
    if shift == 0:
        return values
    return pltpu.roll(values, shift, 1)


class Plan:
    def __init__(self, field_shape, weight_shape, size_x, size_y):
        self.channels, self.rows_x, self.rows_y, self.depth = field_shape
        self.size_x, self.size_y = size_x, size_y
        self.blocks_z = weight_shape[3]
        self.pair_rows = weight_shape[4]
        self.full_x = self.rows_x * size_x
        self.full_y = self.rows_y * size_y
        self.width_x, self.width_y = 2 * MX, 2 * MY
        self.cells = self.rows_x * self.rows_y
        self.part_c, self.part_z = 0, 0
        for part_z in range(1, self.blocks_z + 1):
            part_c = size_x // part_z
            if size_x % part_z or self.blocks_z % part_z or self.channels % part_c:
                continue
            self.part_c, self.part_z = part_c, part_z
        self.fits = False
        if self.part_c == 0:
            return
        self.own_c = self.channels // self.part_c
        self.own_z = self.blocks_z // self.part_z
        self.planes = self.own_c * self.own_z
        self.plane_rows = 16
        self.own_kx = self.pair_rows // self.width_y
        self.devices = size_x * size_y
        self.fits = (
            self.cells == LANES
            and self.rows_y == 16
            and self.size_y * 2 == self.rows_x
            and self.depth % LANES == 0
            and self.planes < self.plane_rows
            and self.pair_rows % self.width_y == 0
            and self.pair_rows == 2 * LANES + 32
            and self.width_y <= HALF
            and size_x == 8
            and self.channels % CHUNKS == 0
            and self.channels <= SLOT
            and self.channels < size_x * (LANES // SLOT)
            and self.own_z * 2 * self.part_z * size_y == 2 * MZ
        )

    def z_table(self, scaled):
        kz = np.arange(MZ)
        phases = phase_table(kz, np.arange(self.depth), self.depth)
        both = np.stack([np.cos(phases), -np.sin(phases)])
        if scaled:
            cells = float(self.full_x * self.full_y * self.depth)
            both = both * (np.where(kz == 0, 1.0, 2.0) / cells)
        both = both.reshape(2, self.depth, self.size_y, self.part_z, self.own_z)
        return both.transpose(2, 3, 0, 4, 1).reshape(2 * MZ, self.depth)

    def y_tables(self):
        freq = frequency_table(MY, self.full_y)
        phases = phase_table(freq, np.arange(self.full_y), self.full_y)
        cosine, sine = np.cos(phases), np.sin(phases)
        one = np.zeros((self.size_y, 2, self.rows_y, 2, HALF))
        by_block = (self.size_y, self.rows_y, self.width_y)
        one[:, 0, :, 0, : self.width_y] = cosine.reshape(by_block)
        one[:, 1, :, 0, : self.width_y] = sine.reshape(by_block)
        one[:, 0, :, 1, : self.width_y] = -sine.reshape(by_block)
        one[:, 1, :, 1, : self.width_y] = cosine.reshape(by_block)
        one = one.reshape(LANES, LANES)
        tables = []
        for table in (one, one.T):
            high, low = split_table(table)
            top = np.concatenate([high, low], axis=1)
            bottom = np.concatenate([high, np.zeros_like(low)], axis=1)
            tables.append(np.concatenate([top, bottom], axis=0))
        return tables

    def x_tables(self):
        freq = frequency_table(MX, self.full_x)
        phases = phase_table(freq, np.arange(self.full_x), self.full_x)
        phases = phases.reshape(self.size_x, self.rows_x, self.width_x).transpose(1, 0, 2)
        phases = phases.reshape(self.full_x, self.width_x)
        cosine, sine = np.cos(phases), np.sin(phases)
        forward = np.concatenate([cosine.T, sine.T], axis=0)
        inverse = np.concatenate([cosine, sine], axis=0)
        tables = []
        for table in (forward, inverse):
            high, low = split_table(table)
            tables.append(np.concatenate([high, low, high], axis=1))
        return tables


def call(kernel, out_shape, scratch, *operands, smem=(), hbm=(), hbm_outs=()):
    operands = [
        pltpu.with_memory_space_constraint(operand, pltpu.HBM) if at in hbm else operand
        for at, operand in enumerate(operands)
    ]
    specs = []
    for at in range(len(operands)):
        space = pltpu.SMEM if at in smem else pltpu.HBM if at in hbm else pltpu.VMEM
        specs.append(pl.BlockSpec(memory_space=space))
    single = not isinstance(out_shape, (tuple, list))
    shapes = [out_shape] if single else out_shape
    outs = [
        pl.BlockSpec(memory_space=pltpu.HBM if at in hbm_outs else pltpu.VMEM)
        for at in range(len(shapes))
    ]
    return pl.pallas_call(
        kernel,
        out_shape=out_shape,
        in_specs=specs,
        out_specs=outs[0] if single else outs,
        scratch_shapes=scratch,
        compiler_params=pltpu.CompilerParams(vmem_limit_bytes=VMEM_BYTES),
    )(*operands)


def put_spectrum(plan, out_ref, channel, rows):
    block, inner = divmod(channel, plan.own_c)
    size = plan.own_z
    at = 0
    for place_y in range(plan.size_y):
        for part in range(plan.part_z):
            place_x = block * plan.part_z + part
            for which in range(2):
                out_ref[place_x, place_y, which, inner * size : (inner + 1) * size, :] = rows[
                    at : at + size
                ]
                at += size


def take_spectrum(plan, in_ref, rows_ref, channel):
    block, inner = divmod(channel, plan.own_c)
    size = plan.own_z
    at = 0
    for place_y in range(plan.size_y):
        for part in range(plan.part_z):
            place_x = block * plan.part_z + part
            for which in range(2):
                rows_ref[at : at + size, :] = in_ref[
                    place_x, place_y, which, inner * size : (inner + 1) * size, :
                ]
                at += size
    return rows_ref[...]


def clear_spare(plan, out_ref):
    zeros = jnp.zeros((plan.plane_rows - plan.planes, LANES), jnp.float32)
    for place_x in range(plan.size_x):
        for place_y in range(plan.size_y):
            for which in range(2):
                out_ref[place_x, place_y, which, plan.planes :, :] = zeros


def depth_analysis_kernel(plan, field_ref, table_ref, out_ref, blocks_ref, held_ref, arrived):
    copies = [pltpu.make_async_copy(table_ref, held_ref, arrived.at[2])]
    size = plan.channels // 2
    for part in range(2):
        mine = pl.ds(part * size, size)
        copies.append(
            pltpu.make_async_copy(field_ref.at[mine], blocks_ref.at[mine], arrived.at[part])
        )
    for copy in copies:
        copy.start()
    clear_spare(plan, out_ref)
    copies[0].wait()
    table = held_ref[...]
    for channel in range(plan.channels):
        if channel % size == 0:
            copies[1 + channel // size].wait()
        block = blocks_ref[channel].reshape(plan.cells, plan.depth)
        both = product(table, block, NT)
        put_spectrum(plan, out_ref, channel, both[: 2 * MZ] + both[2 * MZ :])


def swap_blocks(values, block):
    values = list(values)
    lanes = lane_ids(values[0].shape[0])
    step = 1
    while step < len(values):
        low = jnp.bitwise_and(lanes, step * block) == 0
        for at in range(len(values)):
            if at & step:
                continue
            first, second = values[at], values[at + step]
            values[at] = jnp.where(low, first, roll_lanes(second, step * block))
            values[at + step] = jnp.where(low, roll_lanes(first, -step * block), second)
        step *= 2
    return values


def along_y(values, table):
    high, low = split(values)
    both = product(jnp.concatenate([high, low], axis=1), table)
    return both[:, :LANES] + both[:, LANES:]


def plane_analysis_kernel(
    plan, in_ref, extra_ref, y_ref, x_ref, out_ref, rows_ref, modes_ref, rest_ref
):
    pad = plan.plane_rows
    left = [
        in_ref[:, place_y, which].reshape(plan.size_x * pad, LANES)
        for place_y in range(plan.size_y)
        for which in range(2)
    ]
    rows_ref[...] = along_y(
        jnp.concatenate(swap_blocks(left, plan.rows_y), axis=0), y_ref[...]
    )
    right = jnp.concatenate(
        [rows_ref[pl.ds(plane, plan.full_x, stride=pad), :] for plane in range(plan.planes)], axis=1
    )
    high, low = split(right)
    both = product(x_ref[...], jnp.concatenate([high, high, low], axis=0))
    sign = jnp.where(lane_ids(plan.width_x) < HALF, 1.0, -1.0)
    for plane in range(plan.planes):
        mine = slice(plane * LANES, (plane + 1) * LANES)
        turned = roll_lanes(both[plan.width_x :, mine], HALF)
        modes_ref[pl.ds(plane, plan.width_x, stride=pad), :] = (
            both[: plan.width_x, mine] + sign * turned
        )
    modes_ref[pl.ds(plan.planes, plan.width_x, stride=pad), :] = jnp.zeros(
        (plan.width_x, LANES), jnp.float32
    )
    lanes = lane_ids(pad)
    width = plan.width_y
    for place_x in range(plan.size_x):
        for which in range(2):
            tiles = [None, None, None]
            for inner in range(plan.own_kx):
                kx = place_x * plan.own_kx + inner
                first = inner * width
                turned = roll_lanes(modes_ref[kx * pad : (kx + 1) * pad, :], first - which * HALF)
                tile, offset = divmod(first, LANES)
                for at in (tile, tile + 1):
                    begin = first - at * LANES
                    if begin >= LANES or begin + width <= 0:
                        continue
                    if tiles[at] is None:
                        tiles[at] = turned
                    else:
                        tiles[at] = jnp.where(lanes < begin, tiles[at], turned)
            for at in range(2):
                row = at * 2 * pad + which * pad
                out_ref[place_x, row : row + pad, :] = tiles[at]
            rest_ref[which * pad : (which + 1) * pad, :] = tiles[2]
        out_ref[place_x, 4 * pad : 4 * pad + 8, :] = pack_rest(rest_ref)
        out_ref[place_x, plan.planes : plan.planes + 1, :] = extra_ref[place_x : place_x + 1, :]


def pack_rest(rest_ref):
    lanes = lane_ids(8)
    packed = rest_ref[0:8, :]
    for group in range(1, 4):
        turned = roll_lanes(rest_ref[group * 8 : (group + 1) * 8, :], group * 32)
        packed = jnp.where(lanes < group * 32, packed, turned)
    return packed


def unpack_rest(packed, rest_ref):
    for group in range(4):
        rest_ref[group * 8 : (group + 1) * 8, :] = roll_lanes(packed, -group * 32)


def take_modes(plan, in_ref, modes_ref, rest_ref):
    pad, size = plan.plane_rows, plan.own_z
    for place_x in range(plan.size_x):
        block, part = divmod(place_x, plan.part_z)
        unpack_rest(in_ref[place_x, 4 * pad : 4 * pad + 8, :], rest_ref)
        for which in range(2):
            for inner in range(plan.own_c):
                channel = block * plan.own_c + inner
                row = which * pad + inner * size
                kz = slice(part * size, (part + 1) * size)
                for at in range(2):
                    begin = at * 2 * pad + row
                    modes_ref[channel, which, kz, at * LANES : (at + 1) * LANES] = in_ref[
                        place_x, begin : begin + size, :
                    ]
                modes_ref[channel, which, kz, 2 * LANES :] = rest_ref[row : row + size, 0:32]


def put_modes(plan, modes_ref, out_ref, rest_ref):
    pad, size = plan.plane_rows, plan.own_z
    zeros = jnp.zeros((pad - plan.planes, LANES), jnp.float32)
    rest_ref[...] = jnp.zeros((2 * pad, LANES), jnp.float32)
    for place_x in range(plan.size_x):
        block, part = divmod(place_x, plan.part_z)
        for which in range(2):
            for inner in range(plan.own_c):
                channel = block * plan.own_c + inner
                row = which * pad + inner * size
                kz = slice(part * size, (part + 1) * size)
                for at in range(2):
                    begin = at * 2 * pad + row
                    out_ref[place_x, begin : begin + size, :] = modes_ref[
                        channel, which, kz, at * LANES : (at + 1) * LANES
                    ]
                rest_ref[row : row + size, 0:32] = modes_ref[channel, which, kz, 2 * LANES :]
            for at in range(2):
                begin = at * 2 * pad + which * pad + plan.planes
                out_ref[place_x, begin : begin + pad - plan.planes, :] = zeros
        out_ref[place_x, 4 * pad : 4 * pad + 8, :] = pack_rest(rest_ref)


def bring_weights(plan, weight_hbm, weight_ref, arrived, by_input):
    copies = []
    size = plan.channels // CHUNKS
    for chunk in range(CHUNKS):
        mine = pl.ds(chunk * size, size)
        at = (slice(None), mine) if by_input else (slice(None), slice(None), mine)
        copies.append(
            pltpu.make_async_copy(weight_hbm.at[at], weight_ref.at[at], arrived.at[chunk])
        )
    for copy in copies:
        copy.start()
    return copies


def mix_kernel(
    plan, in_ref, weight_hbm, out_ref, spectrum_ref, mixed_ref, rest_ref, weight_ref, arrived
):
    copies = bring_weights(plan, weight_hbm, weight_ref, arrived, False)
    take_modes(plan, in_ref, spectrum_ref, rest_ref)
    shape = (plan.blocks_z, plan.pair_rows)

    def one(out_channel, carry):
        real_part = jnp.zeros(shape, jnp.float32)
        imag_part = jnp.zeros(shape, jnp.float32)
        for channel in range(plan.channels):
            weight_re = weight_ref[0, channel, out_channel].astype(jnp.float32)
            weight_im = weight_ref[1, channel, out_channel].astype(jnp.float32)
            value_re = spectrum_ref[channel, 0]
            value_im = spectrum_ref[channel, 1]
            real_part += weight_re * value_re - weight_im * value_im
            imag_part += weight_re * value_im + weight_im * value_re
        mixed_ref[out_channel, 0] = real_part
        mixed_ref[out_channel, 1] = imag_part
        return carry

    size = plan.channels // CHUNKS
    for chunk, copy in enumerate(copies):
        copy.wait()
        lax.fori_loop(chunk * size, (chunk + 1) * size, one, 0)
    put_modes(plan, mixed_ref, out_ref, rest_ref)


def mix_back_kernel(
    plan,
    in_ref,
    weight_hbm,
    out_ref,
    grad_ref,
    sums_ref,
    mixed_ref,
    rest_ref,
    weight_ref,
    arrived,
):
    copies = bring_weights(plan, weight_hbm, weight_ref, arrived, True)
    spare = jnp.zeros((1, LANES), jnp.float32)
    for place_x in range(plan.size_x):
        spare = spare + in_ref[place_x, plan.planes : plan.planes + 1, :]
    sums_ref[...] = jnp.broadcast_to(spare, (8, LANES))
    take_modes(plan, in_ref, grad_ref, rest_ref)
    shape = (plan.blocks_z, plan.pair_rows)

    def one(channel, carry):
        real_part = jnp.zeros(shape, jnp.float32)
        imag_part = jnp.zeros(shape, jnp.float32)
        for out_channel in range(plan.channels):
            weight_re = weight_ref[0, channel, out_channel].astype(jnp.float32)
            weight_im = weight_ref[1, channel, out_channel].astype(jnp.float32)
            value_re = grad_ref[out_channel, 0]
            value_im = grad_ref[out_channel, 1]
            real_part += weight_re * value_re + weight_im * value_im
            imag_part += weight_re * value_im - weight_im * value_re
        mixed_ref[channel, 0] = real_part
        mixed_ref[channel, 1] = imag_part
        return carry

    size = plan.channels // CHUNKS
    for chunk, copy in enumerate(copies):
        copy.wait()
        lax.fori_loop(chunk * size, (chunk + 1) * size, one, 0)
    put_modes(plan, mixed_ref, out_ref, rest_ref)


def weight_grad_kernel(plan, spectrum_ref, grad_ref, sums_ref, out_ref, passed_ref):
    passed_ref[...] = sums_ref[...]
    value_re = spectrum_ref[0, 0]
    value_im = spectrum_ref[0, 1]
    for out_channel in range(plan.channels):
        grad_re = grad_ref[out_channel, 0]
        grad_im = grad_ref[out_channel, 1]
        out_ref[0, 0, out_channel] = value_re * grad_re + value_im * grad_im
        out_ref[1, 0, out_channel] = value_re * grad_im - value_im * grad_re


def weight_grad(plan, spectrum, grad, sums):
    modes = (plan.blocks_z, plan.pair_rows)
    return pl.pallas_call(
        functools.partial(weight_grad_kernel, plan),
        grid=(plan.channels,),
        out_shape=[
            jax.ShapeDtypeStruct((2, plan.channels, plan.channels) + modes, jnp.float32),
            jax.ShapeDtypeStruct(sums.shape, jnp.float32),
        ],
        in_specs=[
            pl.BlockSpec((1, 2) + modes, lambda channel: (channel, 0, 0, 0)),
            pl.BlockSpec((plan.channels, 2) + modes, lambda channel: (0, 0, 0, 0)),
            pl.BlockSpec(sums.shape, lambda channel: (0, 0)),
        ],
        out_specs=[
            pl.BlockSpec((2, 1, plan.channels) + modes, lambda channel: (0, channel, 0, 0, 0)),
            pl.BlockSpec(sums.shape, lambda channel: (0, 0)),
        ],
        compiler_params=pltpu.CompilerParams(vmem_limit_bytes=VMEM_BYTES),
    )(spectrum, grad, sums)


def plane_synthesis_kernel(
    plan, in_ref, extra_ref, y_ref, x_ref, out_ref, rows_ref, modes_ref, rest_ref
):
    pad, width = plan.plane_rows, plan.width_y
    lanes = lane_ids(pad)
    for place_x in range(plan.size_x):
        unpack_rest(in_ref[place_x, 4 * pad : 4 * pad + 8, :], rest_ref)
        tiles = []
        for which in range(2):
            row = which * pad
            tiles.append(
                [
                    in_ref[place_x, row : row + pad, :],
                    in_ref[place_x, 2 * pad + row : 3 * pad + row, :],
                    rest_ref[row : row + pad, :],
                ]
            )
        for inner in range(plan.own_kx):
            first = inner * width
            tile, offset = divmod(first, LANES)
            pieces = []
            for which in range(2):
                piece = roll_lanes(tiles[which][tile], which * HALF - offset)
                if offset + width > LANES:
                    later = roll_lanes(tiles[which][tile + 1], which * HALF - offset)
                    piece = jnp.where(lanes < which * HALF + LANES - offset, piece, later)
                pieces.append(piece)
            merged = jnp.where(lanes < HALF, pieces[0], pieces[1])
            used = jnp.bitwise_and(lanes, HALF - 1) < width
            at = (place_x * plan.own_kx + inner) * pad
            modes_ref[at : at + pad, :] = jnp.where(used, merged, 0.0)
    right = jnp.concatenate(
        [modes_ref[pl.ds(plane, plan.width_x, stride=pad), :] for plane in range(plan.planes)],
        axis=1,
    )
    high, low = split(right)
    both = product(x_ref[...], jnp.concatenate([high, high, low], axis=0))
    sign = jnp.where(lane_ids(plan.full_x) < HALF, -1.0, 1.0)
    for plane in range(plan.planes):
        mine = slice(plane * LANES, (plane + 1) * LANES)
        turned = roll_lanes(both[plan.full_x :, mine], HALF)
        rows_ref[pl.ds(plane, plan.full_x, stride=pad), :] = (
            both[: plan.full_x, mine] + sign * turned
        )
    rows_ref[pl.ds(plan.planes, plan.full_x, stride=pad), :] = jnp.zeros(
        (plan.full_x, LANES), jnp.float32
    )
    cells = along_y(rows_ref[...], y_ref[...])
    size = plan.size_x * pad
    cells = swap_blocks(
        [cells[row * size : (row + 1) * size] for row in range(plan.rows_x)], plan.rows_y
    )
    for place_y in range(plan.size_y):
        for which in range(2):
            out_ref[:, place_y, which] = cells[place_y * 2 + which].reshape(
                plan.size_x, pad, LANES
            )
    spare = extra_ref[0:1, :]
    for place_x in range(plan.size_x):
        for place_y in range(plan.size_y):
            out_ref[place_x, place_y, 0, plan.planes : plan.planes + 1, :] = spare


def widen_map(plan, small, transposed):
    rows = plan.channels * plan.rows_y
    row_ids = lax.broadcasted_iota(jnp.int32, (rows, plan.channels), 0)
    column_ids = lax.broadcasted_iota(jnp.int32, (rows, plan.channels), 1)
    spread = jnp.where(row_ids // plan.rows_y == column_ids, 1.0, 0.0).astype(jnp.bfloat16)
    wide = product(spread, small, ((1,), (0,)) if transposed else ((1,), (1,)))
    wide = product(wide.astype(jnp.bfloat16), spread, NT)
    return jnp.where(same_cell(plan), wide, 0.0).astype(jnp.bfloat16)


def same_cell(plan):
    rows = plan.channels * plan.rows_y
    row_ids = lax.broadcasted_iota(jnp.int32, (rows, rows), 0)
    column_ids = lax.broadcasted_iota(jnp.int32, (rows, rows), 1)
    return jnp.bitwise_and(row_ids, plan.rows_y - 1) == jnp.bitwise_and(
        column_ids, plan.rows_y - 1
    )


def synthesize_depth(plan, in_ref, rows_ref, table, channel):
    rows = take_spectrum(plan, in_ref, rows_ref, channel)
    high, low = split(rows)
    return product(jnp.concatenate([high, high, low], axis=0), table, TN)


def pointwise_kernel(plan, field_ref, map_ref, bias_ref, weight_ref, out_ref, nothing_ref):
    del weight_ref
    nothing_ref[...] = jnp.zeros((8, LANES), jnp.float32)
    rows, size = plan.channels * plan.rows_y, plan.rows_y
    wide = widen_map(plan, map_ref[...], False)

    def one(row, carry):
        here = pl.ds(row, 1)
        mapped = product(wide, field_ref[:, here].reshape(rows, plan.depth))
        for channel in range(plan.channels):
            part = mapped[channel * size : (channel + 1) * size] + bias_ref[channel]
            out_ref[channel, here] = part.reshape(1, size, plan.depth)
        return carry

    lax.fori_loop(0, plan.rows_x, one, 0)


def activation_kernel(
    plan,
    in_ref,
    pointwise_ref,
    cotangent_ref,
    inverse_ref,
    forward_ref,
    output_hbm,
    spectrum_ref,
    high_hbm,
    low_hbm,
    rows_ref,
    output_ref,
    high_ref,
    low_ref,
    sent,
):
    pairs = ((output_ref, output_hbm), (high_ref, high_hbm), (low_ref, low_hbm))
    copies = []
    clear_spare(plan, spectrum_ref)
    flat = (plan.cells, plan.depth)
    block = (plan.rows_x, plan.rows_y, plan.depth)
    inverse = inverse_ref[...]
    forward = forward_ref[...]
    scale = math.sqrt(2.0 / math.pi)
    for channel in range(plan.channels):
        preact = synthesize_depth(plan, in_ref, rows_ref, inverse, channel)
        preact = preact + pointwise_ref[channel].reshape(flat)
        square = preact * preact
        bend = jnp.tanh(scale * preact * (1.0 + 0.044715 * square))
        half = 0.5 * (1.0 + bend)
        output_ref[channel] = (preact * half).astype(jnp.bfloat16).reshape(block)
        slope = half + (0.5 * scale) * preact * (1.0 - bend * bend) * (
            1.0 + (3.0 * 0.044715) * square
        )
        grad = cotangent_ref[channel].reshape(flat).astype(jnp.float32) * slope
        high, low = split(grad)
        high_ref[channel] = high.reshape(block)
        low_ref[channel] = low.reshape(block)
        both = product(forward, high, NT)
        more = product(forward[: 2 * MZ], low, NT)
        put_spectrum(plan, spectrum_ref, channel, both[: 2 * MZ] + both[2 * MZ :] + more)
        copies += send_block(plan, channel, pairs, sent)
    for copy in copies:
        copy.wait()


def send_block(plan, channel, pairs, sent):
    block, inner = divmod(channel, plan.own_c)
    if inner < plan.own_c - 1:
        return []
    mine = pl.ds(block * plan.own_c, plan.own_c)
    copies = [
        pltpu.make_async_copy(held.at[mine], target.at[mine], sent.at[at, block])
        for at, (held, target) in enumerate(pairs)
    ]
    for copy in copies:
        copy.start()
    return copies


def pointwise_grad_kernel(
    plan, field_ref, high_ref, low_ref, map_ref, back_ref, sums_ref, cross_ref
):
    rows = plan.channels * plan.rows_y
    wide = widen_map(plan, map_ref[...], True)
    cross_ref[...] = jnp.zeros((rows + 16, rows), jnp.float32)
    ones = jnp.ones((16, plan.depth), jnp.bfloat16)
    slab = (plan.channels, 1, plan.rows_y, plan.depth)

    def one(row, carry):
        here = pl.ds(row, 1)
        values = field_ref[:, here].reshape(rows, plan.depth)
        values = jnp.concatenate([values, ones], axis=0)
        high = high_ref[:, here].reshape(rows, plan.depth)
        low = low_ref[:, here].reshape(rows, plan.depth)
        back_ref[:, here] = (product(wide, high) + product(wide, low)).reshape(slab)
        cross_ref[...] += product(values, high, NT) + product(values, low, NT)
        return carry

    lax.fori_loop(0, plan.rows_x, one, 0)
    row_ids = lax.broadcasted_iota(jnp.int32, (rows, LANES), 0)
    gather = jnp.where(row_ids // plan.rows_y == lane_ids(rows), 1.0, 0.0)
    exact = lax.Precision.HIGHEST
    cross = jnp.where(same_cell(plan), cross_ref[:rows], 0.0)
    by_out = product(cross, gather, precision=exact)
    sums = product(gather, by_out, TN, precision=exact)
    bias_sums = product(cross_ref[rows : rows + 8], gather, precision=exact)
    lanes = lane_ids(1)
    per_row = LANES // SLOT
    for at in range(8):
        packed = jnp.zeros((1, LANES), jnp.float32)
        for slot in range(per_row):
            row = at * per_row + slot
            if row > plan.channels:
                continue
            line = sums[row : row + 1] if row < plan.channels else bias_sums[0:1]
            packed = jnp.where(lanes // SLOT == slot, roll_lanes(line, slot * SLOT), packed)
        sums_ref[at : at + 1, :] = packed


def last_kernel(
    plan,
    in_ref,
    back_ref,
    inverse_ref,
    grad_ref,
    map_grad_ref,
    bias_grad_ref,
    rows_ref,
):
    block = (plan.rows_x, plan.rows_y, plan.depth)
    flat = (plan.cells, plan.depth)
    inverse = inverse_ref[...]
    for channel in range(plan.channels):
        total = synthesize_depth(plan, in_ref, rows_ref, inverse, channel)
        total = total + back_ref[channel].reshape(flat)
        grad_ref[channel] = total.astype(jnp.bfloat16).reshape(block)
    shrink = float(plan.full_x * plan.full_y * plan.depth) ** (-0.5)
    per_row = LANES // SLOT
    for at in range(plan.size_x):
        line = jnp.zeros((1, LANES), jnp.float32)
        for place_y in range(plan.size_y):
            line = line + in_ref[at, place_y, 0, plan.planes : plan.planes + 1, :]
        for slot in range(per_row):
            row = at * per_row + slot
            mine = shrink * roll_lanes(line, -slot * SLOT)[:, : plan.channels]
            if row < plan.channels:
                map_grad_ref[row : row + 1, :] = mine
            elif row == plan.channels:
                bias_grad_ref[...] = mine


def by_planes(plan, field, cotangent, spectral_weight, pointwise_weight, bias):
    pad = plan.plane_rows
    f32 = jnp.float32
    cell_shape = (plan.size_x, plan.size_y, 2, pad, LANES)
    mode_shape = (plan.size_x, 4 * pad + 8, LANES)
    own_shape = (plan.channels, 2, plan.blocks_z, plan.pair_rows)
    grid_shape = field.shape

    def shape(dims, kind=f32):
        return jax.ShapeDtypeStruct(dims, kind)

    def cell_exchange(values):
        flat = values.reshape(plan.devices, 2 * pad, LANES)
        return lax.all_to_all(flat, ("gx", "gy"), 0, 0, tiled=True).reshape(cell_shape)

    def mode_exchange(values):
        return lax.all_to_all(values, "gx", 0, 0, tiled=True)

    z_high, z_low = split_table(plan.z_table(False))
    scaled_high, scaled_low = split_table(plan.z_table(True))
    z_forward = jnp.asarray(np.concatenate([z_high, z_low]))
    z_inverse = jnp.asarray(np.concatenate([z_high, z_low, z_high]))
    scaled_forward = jnp.asarray(np.concatenate([scaled_high, scaled_low]))
    scaled_inverse = jnp.asarray(np.concatenate([scaled_high, scaled_low, scaled_high]))
    y_forward, y_inverse = (jnp.asarray(table) for table in plan.y_tables())
    x_forward, x_inverse = (jnp.asarray(table) for table in plan.x_tables())

    lane_rows = pltpu.VMEM((plan.full_x * pad, LANES), f32)
    lane_modes = pltpu.VMEM((plan.width_x * pad, LANES), f32)
    rest = pltpu.VMEM((2 * pad, LANES), f32)
    own = pltpu.VMEM(own_shape, f32)
    lines = pltpu.VMEM((2 * MZ, LANES), f32)
    wide = plan.channels * plan.rows_y
    row_shape = shape((8, LANES))

    blocks_sent = pltpu.SemaphoreType.DMA((3, plan.part_c))

    held_weights = [
        pltpu.VMEM(spectral_weight.shape, spectral_weight.dtype),
        pltpu.SemaphoreType.DMA((CHUNKS,)),
    ]

    def in_hbm(struct):
        return pltpu.HBM(struct.shape, struct.dtype)

    def with_plan(kernel):
        return functools.partial(kernel, plan)

    def plane_analysis(cells, extra):
        return call(
            with_plan(plane_analysis_kernel),
            shape(mode_shape),
            [lane_rows, lane_modes, rest],
            cells,
            extra,
            y_forward,
            x_forward,
        )

    def plane_synthesis(modes, extra):
        return call(
            with_plan(plane_synthesis_kernel),
            shape(cell_shape),
            [lane_rows, lane_modes, rest],
            modes,
            extra,
            y_inverse,
            x_inverse,
        )

    with jax.named_scope("depth_analysis"):
        cells = call(
            with_plan(depth_analysis_kernel),
            in_hbm(shape(cell_shape)),
            [
                pltpu.VMEM(grid_shape, jnp.bfloat16),
                pltpu.VMEM(z_forward.shape, jnp.bfloat16),
                pltpu.SemaphoreType.DMA((3,)),
            ],
            field,
            z_forward,
            hbm=(0, 1),
        )
    with jax.named_scope("cells_to_planes"):
        cells = cell_exchange(cells)
    with jax.named_scope("pointwise"):
        weights = with_layout_constraint(spectral_weight, Layout((0, 1, 2, 3, 4)))
        pointwise, nothing = call(
            with_plan(pointwise_kernel),
            [in_hbm(shape(grid_shape)), row_shape],
            [],
            field,
            pointwise_weight,
            bias,
            weights,
            smem=(2,),
            hbm=(3,),
        )
    with jax.named_scope("plane_analysis"):
        modes = plane_analysis(cells, nothing)
    with jax.named_scope("planes_to_modes"):
        modes = mode_exchange(modes)
    with jax.named_scope("mix"):
        modes, spectrum = call(
            with_plan(mix_kernel),
            [shape(mode_shape), shape(own_shape)],
            [own, rest] + held_weights,
            modes,
            weights,
            hbm=(1,),
        )
    with jax.named_scope("modes_to_planes"):
        modes = mode_exchange(modes)
    with jax.named_scope("plane_synthesis"):
        cells = plane_synthesis(modes, nothing)
    with jax.named_scope("planes_to_cells"):
        cells = cell_exchange(cells)
    with jax.named_scope("activation"):
        half_grid = shape(grid_shape, jnp.bfloat16)
        output, cells, grad_high, grad_low = call(
            with_plan(activation_kernel),
            [in_hbm(half_grid), in_hbm(shape(cell_shape)), in_hbm(half_grid), in_hbm(half_grid)],
            [lines] + [pltpu.VMEM(grid_shape, jnp.bfloat16)] * 3 + [blocks_sent],
            cells,
            pointwise,
            cotangent,
            scaled_inverse,
            scaled_forward,
            hbm_outs=(0, 2, 3),
        )
    with jax.named_scope("grad_cells_to_planes"):
        cells = cell_exchange(cells)
    with jax.named_scope("pointwise_grad"):
        back, sums = call(
            with_plan(pointwise_grad_kernel),
            [in_hbm(shape(grid_shape)), row_shape],
            [pltpu.VMEM((wide + 16, wide), f32)],
            field,
            grad_high,
            grad_low,
            pointwise_weight,
        )
    with jax.named_scope("grad_plane_analysis"):
        modes = plane_analysis(cells, sums)
    with jax.named_scope("grad_planes_to_modes"):
        modes = mode_exchange(modes)
    with jax.named_scope("grad_mix"):
        modes, grad_mix, sums = call(
            with_plan(mix_back_kernel),
            [shape(mode_shape), shape(own_shape), row_shape],
            [own, rest] + held_weights,
            modes,
            weights,
            hbm=(1,),
        )
    with jax.named_scope("grad_modes_to_planes"):
        modes = mode_exchange(modes)
    with jax.named_scope("grad_spectral"):
        grad_spectral, sums = weight_grad(plan, spectrum, grad_mix, sums)
    with jax.named_scope("grad_plane_synthesis"):
        cells = plane_synthesis(modes, sums)
    with jax.named_scope("grad_planes_to_cells"):
        cells = cell_exchange(cells)
    with jax.named_scope("grad_field"):
        channels = plan.channels
        grad_field, map_grad, bias_grad = call(
            with_plan(last_kernel),
            [half_grid, shape((channels, channels)), shape((1, channels))],
            [lines],
            cells,
            back,
            z_inverse,
        )
    return output, grad_field, grad_spectral, map_grad, bias_grad.reshape(channels)


def layer(field, cotangent, spectral_weight, pointwise_weight, bias):
    plan = Plan(
        field.shape, spectral_weight.shape, lax.axis_size("gx"), lax.axis_size("gy")
    )
    if plan.fits:
        return by_planes(plan, field, cotangent, spectral_weight, pointwise_weight, bias)
    return local(field, cotangent, spectral_weight, pointwise_weight, bias)


def solution(mesh):
    placed = (
        P(None, "gx", "gy", None),
        P(None, "gx", "gy", None),
        P(None, None, None, "gy", "gx"),
        P(),
        P(),
    )
    return jax.shard_map(
        layer,
        mesh=mesh,
        in_specs=placed,
        out_specs=(
            P(None, "gx", "gy", None),
            P(None, "gx", "gy", None),
            P(None, None, None, "gy", "gx"),
            P(),
            P(),
        ),
        check_vma=False,
    )
```

```python
import functools
import math

import jax
import jax.numpy as jnp
from jax import lax
import numpy as np
from jax.experimental import pallas as pl
from jax.experimental.layout import Layout, with_layout_constraint
from jax.experimental.pallas import tpu as pltpu
from jax.sharding import PartitionSpec as P

MX = 24
MY = 24
MZ = 24


PRECISE = lax.Precision.HIGHEST
TWO_PI = 2.0 * math.pi


def angles(frequencies, places, length):
    product = places[:, None] * frequencies[None, :] % length
    return product.astype(jnp.float32) * (TWO_PI / length)


def frequency(position, kept_modes, length):
    return jnp.where(position < kept_modes, position, position - 2 * kept_modes + length)


def forward_y(values, phases):
    cosine_table = jnp.cos(phases)
    sine_table = jnp.sin(phases)
    with_cos = jnp.einsum("brcxy,yj->brcxj", values, cosine_table, precision=PRECISE)
    with_sin = jnp.einsum("brcxy,yj->brcxj", values, sine_table, precision=PRECISE)
    real_part = with_cos[:, 0] + with_sin[:, 1]
    imag_part = with_cos[:, 1] - with_sin[:, 0]
    return jnp.stack([real_part, imag_part], axis=1)


def inverse_y(values, phases):
    cosine_table = jnp.cos(phases)
    sine_table = jnp.sin(phases)
    with_cos = jnp.einsum("brcxj,yj->brcxy", values, cosine_table, precision=PRECISE)
    with_sin = jnp.einsum("brcxj,yj->brcxy", values, sine_table, precision=PRECISE)
    real_part = with_cos[:, 0] - with_sin[:, 1]
    imag_part = with_sin[:, 0] + with_cos[:, 1]
    return jnp.stack([real_part, imag_part], axis=1)


def local(field, cotangent, spectral_weight, pointwise_weight, bias):
    channels, rows_x, rows_y, depth_cells = field.shape
    blocks_z = spectral_weight.shape[3]
    pair_rows = spectral_weight.shape[4]
    width_x = 2 * MX
    width_y = 2 * MY
    full_x = rows_x * lax.axis_size("gx")
    full_y = rows_y * lax.axis_size("gy")
    cell_count = float(full_x * full_y * depth_cells)
    place_x = lax.axis_index("gx")
    place_y = lax.axis_index("gy")
    own_x = place_x * rows_x + jnp.arange(rows_x, dtype=jnp.int32)
    freq_x = frequency(jnp.arange(width_x, dtype=jnp.int32), MX, full_x)
    freq_y = frequency(jnp.arange(width_y, dtype=jnp.int32), MY, full_y)
    phases_full_y = angles(freq_y, jnp.arange(full_y, dtype=jnp.int32), full_y)
    z_phases = angles(
        jnp.arange(MZ, dtype=jnp.int32), jnp.arange(depth_cells, dtype=jnp.int32), depth_cells
    )
    table_z = jnp.stack([jnp.cos(z_phases), -jnp.sin(z_phases)], axis=2).reshape(
        depth_cells, 2 * MZ
    )
    kz_own = place_y * blocks_z + jnp.arange(blocks_z, dtype=jnp.int32)
    weight_z = (jnp.where(kz_own == 0, 1.0, 2.0).astype(jnp.float32) / cell_count)[None, :, None]
    own_first = place_x * pair_rows
    flat_width = blocks_z * 2 * channels

    def kx_terms(values, places, first_pair, count):
        kx_count = min(count // width_y + 2, width_x)
        kx_first = jnp.minimum(first_pair // width_y, width_x - kx_count)
        kx_ids = kx_first + jnp.arange(kx_count, dtype=jnp.int32)
        phases = angles(frequency(kx_ids, MX, full_x), places, full_x)
        cosine_table = jnp.cos(phases)
        sine_table = jnp.sin(phases)
        real_part = jnp.einsum(
            "bcxj,xi->ijbc", values[:, 0], cosine_table, precision=PRECISE
        ) + jnp.einsum("bcxj,xi->ijbc", values[:, 1], sine_table, precision=PRECISE)
        imag_part = jnp.einsum(
            "bcxj,xi->ijbc", values[:, 1], cosine_table, precision=PRECISE
        ) - jnp.einsum("bcxj,xi->ijbc", values[:, 0], sine_table, precision=PRECISE)
        terms = jnp.stack([real_part, imag_part], axis=3).reshape(kx_count * width_y, flat_width)
        offset = first_pair - kx_first * width_y
        return lax.dynamic_slice_in_dim(terms, offset, count, 0)

    def analyze(values):
        flat = values.reshape(-1, depth_cells)
        spectra = jnp.einsum("zk,mz->km", table_z, flat, precision=PRECISE).reshape(
            2 * MZ, channels, rows_x, rows_y
        )
        columns = lax.all_to_all(spectra, "gy", split_axis=0, concat_axis=3, tiled=True)
        mode_data = forward_y(columns.reshape(blocks_z, 2, channels, rows_x, full_y), phases_full_y)
        portion = lax.all_gather(mode_data, "gx", axis=3, tiled=True)
        places = jnp.arange(portion.shape[3], dtype=jnp.int32)
        owned = kx_terms(portion, places, own_first, pair_rows)
        return jnp.transpose(owned.reshape(pair_rows, blocks_z, 2, channels), (2, 3, 1, 0))

    def synthesize(spectrum):
        portion = lax.all_gather(spectrum, "gx", axis=3, tiled=True)
        blocks = portion.reshape(2, channels, blocks_z, width_x, width_y)
        phases = angles(freq_x, own_x, full_x)
        cosine_table = jnp.cos(phases)
        sine_table = jnp.sin(phases)
        real_part = jnp.einsum(
            "cbij,xi->bcxj", blocks[0], cosine_table, precision=PRECISE
        ) - jnp.einsum("cbij,xi->bcxj", blocks[1], sine_table, precision=PRECISE)
        imag_part = jnp.einsum(
            "cbij,xi->bcxj", blocks[0], sine_table, precision=PRECISE
        ) + jnp.einsum("cbij,xi->bcxj", blocks[1], cosine_table, precision=PRECISE)
        mode_data = jnp.stack([real_part, imag_part], axis=1)
        fields = inverse_y(mode_data, phases_full_y)
        columns = lax.all_to_all(fields, "gy", split_axis=4, concat_axis=0, tiled=True)
        flat = columns.reshape(2 * MZ, -1)
        return jnp.einsum("km,zk->mz", flat, table_z, precision=PRECISE).reshape(
            channels, rows_x, rows_y, depth_cells
        )

    weights = spectral_weight.astype(jnp.float32)
    widened = field.astype(jnp.float32)
    spec_u = analyze(widened)
    mixed_re = jnp.einsum("cobp,cbp->obp", weights[0], spec_u[0], precision=PRECISE) - jnp.einsum(
        "cobp,cbp->obp", weights[1], spec_u[1], precision=PRECISE
    )
    mixed_im = jnp.einsum("cobp,cbp->obp", weights[0], spec_u[1], precision=PRECISE) + jnp.einsum(
        "cobp,cbp->obp", weights[1], spec_u[0], precision=PRECISE
    )
    mixed_modes = jnp.stack([mixed_re, mixed_im]) * weight_z
    conv = synthesize(mixed_modes)
    pointwise = jnp.dot(
        pointwise_weight.T, field.reshape(channels, -1), preferred_element_type=jnp.float32
    ).reshape(field.shape)
    preact = pointwise + bias[:, None, None, None] + conv
    activated, pullback = jax.vjp(jax.nn.gelu, preact)
    gradient = pullback(cotangent.astype(jnp.float32))[0]
    grad_mix = analyze(gradient) * weight_z
    spec_re = jnp.einsum("cobp,obp->cbp", weights[0], grad_mix[0], precision=PRECISE) + jnp.einsum(
        "cobp,obp->cbp", weights[1], grad_mix[1], precision=PRECISE
    )
    spec_im = jnp.einsum("cobp,obp->cbp", weights[0], grad_mix[1], precision=PRECISE) - jnp.einsum(
        "cobp,obp->cbp", weights[1], grad_mix[0], precision=PRECISE
    )
    grad_spec = jnp.stack([spec_re, spec_im])
    weight_re = jnp.einsum("cbp,obp->cobp", spec_u[0], grad_mix[0], precision=PRECISE) + jnp.einsum(
        "cbp,obp->cobp", spec_u[1], grad_mix[1], precision=PRECISE
    )
    weight_im = jnp.einsum("cbp,obp->cobp", spec_u[0], grad_mix[1], precision=PRECISE) - jnp.einsum(
        "cbp,obp->cobp", spec_u[1], grad_mix[0], precision=PRECISE
    )
    grad_spectral = jnp.stack([weight_re, weight_im])
    returned = synthesize(grad_spec)
    grad_flat = gradient.reshape(channels, -1)
    back_point = jnp.dot(
        pointwise_weight.astype(jnp.float32), grad_flat, precision=PRECISE
    ).reshape(field.shape)
    grad_field = (back_point + returned).astype(jnp.bfloat16)
    local_weight = jnp.dot(widened.reshape(channels, -1), grad_flat.T, precision=PRECISE)
    local_bias = jnp.sum(grad_flat, axis=1)
    summed_weight, summed_bias = lax.psum((local_weight, local_bias), ("gx", "gy"))
    shrink = cell_count ** (-0.5)
    return (
        activated.astype(jnp.bfloat16),
        grad_field,
        grad_spectral,
        summed_weight * shrink,
        summed_bias * shrink,
    )


LANES = 128
HALF = 64
SLOT = 32
CHUNKS = 5
VMEM_BYTES = 20 * 1024 * 1024


def split_table(table):
    high = table.astype(jnp.bfloat16)
    low = (table - high.astype(np.float64)).astype(jnp.bfloat16)
    return high, low


def frequency_table(kept_modes, length):
    position = np.arange(2 * kept_modes)
    return np.where(position < kept_modes, position, position - 2 * kept_modes + length)


def phase_table(frequencies, places, length):
    product = places[:, None] * frequencies[None, :] % length
    return product.astype(np.float64) * (TWO_PI / length)


def split(values):
    high = values.astype(jnp.bfloat16)
    low = (values - high.astype(jnp.float32)).astype(jnp.bfloat16)
    return high, low


def product(left, right, contract=((1,), (0,)), precision=None):
    return lax.dot_general(
        left, right, (contract, ((), ())), preferred_element_type=jnp.float32, precision=precision
    )


NT = ((1,), (1,))
TN = ((0,), (0,))


def lane_ids(rows):
    return lax.broadcasted_iota(jnp.int32, (rows, LANES), 1)


def roll_lanes(values, shift):
    shift = shift % LANES
    if shift == 0:
        return values
    return pltpu.roll(values, shift, 1)


class Plan:
    def __init__(self, field_shape, weight_shape, size_x, size_y):
        self.channels, self.rows_x, self.rows_y, self.depth = field_shape
        self.size_x, self.size_y = size_x, size_y
        self.blocks_z = weight_shape[3]
        self.pair_rows = weight_shape[4]
        self.full_x = self.rows_x * size_x
        self.full_y = self.rows_y * size_y
        self.width_x, self.width_y = 2 * MX, 2 * MY
        self.cells = self.rows_x * self.rows_y
        self.part_c, self.part_z = 0, 0
        for part_z in range(1, self.blocks_z + 1):
            part_c = size_x // part_z
            if size_x % part_z or self.blocks_z % part_z or self.channels % part_c:
                continue
            self.part_c, self.part_z = part_c, part_z
        self.fits = False
        if self.part_c == 0:
            return
        self.own_c = self.channels // self.part_c
        self.own_z = self.blocks_z // self.part_z
        self.planes = self.own_c * self.own_z
        self.plane_rows = 16
        self.own_kx = self.pair_rows // self.width_y
        self.devices = size_x * size_y
        self.fits = (
            self.cells == LANES
            and self.rows_y == 16
            and self.size_y * 2 == self.rows_x
            and self.depth % LANES == 0
            and self.planes < self.plane_rows
            and self.pair_rows % self.width_y == 0
            and self.pair_rows == 2 * LANES + 32
            and self.width_y <= HALF
            and size_x == 8
            and self.channels % CHUNKS == 0
            and self.channels % 4 == 0
            and self.channels <= SLOT
            and self.channels < size_x * (LANES // SLOT)
            and self.own_z * 2 * self.part_z * size_y == 2 * MZ
        )

    def z_table(self, scaled):
        kz = np.arange(MZ)
        phases = phase_table(kz, np.arange(self.depth), self.depth)
        both = np.stack([np.cos(phases), -np.sin(phases)])
        if scaled:
            cells = float(self.full_x * self.full_y * self.depth)
            both = both * (np.where(kz == 0, 1.0, 2.0) / cells)
        both = both.reshape(2, self.depth, self.size_y, self.part_z, self.own_z)
        return both.transpose(2, 3, 0, 4, 1).reshape(2 * MZ, self.depth)

    def y_tables(self):
        freq = frequency_table(MY, self.full_y)
        phases = phase_table(freq, np.arange(self.full_y), self.full_y)
        cosine, sine = np.cos(phases), np.sin(phases)
        one = np.zeros((self.size_y, 2, self.rows_y, 2, HALF))
        by_block = (self.size_y, self.rows_y, self.width_y)
        one[:, 0, :, 0, : self.width_y] = cosine.reshape(by_block)
        one[:, 1, :, 0, : self.width_y] = sine.reshape(by_block)
        one[:, 0, :, 1, : self.width_y] = -sine.reshape(by_block)
        one[:, 1, :, 1, : self.width_y] = cosine.reshape(by_block)
        one = one.reshape(LANES, LANES)
        tables = []
        for table in (one, one.T):
            high, low = split_table(table)
            top = np.concatenate([high, low], axis=1)
            bottom = np.concatenate([high, np.zeros_like(low)], axis=1)
            tables.append(np.concatenate([top, bottom], axis=0))
        return tables

    def x_tables(self):
        freq = frequency_table(MX, self.full_x)
        phases = phase_table(freq, np.arange(self.full_x), self.full_x)
        phases = phases.reshape(self.size_x, self.rows_x, self.width_x).transpose(1, 0, 2)
        phases = phases.reshape(self.full_x, self.width_x)
        cosine, sine = np.cos(phases), np.sin(phases)
        forward = np.concatenate([cosine.T, sine.T], axis=0)
        inverse = np.concatenate([cosine, sine], axis=0)
        tables = []
        for table in (forward, inverse):
            high, low = split_table(table)
            tables.append(np.concatenate([high, low, high], axis=1))
        return tables


def call(kernel, out_shape, scratch, *operands, smem=(), hbm=(), hbm_outs=()):
    operands = [
        pltpu.with_memory_space_constraint(operand, pltpu.HBM) if at in hbm else operand
        for at, operand in enumerate(operands)
    ]
    specs = []
    for at in range(len(operands)):
        space = pltpu.SMEM if at in smem else pltpu.HBM if at in hbm else pltpu.VMEM
        specs.append(pl.BlockSpec(memory_space=space))
    single = not isinstance(out_shape, (tuple, list))
    shapes = [out_shape] if single else out_shape
    outs = [
        pl.BlockSpec(memory_space=pltpu.HBM if at in hbm_outs else pltpu.VMEM)
        for at in range(len(shapes))
    ]
    return pl.pallas_call(
        kernel,
        out_shape=out_shape,
        in_specs=specs,
        out_specs=outs[0] if single else outs,
        scratch_shapes=scratch,
        compiler_params=pltpu.CompilerParams(vmem_limit_bytes=VMEM_BYTES),
    )(*operands)


def put_spectrum(plan, out_ref, channel, rows):
    block, inner = divmod(channel, plan.own_c)
    size = plan.own_z
    at = 0
    for place_y in range(plan.size_y):
        for part in range(plan.part_z):
            place_x = block * plan.part_z + part
            for which in range(2):
                out_ref[place_x, place_y, which, inner * size : (inner + 1) * size, :] = rows[
                    at : at + size
                ]
                at += size


def take_spectrum(plan, in_ref, rows_ref, channel):
    block, inner = divmod(channel, plan.own_c)
    size = plan.own_z
    at = 0
    for place_y in range(plan.size_y):
        for part in range(plan.part_z):
            place_x = block * plan.part_z + part
            for which in range(2):
                rows_ref[at : at + size, :] = in_ref[
                    place_x, place_y, which, inner * size : (inner + 1) * size, :
                ]
                at += size
    return rows_ref[...]


def clear_spare(plan, out_ref):
    zeros = jnp.zeros((plan.plane_rows - plan.planes, LANES), jnp.float32)
    for place_x in range(plan.size_x):
        for place_y in range(plan.size_y):
            for which in range(2):
                out_ref[place_x, place_y, which, plan.planes :, :] = zeros


def depth_analysis_kernel(
    plan, field_ref, table_ref, out_hbm, blocks_ref, held_ref, out_ref, arrived, sent
):
    copies = [pltpu.make_async_copy(table_ref, held_ref, arrived.at[2])]
    size = plan.channels // 2
    for part in range(2):
        mine = pl.ds(part * size, size)
        copies.append(
            pltpu.make_async_copy(field_ref.at[mine], blocks_ref.at[mine], arrived.at[part])
        )
    for copy in copies:
        copy.start()
    clear_spare(plan, out_ref)
    leaving = []
    copies[0].wait()
    table = held_ref[...]
    for channel in range(plan.channels):
        if channel % size == 0:
            copies[1 + channel // size].wait()
        block = blocks_ref[channel].reshape(plan.cells, plan.depth)
        both = product(table, block, NT)
        put_spectrum(plan, out_ref, channel, both[: 2 * MZ] + both[2 * MZ :])
        leaving += send_block(plan, channel, ((out_ref, out_hbm, plan.part_z),), sent)
    for copy in leaving:
        copy.wait()


def swap_blocks(values, block):
    values = list(values)
    lanes = lane_ids(values[0].shape[0])
    step = 1
    while step < len(values):
        low = jnp.bitwise_and(lanes, step * block) == 0
        for at in range(len(values)):
            if at & step:
                continue
            first, second = values[at], values[at + step]
            values[at] = jnp.where(low, first, roll_lanes(second, step * block))
            values[at + step] = jnp.where(low, roll_lanes(first, -step * block), second)
        step *= 2
    return values


def along_y(values, table):
    high, low = split(values)
    both = product(jnp.concatenate([high, low], axis=1), table)
    return both[:, :LANES] + both[:, LANES:]


def plane_analysis_kernel(
    plan, in_ref, extra_ref, y_ref, x_ref, out_ref, rows_ref, modes_ref, rest_ref
):
    pad = plan.plane_rows
    left = [
        in_ref[:, place_y, which].reshape(plan.size_x * pad, LANES)
        for place_y in range(plan.size_y)
        for which in range(2)
    ]
    rows_ref[...] = along_y(
        jnp.concatenate(swap_blocks(left, plan.rows_y), axis=0), y_ref[...]
    )
    right = jnp.concatenate(
        [rows_ref[pl.ds(plane, plan.full_x, stride=pad), :] for plane in range(plan.planes)], axis=1
    )
    high, low = split(right)
    both = product(x_ref[...], jnp.concatenate([high, high, low], axis=0))
    sign = jnp.where(lane_ids(plan.width_x) < HALF, 1.0, -1.0)
    for plane in range(plan.planes):
        mine = slice(plane * LANES, (plane + 1) * LANES)
        turned = roll_lanes(both[plan.width_x :, mine], HALF)
        modes_ref[pl.ds(plane, plan.width_x, stride=pad), :] = (
            both[: plan.width_x, mine] + sign * turned
        )
    modes_ref[pl.ds(plan.planes, plan.width_x, stride=pad), :] = jnp.zeros(
        (plan.width_x, LANES), jnp.float32
    )
    lanes = lane_ids(pad)
    width = plan.width_y
    for place_x in range(plan.size_x):
        for which in range(2):
            tiles = [None, None, None]
            for inner in range(plan.own_kx):
                kx = place_x * plan.own_kx + inner
                first = inner * width
                turned = roll_lanes(modes_ref[kx * pad : (kx + 1) * pad, :], first - which * HALF)
                tile, offset = divmod(first, LANES)
                for at in (tile, tile + 1):
                    begin = first - at * LANES
                    if begin >= LANES or begin + width <= 0:
                        continue
                    if tiles[at] is None:
                        tiles[at] = turned
                    else:
                        tiles[at] = jnp.where(lanes < begin, tiles[at], turned)
            for at in range(2):
                row = at * 2 * pad + which * pad
                out_ref[place_x, row : row + pad, :] = tiles[at]
            rest_ref[which * pad : (which + 1) * pad, :] = tiles[2]
        out_ref[place_x, 4 * pad : 4 * pad + 8, :] = pack_rest(rest_ref)
        out_ref[place_x, plan.planes : plan.planes + 1, :] = extra_ref[place_x : place_x + 1, :]


def pack_rest(rest_ref):
    lanes = lane_ids(8)
    packed = rest_ref[0:8, :]
    for group in range(1, 4):
        turned = roll_lanes(rest_ref[group * 8 : (group + 1) * 8, :], group * 32)
        packed = jnp.where(lanes < group * 32, packed, turned)
    return packed


def unpack_rest(packed, rest_ref, repeated=False):
    lanes = lane_ids(8)
    for group in range(4):
        turned = roll_lanes(packed, -group * 32)
        if repeated:
            turned = jnp.where(lanes < 32, turned, roll_lanes(turned, 32))
            turned = jnp.where(lanes < 64, turned, roll_lanes(turned, 64))
        rest_ref[group * 8 : (group + 1) * 8, :] = turned


def take_modes(plan, in_ref, modes_ref, rest_ref, beside_ref=None):
    pad, size = plan.plane_rows, plan.own_z
    for place_x in range(plan.size_x):
        block, part = divmod(place_x, plan.part_z)
        unpack_rest(in_ref[place_x, 4 * pad : 4 * pad + 8, :], rest_ref, True)
        for which in range(2):
            for inner in range(plan.own_c):
                channel = block * plan.own_c + inner
                row = which * pad + inner * size
                kz = slice(part * size, (part + 1) * size)
                for at in range(2):
                    begin = at * 2 * pad + row
                    modes_ref[channel, which, kz, at * LANES : (at + 1) * LANES] = in_ref[
                        place_x, begin : begin + size, :
                    ]
                modes_ref[channel, which, kz, 2 * LANES :] = rest_ref[row : row + size, :]
                if beside_ref is not None:
                    group, slot = divmod(channel, 4)
                    mine = slice(slot * 32, (slot + 1) * 32)
                    beside_ref[group, which, kz, mine] = rest_ref[row : row + size, mine]


def put_modes(plan, modes_ref, tail, out_ref, rest_ref):
    pad, size = plan.plane_rows, plan.own_z
    zeros = jnp.zeros((pad - plan.planes, LANES), jnp.float32)
    rest_ref[...] = jnp.zeros((2 * pad, LANES), jnp.float32)
    for place_x in range(plan.size_x):
        block, part = divmod(place_x, plan.part_z)
        for which in range(2):
            for inner in range(plan.own_c):
                channel = block * plan.own_c + inner
                row = which * pad + inner * size
                kz = slice(part * size, (part + 1) * size)
                for at in range(2):
                    begin = at * 2 * pad + row
                    out_ref[place_x, begin : begin + size, :] = modes_ref[
                        channel, which, kz, at * LANES : (at + 1) * LANES
                    ]
                rest_ref[row : row + size, 0:32] = tail(channel, which)[kz, 0:32]
            for at in range(2):
                begin = at * 2 * pad + which * pad + plan.planes
                out_ref[place_x, begin : begin + pad - plan.planes, :] = zeros
        out_ref[place_x, 4 * pad : 4 * pad + 8, :] = pack_rest(rest_ref)


def bring_weights(plan, weight_hbm, weight_ref, beside_hbm, beside_ref, arrived, by_input):
    full = pl.ds(0, 2 * LANES)
    size = plan.channels // CHUNKS
    copies = [pltpu.make_async_copy(beside_hbm, beside_ref, arrived.at[CHUNKS])]
    for chunk in range(CHUNKS):
        mine = pl.ds(chunk * size, size)
        whole = slice(None)
        source = (whole, mine) if by_input else (whole, whole, mine)
        source = source + (whole,) * (4 - len(source)) + (full,)
        target = source[:4]
        copies.append(
            pltpu.make_async_copy(weight_hbm.at[source], weight_ref.at[target], arrived.at[chunk])
        )
    for copy in copies:
        copy.start()
    return copies


def add_product(sums, weight_re, weight_im, value_re, value_im, back):
    weight_re = weight_re.astype(jnp.float32)
    weight_im = weight_im.astype(jnp.float32)
    if back:
        return (
            sums[0] + (weight_re * value_re + weight_im * value_im),
            sums[1] + (weight_re * value_im - weight_im * value_re),
        )
    return (
        sums[0] + (weight_re * value_re - weight_im * value_im),
        sums[1] + (weight_re * value_im + weight_im * value_re),
    )


def mix_kernel(
    plan,
    in_ref,
    weight_hbm,
    beside_hbm,
    out_ref,
    spectrum_ref,
    mixed_ref,
    rest_ref,
    tails_ref,
    weight_ref,
    beside_ref,
    arrived,
):
    copies = bring_weights(plan, weight_hbm, weight_ref, beside_hbm, beside_ref, arrived, False)
    take_modes(plan, in_ref, spectrum_ref, rest_ref)
    full, end = slice(0, 2 * LANES), slice(2 * LANES, 3 * LANES)
    size = plan.channels // CHUNKS
    copies[0].wait()
    for chunk, copy in enumerate(copies[1:]):
        copy.wait()
        for out_channel in range(chunk * size, (chunk + 1) * size):
            zeros = jnp.zeros((plan.blocks_z, 2 * LANES), jnp.float32)
            sums = (zeros, zeros)
            for channel in range(plan.channels):
                sums = add_product(
                    sums,
                    weight_ref[0, channel, out_channel],
                    weight_ref[1, channel, out_channel],
                    spectrum_ref[channel, 0, :, full],
                    spectrum_ref[channel, 1, :, full],
                    False,
                )
            mixed_ref[out_channel, 0], mixed_ref[out_channel, 1] = sums
    for group in range(plan.channels // 4):
        zeros = jnp.zeros((plan.blocks_z, LANES), jnp.float32)
        sums = (zeros, zeros)
        for channel in range(plan.channels):
            sums = add_product(
                sums,
                beside_ref[0, channel, group],
                beside_ref[1, channel, group],
                spectrum_ref[channel, 0, :, end],
                spectrum_ref[channel, 1, :, end],
                False,
            )
        tails_ref[group, 0], tails_ref[group, 1] = sums

    def tail(channel, which):
        group, slot = divmod(channel, 4)
        return roll_lanes(tails_ref[group, which], -slot * 32)

    put_modes(plan, mixed_ref, tail, out_ref, rest_ref)


def mix_back_kernel(
    plan,
    in_ref,
    weight_hbm,
    beside_hbm,
    out_ref,
    grad_ref,
    sums_ref,
    mixed_ref,
    rest_ref,
    tails_ref,
    weight_ref,
    beside_ref,
    arrived,
    grad_beside_ref,
):
    copies = bring_weights(plan, weight_hbm, weight_ref, beside_hbm, beside_ref, arrived, True)
    spare = jnp.zeros((1, LANES), jnp.float32)
    for place_x in range(plan.size_x):
        spare = spare + in_ref[place_x, plan.planes : plan.planes + 1, :]
    sums_ref[...] = jnp.broadcast_to(spare, (8, LANES))
    take_modes(plan, in_ref, grad_ref, rest_ref, grad_beside_ref)
    full = slice(0, 2 * LANES)
    size = plan.channels // CHUNKS
    copies[0].wait()
    for chunk, copy in enumerate(copies[1:]):
        copy.wait()
        for channel in range(chunk * size, (chunk + 1) * size):
            zeros = jnp.zeros((plan.blocks_z, 2 * LANES), jnp.float32)
            sums = (zeros, zeros)
            for out_channel in range(plan.channels):
                sums = add_product(
                    sums,
                    weight_ref[0, channel, out_channel],
                    weight_ref[1, channel, out_channel],
                    grad_ref[out_channel, 0, :, full],
                    grad_ref[out_channel, 1, :, full],
                    True,
                )
            mixed_ref[channel, 0], mixed_ref[channel, 1] = sums
            zeros = jnp.zeros((plan.blocks_z, LANES), jnp.float32)
            sums = (zeros, zeros)
            for group in range(plan.channels // 4):
                sums = add_product(
                    sums,
                    beside_ref[0, channel, group],
                    beside_ref[1, channel, group],
                    grad_beside_ref[group, 0],
                    grad_beside_ref[group, 1],
                    True,
                )
            for which in range(2):
                total = sums[which] + roll_lanes(sums[which], 64)
                tails_ref[channel, which] = total + roll_lanes(total, 32)

    def tail(channel, which):
        return tails_ref[channel, which]

    put_modes(plan, mixed_ref, tail, out_ref, rest_ref)


def weight_grad_kernel(plan, spectrum_ref, grad_ref, sums_ref, out_ref, passed_ref):
    passed_ref[...] = sums_ref[...]
    kept = slice(0, plan.pair_rows)
    value_re = spectrum_ref[0, 0, :, kept]
    value_im = spectrum_ref[0, 1, :, kept]
    for out_channel in range(plan.channels):
        grad_re = grad_ref[out_channel, 0, :, kept]
        grad_im = grad_ref[out_channel, 1, :, kept]
        out_ref[0, 0, out_channel] = value_re * grad_re + value_im * grad_im
        out_ref[1, 0, out_channel] = value_re * grad_im - value_im * grad_re


def weight_grad(plan, spectrum, grad, sums):
    modes = (plan.blocks_z, plan.pair_rows)
    wide = (plan.blocks_z, 3 * LANES)
    return pl.pallas_call(
        functools.partial(weight_grad_kernel, plan),
        grid=(plan.channels,),
        out_shape=[
            jax.ShapeDtypeStruct((2, plan.channels, plan.channels) + modes, jnp.float32),
            jax.ShapeDtypeStruct(sums.shape, jnp.float32),
        ],
        in_specs=[
            pl.BlockSpec((1, 2) + wide, lambda channel: (channel, 0, 0, 0)),
            pl.BlockSpec((plan.channels, 2) + wide, lambda channel: (0, 0, 0, 0)),
            pl.BlockSpec(sums.shape, lambda channel: (0, 0)),
        ],
        out_specs=[
            pl.BlockSpec((2, 1, plan.channels) + modes, lambda channel: (0, channel, 0, 0, 0)),
            pl.BlockSpec(sums.shape, lambda channel: (0, 0)),
        ],
        compiler_params=pltpu.CompilerParams(vmem_limit_bytes=VMEM_BYTES),
    )(spectrum, grad, sums)


def plane_synthesis_kernel(
    plan, in_ref, extra_ref, y_ref, x_ref, out_ref, rows_ref, modes_ref, rest_ref
):
    pad, width = plan.plane_rows, plan.width_y
    lanes = lane_ids(pad)
    for place_x in range(plan.size_x):
        unpack_rest(in_ref[place_x, 4 * pad : 4 * pad + 8, :], rest_ref)
        tiles = []
        for which in range(2):
            row = which * pad
            tiles.append(
                [
                    in_ref[place_x, row : row + pad, :],
                    in_ref[place_x, 2 * pad + row : 3 * pad + row, :],
                    rest_ref[row : row + pad, :],
                ]
            )
        for inner in range(plan.own_kx):
            first = inner * width
            tile, offset = divmod(first, LANES)
            pieces = []
            for which in range(2):
                piece = roll_lanes(tiles[which][tile], which * HALF - offset)
                if offset + width > LANES:
                    later = roll_lanes(tiles[which][tile + 1], which * HALF - offset)
                    piece = jnp.where(lanes < which * HALF + LANES - offset, piece, later)
                pieces.append(piece)
            merged = jnp.where(lanes < HALF, pieces[0], pieces[1])
            used = jnp.bitwise_and(lanes, HALF - 1) < width
            at = (place_x * plan.own_kx + inner) * pad
            modes_ref[at : at + pad, :] = jnp.where(used, merged, 0.0)
    right = jnp.concatenate(
        [modes_ref[pl.ds(plane, plan.width_x, stride=pad), :] for plane in range(plan.planes)],
        axis=1,
    )
    high, low = split(right)
    both = product(x_ref[...], jnp.concatenate([high, high, low], axis=0))
    sign = jnp.where(lane_ids(plan.full_x) < HALF, -1.0, 1.0)
    for plane in range(plan.planes):
        mine = slice(plane * LANES, (plane + 1) * LANES)
        turned = roll_lanes(both[plan.full_x :, mine], HALF)
        rows_ref[pl.ds(plane, plan.full_x, stride=pad), :] = (
            both[: plan.full_x, mine] + sign * turned
        )
    rows_ref[pl.ds(plan.planes, plan.full_x, stride=pad), :] = jnp.zeros(
        (plan.full_x, LANES), jnp.float32
    )
    cells = along_y(rows_ref[...], y_ref[...])
    size = plan.size_x * pad
    cells = swap_blocks(
        [cells[row * size : (row + 1) * size] for row in range(plan.rows_x)], plan.rows_y
    )
    for place_y in range(plan.size_y):
        for which in range(2):
            out_ref[:, place_y, which] = cells[place_y * 2 + which].reshape(
                plan.size_x, pad, LANES
            )
    spare = extra_ref[0:1, :]
    for place_x in range(plan.size_x):
        for place_y in range(plan.size_y):
            out_ref[place_x, place_y, 0, plan.planes : plan.planes + 1, :] = spare


def widen_map(plan, small, transposed):
    rows = plan.channels * plan.rows_y
    row_ids = lax.broadcasted_iota(jnp.int32, (rows, plan.channels), 0)
    column_ids = lax.broadcasted_iota(jnp.int32, (rows, plan.channels), 1)
    spread = jnp.where(row_ids // plan.rows_y == column_ids, 1.0, 0.0).astype(jnp.bfloat16)
    wide = product(spread, small, ((1,), (0,)) if transposed else ((1,), (1,)))
    wide = product(wide.astype(jnp.bfloat16), spread, NT)
    return jnp.where(same_cell(plan), wide, 0.0).astype(jnp.bfloat16)


def same_cell(plan):
    rows = plan.channels * plan.rows_y
    row_ids = lax.broadcasted_iota(jnp.int32, (rows, rows), 0)
    column_ids = lax.broadcasted_iota(jnp.int32, (rows, rows), 1)
    return jnp.bitwise_and(row_ids, plan.rows_y - 1) == jnp.bitwise_and(
        column_ids, plan.rows_y - 1
    )


def synthesize_depth(plan, in_ref, rows_ref, table, channel):
    rows = take_spectrum(plan, in_ref, rows_ref, channel)
    high, low = split(rows)
    return product(jnp.concatenate([high, high, low], axis=0), table, TN)


def pointwise_kernel(
    plan, field_ref, map_ref, bias_ref, weight_ref, out_ref, nothing_ref, beside_ref
):
    def beside(channel, carry):
        for which in range(2):
            for group in range(plan.channels // 4):
                parts = [
                    weight_ref[which, channel, group * 4 + slot, :, 2 * LANES :]
                    for slot in range(4)
                ]
                beside_ref[which, channel, group] = jnp.concatenate(
                    [part.astype(jnp.float32) for part in parts], axis=1
                ).astype(jnp.bfloat16)
        return carry

    lax.fori_loop(0, plan.channels, beside, 0)
    nothing_ref[...] = jnp.zeros((8, LANES), jnp.float32)
    rows, size = plan.channels * plan.rows_y, plan.rows_y
    wide = widen_map(plan, map_ref[...], False)

    def one(row, carry):
        here = pl.ds(row, 1)
        mapped = product(wide, field_ref[:, here].reshape(rows, plan.depth))
        for channel in range(plan.channels):
            part = mapped[channel * size : (channel + 1) * size] + bias_ref[channel]
            out_ref[channel, here] = part.reshape(1, size, plan.depth)
        return carry

    lax.fori_loop(0, plan.rows_x, one, 0)


def activation_kernel(
    plan,
    in_ref,
    pointwise_ref,
    cotangent_ref,
    inverse_ref,
    forward_ref,
    output_hbm,
    spectrum_hbm,
    high_hbm,
    low_hbm,
    rows_ref,
    output_ref,
    spectrum_ref,
    high_ref,
    low_ref,
    sent,
):
    pairs = (
        (spectrum_ref, spectrum_hbm, plan.part_z),
        (output_ref, output_hbm, plan.own_c),
        (high_ref, high_hbm, plan.own_c),
        (low_ref, low_hbm, plan.own_c),
    )
    copies = []
    clear_spare(plan, spectrum_ref)
    flat = (plan.cells, plan.depth)
    block = (plan.rows_x, plan.rows_y, plan.depth)
    inverse = inverse_ref[...]
    forward = forward_ref[...]
    scale = math.sqrt(2.0 / math.pi)
    for channel in range(plan.channels):
        preact = synthesize_depth(plan, in_ref, rows_ref, inverse, channel)
        preact = preact + pointwise_ref[channel].reshape(flat)
        square = preact * preact
        bend = jnp.tanh(preact * (scale + (scale * 0.044715) * square))
        half = 0.5 + 0.5 * bend
        active = preact * half
        output_ref[channel] = active.astype(jnp.bfloat16).reshape(block)
        slope = half + active * (1.0 - half) * (
            2.0 * scale + (6.0 * scale * 0.044715) * square
        )
        grad = cotangent_ref[channel].reshape(flat).astype(jnp.float32) * slope
        high, low = split(grad)
        high_ref[channel] = high.reshape(block)
        low_ref[channel] = low.reshape(block)
        both = product(forward, high, NT)
        more = product(forward[: 2 * MZ], low, NT)
        put_spectrum(plan, spectrum_ref, channel, both[: 2 * MZ] + both[2 * MZ :] + more)
        copies += send_block(plan, channel, pairs, sent)
    for copy in copies:
        copy.wait()


def send_block(plan, channel, pairs, sent):
    block, inner = divmod(channel, plan.own_c)
    if inner < plan.own_c - 1:
        return []
    copies = []
    for at, (held, target, size) in enumerate(pairs):
        mine = pl.ds(block * size, size)
        copies.append(pltpu.make_async_copy(held.at[mine], target.at[mine], sent.at[at, block]))
    for copy in copies:
        copy.start()
    return copies


def pointwise_grad_kernel(
    plan, field_ref, high_ref, low_ref, map_ref, back_ref, sums_ref, cross_ref
):
    rows = plan.channels * plan.rows_y
    wide = widen_map(plan, map_ref[...], True)
    cross_ref[...] = jnp.zeros((rows + 16, rows), jnp.float32)
    ones = jnp.ones((16, plan.depth), jnp.bfloat16)
    slab = (plan.channels, 1, plan.rows_y, plan.depth)

    def one(row, carry):
        here = pl.ds(row, 1)
        values = field_ref[:, here].reshape(rows, plan.depth)
        values = jnp.concatenate([values, ones], axis=0)
        high = high_ref[:, here].reshape(rows, plan.depth)
        low = low_ref[:, here].reshape(rows, plan.depth)
        back_ref[:, here] = (product(wide, high) + product(wide, low)).reshape(slab)
        cross_ref[...] += product(values, high, NT) + product(values, low, NT)
        return carry

    lax.fori_loop(0, plan.rows_x, one, 0)
    row_ids = lax.broadcasted_iota(jnp.int32, (rows, LANES), 0)
    gather = jnp.where(row_ids // plan.rows_y == lane_ids(rows), 1.0, 0.0)
    exact = lax.Precision.HIGHEST
    cross = jnp.where(same_cell(plan), cross_ref[:rows], 0.0)
    by_out = product(cross, gather, precision=exact)
    sums = product(gather, by_out, TN, precision=exact)
    bias_sums = product(cross_ref[rows : rows + 8], gather, precision=exact)
    lanes = lane_ids(1)
    per_row = LANES // SLOT
    for at in range(8):
        packed = jnp.zeros((1, LANES), jnp.float32)
        for slot in range(per_row):
            row = at * per_row + slot
            if row > plan.channels:
                continue
            line = sums[row : row + 1] if row < plan.channels else bias_sums[0:1]
            packed = jnp.where(lanes // SLOT == slot, roll_lanes(line, slot * SLOT), packed)
        sums_ref[at : at + 1, :] = packed


def last_kernel(
    plan,
    in_ref,
    back_ref,
    inverse_ref,
    grad_ref,
    map_grad_ref,
    bias_grad_ref,
    rows_ref,
):
    block = (plan.rows_x, plan.rows_y, plan.depth)
    flat = (plan.cells, plan.depth)
    inverse = inverse_ref[...]
    for channel in range(plan.channels):
        total = synthesize_depth(plan, in_ref, rows_ref, inverse, channel)
        total = total + back_ref[channel].reshape(flat)
        grad_ref[channel] = total.astype(jnp.bfloat16).reshape(block)
    shrink = float(plan.full_x * plan.full_y * plan.depth) ** (-0.5)
    per_row = LANES // SLOT
    for at in range(plan.size_x):
        line = jnp.zeros((1, LANES), jnp.float32)
        for place_y in range(plan.size_y):
            line = line + in_ref[at, place_y, 0, plan.planes : plan.planes + 1, :]
        for slot in range(per_row):
            row = at * per_row + slot
            mine = shrink * roll_lanes(line, -slot * SLOT)[:, : plan.channels]
            if row < plan.channels:
                map_grad_ref[row : row + 1, :] = mine
            elif row == plan.channels:
                bias_grad_ref[...] = mine


def by_planes(plan, field, cotangent, spectral_weight, pointwise_weight, bias):
    pad = plan.plane_rows
    f32 = jnp.float32
    cell_shape = (plan.size_x, plan.size_y, 2, pad, LANES)
    mode_shape = (plan.size_x, 4 * pad + 8, LANES)
    own_shape = (plan.channels, 2, plan.blocks_z, 3 * LANES)
    groups = plan.channels // 4
    beside_shape = (2, plan.channels, groups, plan.blocks_z, LANES)
    grid_shape = field.shape

    def shape(dims, kind=f32):
        return jax.ShapeDtypeStruct(dims, kind)

    def cell_exchange(values):
        flat = values.reshape(plan.devices, 2 * pad, LANES)
        return lax.all_to_all(flat, ("gx", "gy"), 0, 0, tiled=True).reshape(cell_shape)

    def mode_exchange(values):
        return lax.all_to_all(values, "gx", 0, 0, tiled=True)

    z_high, z_low = split_table(plan.z_table(False))
    scaled_high, scaled_low = split_table(plan.z_table(True))
    z_forward = jnp.asarray(np.concatenate([z_high, z_low]))
    z_inverse = jnp.asarray(np.concatenate([z_high, z_low, z_high]))
    scaled_forward = jnp.asarray(np.concatenate([scaled_high, scaled_low]))
    scaled_inverse = jnp.asarray(np.concatenate([scaled_high, scaled_low, scaled_high]))
    y_forward, y_inverse = (jnp.asarray(table) for table in plan.y_tables())
    x_forward, x_inverse = (jnp.asarray(table) for table in plan.x_tables())

    lane_rows = pltpu.VMEM((plan.full_x * pad, LANES), f32)
    lane_modes = pltpu.VMEM((plan.width_x * pad, LANES), f32)
    rest = pltpu.VMEM((2 * pad, LANES), f32)
    own_full = pltpu.VMEM(own_shape[:3] + (2 * LANES,), f32)
    tails = pltpu.VMEM(own_shape[:3] + (LANES,), f32)
    group_tails = pltpu.VMEM((groups,) + own_shape[1:3] + (LANES,), f32)
    lines = pltpu.VMEM((2 * MZ, LANES), f32)
    wide = plan.channels * plan.rows_y
    row_shape = shape((8, LANES))

    blocks_sent = pltpu.SemaphoreType.DMA((4, plan.part_c))

    held_weights = [
        pltpu.VMEM(spectral_weight.shape[:4] + (2 * LANES,), spectral_weight.dtype),
        pltpu.VMEM(beside_shape, jnp.bfloat16),
        pltpu.SemaphoreType.DMA((CHUNKS + 1,)),
    ]

    held_grid = pltpu.VMEM(grid_shape, jnp.bfloat16)

    def in_hbm(struct):
        return pltpu.HBM(struct.shape, struct.dtype)

    def with_plan(kernel):
        return functools.partial(kernel, plan)

    def plane_analysis(cells, extra):
        return call(
            with_plan(plane_analysis_kernel),
            shape(mode_shape),
            [lane_rows, lane_modes, rest],
            cells,
            extra,
            y_forward,
            x_forward,
        )

    def plane_synthesis(modes, extra):
        return call(
            with_plan(plane_synthesis_kernel),
            shape(cell_shape),
            [lane_rows, lane_modes, rest],
            modes,
            extra,
            y_inverse,
            x_inverse,
        )

    with jax.named_scope("depth_analysis"):
        cells = call(
            with_plan(depth_analysis_kernel),
            in_hbm(shape(cell_shape)),
            [
                pltpu.VMEM(grid_shape, jnp.bfloat16),
                pltpu.VMEM(z_forward.shape, jnp.bfloat16),
                pltpu.VMEM(cell_shape, f32),
                pltpu.SemaphoreType.DMA((3,)),
                blocks_sent,
            ],
            field,
            z_forward,
            hbm=(0, 1),
            hbm_outs=(0,),
        )
    with jax.named_scope("cells_to_planes"):
        cells = cell_exchange(cells)
    with jax.named_scope("pointwise"):
        weights = with_layout_constraint(spectral_weight, Layout((0, 1, 2, 3, 4)))
        pointwise, nothing, beside = call(
            with_plan(pointwise_kernel),
            [in_hbm(shape(grid_shape)), row_shape, in_hbm(shape(beside_shape, jnp.bfloat16))],
            [],
            field,
            pointwise_weight,
            bias,
            weights,
            smem=(2,),
        )
    with jax.named_scope("plane_analysis"):
        modes = plane_analysis(cells, nothing)
    with jax.named_scope("planes_to_modes"):
        modes = mode_exchange(modes)
    with jax.named_scope("mix"):
        modes, spectrum = call(
            with_plan(mix_kernel),
            [shape(mode_shape), shape(own_shape)],
            [own_full, rest, group_tails] + held_weights,
            modes,
            weights,
            beside,
            hbm=(1, 2),
        )
    with jax.named_scope("modes_to_planes"):
        modes = mode_exchange(modes)
    with jax.named_scope("plane_synthesis"):
        cells = plane_synthesis(modes, nothing)
    with jax.named_scope("planes_to_cells"):
        cells = cell_exchange(cells)
    with jax.named_scope("activation"):
        half_grid = shape(grid_shape, jnp.bfloat16)
        output, cells, grad_high, grad_low = call(
            with_plan(activation_kernel),
            [in_hbm(half_grid), in_hbm(shape(cell_shape)), in_hbm(half_grid), in_hbm(half_grid)],
            [lines, held_grid, pltpu.VMEM(cell_shape, f32), held_grid, held_grid, blocks_sent],
            cells,
            pointwise,
            cotangent,
            scaled_inverse,
            scaled_forward,
            hbm_outs=(0, 1, 2, 3),
        )
    with jax.named_scope("grad_cells_to_planes"):
        cells = cell_exchange(cells)
    with jax.named_scope("pointwise_grad"):
        back, sums = call(
            with_plan(pointwise_grad_kernel),
            [in_hbm(shape(grid_shape)), row_shape],
            [pltpu.VMEM((wide + 16, wide), f32)],
            field,
            grad_high,
            grad_low,
            pointwise_weight,
        )
    with jax.named_scope("grad_plane_analysis"):
        modes = plane_analysis(cells, sums)
    with jax.named_scope("grad_planes_to_modes"):
        modes = mode_exchange(modes)
    with jax.named_scope("grad_mix"):
        modes, grad_mix, sums = call(
            with_plan(mix_back_kernel),
            [shape(mode_shape), shape(own_shape), row_shape],
            [own_full, rest, tails] + held_weights + [group_tails],
            modes,
            weights,
            beside,
            hbm=(1, 2),
        )
    with jax.named_scope("grad_modes_to_planes"):
        modes = mode_exchange(modes)
    with jax.named_scope("grad_spectral"):
        grad_spectral, sums = weight_grad(plan, spectrum, grad_mix, sums)
    with jax.named_scope("grad_plane_synthesis"):
        cells = plane_synthesis(modes, sums)
    with jax.named_scope("grad_planes_to_cells"):
        cells = cell_exchange(cells)
    with jax.named_scope("grad_field"):
        channels = plan.channels
        grad_field, map_grad, bias_grad = call(
            with_plan(last_kernel),
            [half_grid, shape((channels, channels)), shape((1, channels))],
            [lines],
            cells,
            back,
            z_inverse,
        )
    return output, grad_field, grad_spectral, map_grad, bias_grad.reshape(channels)


def layer(field, cotangent, spectral_weight, pointwise_weight, bias):
    plan = Plan(
        field.shape, spectral_weight.shape, lax.axis_size("gx"), lax.axis_size("gy")
    )
    if plan.fits:
        return by_planes(plan, field, cotangent, spectral_weight, pointwise_weight, bias)
    return local(field, cotangent, spectral_weight, pointwise_weight, bias)


def solution(mesh):
    placed = (
        P(None, "gx", "gy", None),
        P(None, "gx", "gy", None),
        P(None, None, None, "gy", "gx"),
        P(),
        P(),
    )
    return jax.shard_map(
        layer,
        mesh=mesh,
        in_specs=placed,
        out_specs=(
            P(None, "gx", "gy", None),
            P(None, "gx", "gy", None),
            P(None, None, None, "gy", "gx"),
            P(),
            P(),
        ),
        check_vma=False,
    )
```

```python
import functools
import math

import jax
import jax.numpy as jnp
from jax import lax
import numpy as np
from jax.experimental import pallas as pl
from jax.experimental.layout import Layout, with_layout_constraint
from jax.experimental.pallas import tpu as pltpu
from jax.sharding import PartitionSpec as P

MX = 24
MY = 24
MZ = 24


PRECISE = lax.Precision.HIGHEST
TWO_PI = 2.0 * math.pi


def angles(frequencies, places, length):
    product = places[:, None] * frequencies[None, :] % length
    return product.astype(jnp.float32) * (TWO_PI / length)


def frequency(position, kept_modes, length):
    return jnp.where(position < kept_modes, position, position - 2 * kept_modes + length)


def forward_y(values, phases):
    cosine_table = jnp.cos(phases)
    sine_table = jnp.sin(phases)
    with_cos = jnp.einsum("brcxy,yj->brcxj", values, cosine_table, precision=PRECISE)
    with_sin = jnp.einsum("brcxy,yj->brcxj", values, sine_table, precision=PRECISE)
    real_part = with_cos[:, 0] + with_sin[:, 1]
    imag_part = with_cos[:, 1] - with_sin[:, 0]
    return jnp.stack([real_part, imag_part], axis=1)


def inverse_y(values, phases):
    cosine_table = jnp.cos(phases)
    sine_table = jnp.sin(phases)
    with_cos = jnp.einsum("brcxj,yj->brcxy", values, cosine_table, precision=PRECISE)
    with_sin = jnp.einsum("brcxj,yj->brcxy", values, sine_table, precision=PRECISE)
    real_part = with_cos[:, 0] - with_sin[:, 1]
    imag_part = with_sin[:, 0] + with_cos[:, 1]
    return jnp.stack([real_part, imag_part], axis=1)


def local(field, cotangent, spectral_weight, pointwise_weight, bias):
    channels, rows_x, rows_y, depth_cells = field.shape
    blocks_z = spectral_weight.shape[3]
    pair_rows = spectral_weight.shape[4]
    width_x = 2 * MX
    width_y = 2 * MY
    full_x = rows_x * lax.axis_size("gx")
    full_y = rows_y * lax.axis_size("gy")
    cell_count = float(full_x * full_y * depth_cells)
    place_x = lax.axis_index("gx")
    place_y = lax.axis_index("gy")
    own_x = place_x * rows_x + jnp.arange(rows_x, dtype=jnp.int32)
    freq_x = frequency(jnp.arange(width_x, dtype=jnp.int32), MX, full_x)
    freq_y = frequency(jnp.arange(width_y, dtype=jnp.int32), MY, full_y)
    phases_full_y = angles(freq_y, jnp.arange(full_y, dtype=jnp.int32), full_y)
    z_phases = angles(
        jnp.arange(MZ, dtype=jnp.int32), jnp.arange(depth_cells, dtype=jnp.int32), depth_cells
    )
    table_z = jnp.stack([jnp.cos(z_phases), -jnp.sin(z_phases)], axis=2).reshape(
        depth_cells, 2 * MZ
    )
    kz_own = place_y * blocks_z + jnp.arange(blocks_z, dtype=jnp.int32)
    weight_z = (jnp.where(kz_own == 0, 1.0, 2.0).astype(jnp.float32) / cell_count)[None, :, None]
    own_first = place_x * pair_rows
    flat_width = blocks_z * 2 * channels

    def kx_terms(values, places, first_pair, count):
        kx_count = min(count // width_y + 2, width_x)
        kx_first = jnp.minimum(first_pair // width_y, width_x - kx_count)
        kx_ids = kx_first + jnp.arange(kx_count, dtype=jnp.int32)
        phases = angles(frequency(kx_ids, MX, full_x), places, full_x)
        cosine_table = jnp.cos(phases)
        sine_table = jnp.sin(phases)
        real_part = jnp.einsum(
            "bcxj,xi->ijbc", values[:, 0], cosine_table, precision=PRECISE
        ) + jnp.einsum("bcxj,xi->ijbc", values[:, 1], sine_table, precision=PRECISE)
        imag_part = jnp.einsum(
            "bcxj,xi->ijbc", values[:, 1], cosine_table, precision=PRECISE
        ) - jnp.einsum("bcxj,xi->ijbc", values[:, 0], sine_table, precision=PRECISE)
        terms = jnp.stack([real_part, imag_part], axis=3).reshape(kx_count * width_y, flat_width)
        offset = first_pair - kx_first * width_y
        return lax.dynamic_slice_in_dim(terms, offset, count, 0)

    def analyze(values):
        flat = values.reshape(-1, depth_cells)
        spectra = jnp.einsum("zk,mz->km", table_z, flat, precision=PRECISE).reshape(
            2 * MZ, channels, rows_x, rows_y
        )
        columns = lax.all_to_all(spectra, "gy", split_axis=0, concat_axis=3, tiled=True)
        mode_data = forward_y(columns.reshape(blocks_z, 2, channels, rows_x, full_y), phases_full_y)
        portion = lax.all_gather(mode_data, "gx", axis=3, tiled=True)
        places = jnp.arange(portion.shape[3], dtype=jnp.int32)
        owned = kx_terms(portion, places, own_first, pair_rows)
        return jnp.transpose(owned.reshape(pair_rows, blocks_z, 2, channels), (2, 3, 1, 0))

    def synthesize(spectrum):
        portion = lax.all_gather(spectrum, "gx", axis=3, tiled=True)
        blocks = portion.reshape(2, channels, blocks_z, width_x, width_y)
        phases = angles(freq_x, own_x, full_x)
        cosine_table = jnp.cos(phases)
        sine_table = jnp.sin(phases)
        real_part = jnp.einsum(
            "cbij,xi->bcxj", blocks[0], cosine_table, precision=PRECISE
        ) - jnp.einsum("cbij,xi->bcxj", blocks[1], sine_table, precision=PRECISE)
        imag_part = jnp.einsum(
            "cbij,xi->bcxj", blocks[0], sine_table, precision=PRECISE
        ) + jnp.einsum("cbij,xi->bcxj", blocks[1], cosine_table, precision=PRECISE)
        mode_data = jnp.stack([real_part, imag_part], axis=1)
        fields = inverse_y(mode_data, phases_full_y)
        columns = lax.all_to_all(fields, "gy", split_axis=4, concat_axis=0, tiled=True)
        flat = columns.reshape(2 * MZ, -1)
        return jnp.einsum("km,zk->mz", flat, table_z, precision=PRECISE).reshape(
            channels, rows_x, rows_y, depth_cells
        )

    weights = spectral_weight.astype(jnp.float32)
    widened = field.astype(jnp.float32)
    spec_u = analyze(widened)
    mixed_re = jnp.einsum("cobp,cbp->obp", weights[0], spec_u[0], precision=PRECISE) - jnp.einsum(
        "cobp,cbp->obp", weights[1], spec_u[1], precision=PRECISE
    )
    mixed_im = jnp.einsum("cobp,cbp->obp", weights[0], spec_u[1], precision=PRECISE) + jnp.einsum(
        "cobp,cbp->obp", weights[1], spec_u[0], precision=PRECISE
    )
    mixed_modes = jnp.stack([mixed_re, mixed_im]) * weight_z
    conv = synthesize(mixed_modes)
    pointwise = jnp.dot(
        pointwise_weight.T, field.reshape(channels, -1), preferred_element_type=jnp.float32
    ).reshape(field.shape)
    preact = pointwise + bias[:, None, None, None] + conv
    activated, pullback = jax.vjp(jax.nn.gelu, preact)
    gradient = pullback(cotangent.astype(jnp.float32))[0]
    grad_mix = analyze(gradient) * weight_z
    spec_re = jnp.einsum("cobp,obp->cbp", weights[0], grad_mix[0], precision=PRECISE) + jnp.einsum(
        "cobp,obp->cbp", weights[1], grad_mix[1], precision=PRECISE
    )
    spec_im = jnp.einsum("cobp,obp->cbp", weights[0], grad_mix[1], precision=PRECISE) - jnp.einsum(
        "cobp,obp->cbp", weights[1], grad_mix[0], precision=PRECISE
    )
    grad_spec = jnp.stack([spec_re, spec_im])
    weight_re = jnp.einsum("cbp,obp->cobp", spec_u[0], grad_mix[0], precision=PRECISE) + jnp.einsum(
        "cbp,obp->cobp", spec_u[1], grad_mix[1], precision=PRECISE
    )
    weight_im = jnp.einsum("cbp,obp->cobp", spec_u[0], grad_mix[1], precision=PRECISE) - jnp.einsum(
        "cbp,obp->cobp", spec_u[1], grad_mix[0], precision=PRECISE
    )
    grad_spectral = jnp.stack([weight_re, weight_im])
    returned = synthesize(grad_spec)
    grad_flat = gradient.reshape(channels, -1)
    back_point = jnp.dot(
        pointwise_weight.astype(jnp.float32), grad_flat, precision=PRECISE
    ).reshape(field.shape)
    grad_field = (back_point + returned).astype(jnp.bfloat16)
    local_weight = jnp.dot(widened.reshape(channels, -1), grad_flat.T, precision=PRECISE)
    local_bias = jnp.sum(grad_flat, axis=1)
    summed_weight, summed_bias = lax.psum((local_weight, local_bias), ("gx", "gy"))
    shrink = cell_count ** (-0.5)
    return (
        activated.astype(jnp.bfloat16),
        grad_field,
        grad_spectral,
        summed_weight * shrink,
        summed_bias * shrink,
    )


LANES = 128
HALF = 64
SLOT = 32
CHUNKS = 5
VMEM_BYTES = 20 * 1024 * 1024


def split_table(table):
    high = table.astype(jnp.bfloat16)
    low = (table - high.astype(np.float64)).astype(jnp.bfloat16)
    return high, low


def frequency_table(kept_modes, length):
    position = np.arange(2 * kept_modes)
    return np.where(position < kept_modes, position, position - 2 * kept_modes + length)


def phase_table(frequencies, places, length):
    product = places[:, None] * frequencies[None, :] % length
    return product.astype(np.float64) * (TWO_PI / length)


def split(values):
    high = values.astype(jnp.bfloat16)
    low = (values - high.astype(jnp.float32)).astype(jnp.bfloat16)
    return high, low


def product(left, right, contract=((1,), (0,)), precision=None):
    return lax.dot_general(
        left, right, (contract, ((), ())), preferred_element_type=jnp.float32, precision=precision
    )


NT = ((1,), (1,))
TN = ((0,), (0,))


def lane_ids(rows):
    return lax.broadcasted_iota(jnp.int32, (rows, LANES), 1)


def roll_lanes(values, shift):
    shift = shift % LANES
    if shift == 0:
        return values
    return pltpu.roll(values, shift, 1)


class Plan:
    def __init__(self, field_shape, weight_shape, size_x, size_y):
        self.channels, self.rows_x, self.rows_y, self.depth = field_shape
        self.size_x, self.size_y = size_x, size_y
        self.blocks_z = weight_shape[3]
        self.pair_rows = weight_shape[4]
        self.full_x = self.rows_x * size_x
        self.full_y = self.rows_y * size_y
        self.width_x, self.width_y = 2 * MX, 2 * MY
        self.cells = self.rows_x * self.rows_y
        self.part_c, self.part_z = 0, 0
        for part_z in range(1, self.blocks_z + 1):
            part_c = size_x // part_z
            if size_x % part_z or self.blocks_z % part_z or self.channels % part_c:
                continue
            self.part_c, self.part_z = part_c, part_z
        self.fits = False
        if self.part_c == 0:
            return
        self.own_c = self.channels // self.part_c
        self.own_z = self.blocks_z // self.part_z
        self.planes = self.own_c * self.own_z
        self.plane_rows = 16
        self.own_kx = self.pair_rows // self.width_y
        self.devices = size_x * size_y
        self.fits = (
            self.cells == LANES
            and self.rows_y == 16
            and self.size_y * 2 == self.rows_x
            and self.depth % LANES == 0
            and self.planes < self.plane_rows
            and self.pair_rows % self.width_y == 0
            and self.pair_rows == 2 * LANES + 32
            and self.width_y <= HALF
            and 3 * max(self.full_x, self.width_x) <= 2 * LANES
            and size_x == 8
            and self.channels % CHUNKS == 0
            and self.channels % 4 == 0
            and self.channels <= SLOT
            and self.channels < size_x * (LANES // SLOT)
            and self.own_z * 2 * self.part_z * size_y == 2 * MZ
        )

    def z_table(self, scaled):
        kz = np.arange(MZ)
        phases = phase_table(kz, np.arange(self.depth), self.depth)
        both = np.stack([np.cos(phases), -np.sin(phases)])
        if scaled:
            cells = float(self.full_x * self.full_y * self.depth)
            both = both * (np.where(kz == 0, 1.0, 2.0) / cells)
        both = both.reshape(2, self.depth, self.size_y, self.part_z, self.own_z)
        return both.transpose(2, 3, 0, 4, 1).reshape(2 * MZ, self.depth)

    def y_tables(self):
        freq = frequency_table(MY, self.full_y)
        phases = phase_table(freq, np.arange(self.full_y), self.full_y)
        cosine, sine = np.cos(phases), np.sin(phases)
        one = np.zeros((self.size_y, 2, self.rows_y, 2, HALF))
        by_block = (self.size_y, self.rows_y, self.width_y)
        one[:, 0, :, 0, : self.width_y] = cosine.reshape(by_block)
        one[:, 1, :, 0, : self.width_y] = sine.reshape(by_block)
        one[:, 0, :, 1, : self.width_y] = -sine.reshape(by_block)
        one[:, 1, :, 1, : self.width_y] = cosine.reshape(by_block)
        one = one.reshape(LANES, LANES)
        tables = []
        for table in (one, one.T):
            high, low = split_table(table)
            top = np.concatenate([high, low], axis=1)
            bottom = np.concatenate([high, np.zeros_like(low)], axis=1)
            tables.append(np.concatenate([top, bottom], axis=0))
        return tables

    def x_tables(self):
        freq = frequency_table(MX, self.full_x)
        phases = phase_table(freq, np.arange(self.full_x), self.full_x)
        phases = phases.reshape(self.size_x, self.rows_x, self.width_x).transpose(1, 0, 2)
        phases = phases.reshape(self.full_x, self.width_x)
        cosine, sine = np.cos(phases), np.sin(phases)
        forward = np.concatenate([cosine.T, sine.T], axis=0)
        inverse = np.concatenate([cosine, sine], axis=0)
        tables = []
        for table in (forward, inverse):
            high, low = split_table(table)
            tables.append(np.concatenate([high, low, high], axis=1))
        return tables

    def plane_tables(self):
        tables = []
        for along_y, along_x in zip(self.y_tables(), self.x_tables()):
            rows, columns = along_x.shape
            spare = ((0, -rows % 16), (0, 2 * LANES - columns))
            tables.append(np.concatenate([along_y, np.pad(along_x, spare)], axis=0))
        return tables


def plane_products(table_ref, rows, columns):
    across = 2 * LANES
    return table_ref[:across], table_ref[across : across + rows, :columns]


def call(kernel, out_shape, scratch, *operands, smem=(), hbm=(), hbm_outs=()):
    operands = [
        pltpu.with_memory_space_constraint(operand, pltpu.HBM) if at in hbm else operand
        for at, operand in enumerate(operands)
    ]
    specs = []
    for at in range(len(operands)):
        space = pltpu.SMEM if at in smem else pltpu.HBM if at in hbm else pltpu.VMEM
        specs.append(pl.BlockSpec(memory_space=space))
    single = not isinstance(out_shape, (tuple, list))
    shapes = [out_shape] if single else out_shape
    outs = [
        pl.BlockSpec(memory_space=pltpu.HBM if at in hbm_outs else pltpu.VMEM)
        for at in range(len(shapes))
    ]
    return pl.pallas_call(
        kernel,
        out_shape=out_shape,
        in_specs=specs,
        out_specs=outs[0] if single else outs,
        scratch_shapes=scratch,
        compiler_params=pltpu.CompilerParams(vmem_limit_bytes=VMEM_BYTES),
    )(*operands)


def put_spectrum(plan, out_ref, channel, rows):
    block, inner = divmod(channel, plan.own_c)
    size = plan.own_z
    at = 0
    for place_y in range(plan.size_y):
        for part in range(plan.part_z):
            place_x = block * plan.part_z + part
            for which in range(2):
                out_ref[place_x, place_y, which, inner * size : (inner + 1) * size, :] = rows[
                    at : at + size
                ]
                at += size


def take_spectrum(plan, in_ref, rows_ref, channel):
    block, inner = divmod(channel, plan.own_c)
    size = plan.own_z
    at = 0
    for place_y in range(plan.size_y):
        for part in range(plan.part_z):
            place_x = block * plan.part_z + part
            for which in range(2):
                rows_ref[channel, at : at + size, :] = in_ref[
                    place_x, place_y, which, inner * size : (inner + 1) * size, :
                ]
                at += size
    return rows_ref[channel]


def clear_spare(plan, out_ref):
    zeros = jnp.zeros((plan.plane_rows - plan.planes, LANES), jnp.float32)
    for place_x in range(plan.size_x):
        for place_y in range(plan.size_y):
            for which in range(2):
                out_ref[place_x, place_y, which, plan.planes :, :] = zeros


def depth_analysis_kernel(
    plan, field_ref, table_ref, out_hbm, blocks_ref, held_ref, out_ref, arrived, sent
):
    copies = [pltpu.make_async_copy(table_ref, held_ref, arrived.at[2])]
    size = plan.channels // 2
    for part in range(2):
        mine = pl.ds(part * size, size)
        copies.append(
            pltpu.make_async_copy(field_ref.at[mine], blocks_ref.at[mine], arrived.at[part])
        )
    for copy in copies:
        copy.start()
    clear_spare(plan, out_ref)
    leaving = []
    copies[0].wait()
    table = held_ref[...]
    for channel in range(plan.channels):
        if channel % size == 0:
            copies[1 + channel // size].wait()
        block = blocks_ref[channel].reshape(plan.cells, plan.depth)
        both = product(table, block, NT)
        put_spectrum(plan, out_ref, channel, both[: 2 * MZ] + both[2 * MZ :])
        leaving += send_block(plan, channel, ((out_ref, out_hbm, plan.part_z),), sent)
    for copy in leaving:
        copy.wait()


def swap_blocks(values, block):
    values = list(values)
    lanes = lane_ids(values[0].shape[0])
    step = 1
    while step < len(values):
        low = jnp.bitwise_and(lanes, step * block) == 0
        for at in range(len(values)):
            if at & step:
                continue
            first, second = values[at], values[at + step]
            values[at] = jnp.where(low, first, roll_lanes(second, step * block))
            values[at + step] = jnp.where(low, roll_lanes(first, -step * block), second)
        step *= 2
    return values


def along_y(values, table):
    high, low = split(values)
    both = product(jnp.concatenate([high, low], axis=1), table)
    return both[:, :LANES] + both[:, LANES:]


def plane_analysis_kernel(
    plan, in_ref, extra_ref, table_ref, out_ref, rows_ref, modes_ref, rest_ref
):
    y_table, x_table = plane_products(table_ref, 2 * plan.width_x, 3 * plan.full_x)
    pad = plan.plane_rows
    left = [
        in_ref[:, place_y, which].reshape(plan.size_x * pad, LANES)
        for place_y in range(plan.size_y)
        for which in range(2)
    ]
    rows_ref[...] = along_y(
        jnp.concatenate(swap_blocks(left, plan.rows_y), axis=0), y_table
    )
    right = jnp.concatenate(
        [rows_ref[pl.ds(plane, plan.full_x, stride=pad), :] for plane in range(plan.planes)], axis=1
    )
    high, low = split(right)
    both = product(x_table, jnp.concatenate([high, high, low], axis=0))
    sign = jnp.where(lane_ids(plan.width_x) < HALF, 1.0, -1.0)
    for plane in range(plan.planes):
        mine = slice(plane * LANES, (plane + 1) * LANES)
        turned = roll_lanes(both[plan.width_x :, mine], HALF)
        modes_ref[pl.ds(plane, plan.width_x, stride=pad), :] = (
            both[: plan.width_x, mine] + sign * turned
        )
    modes_ref[pl.ds(plan.planes, plan.width_x, stride=pad), :] = jnp.zeros(
        (plan.width_x, LANES), jnp.float32
    )
    lanes = lane_ids(pad)
    width = plan.width_y
    for place_x in range(plan.size_x):
        for which in range(2):
            tiles = [None, None, None]
            for inner in range(plan.own_kx):
                kx = place_x * plan.own_kx + inner
                first = inner * width
                turned = roll_lanes(modes_ref[kx * pad : (kx + 1) * pad, :], first - which * HALF)
                tile, offset = divmod(first, LANES)
                for at in (tile, tile + 1):
                    begin = first - at * LANES
                    if begin >= LANES or begin + width <= 0:
                        continue
                    if tiles[at] is None:
                        tiles[at] = turned
                    else:
                        tiles[at] = jnp.where(lanes < begin, tiles[at], turned)
            for at in range(2):
                row = at * 2 * pad + which * pad
                out_ref[place_x, row : row + pad, :] = tiles[at]
            rest_ref[place_x, which * pad : (which + 1) * pad, :] = tiles[2]
        out_ref[place_x, 4 * pad : 4 * pad + 8, :] = pack_rest(rest_ref.at[place_x])
        out_ref[place_x, plan.planes : plan.planes + 1, :] = extra_ref[place_x : place_x + 1, :]


def pack_rest(rest_ref):
    lanes = lane_ids(8)
    packed = rest_ref[0:8, :]
    for group in range(1, 4):
        turned = roll_lanes(rest_ref[group * 8 : (group + 1) * 8, :], group * 32)
        packed = jnp.where(lanes < group * 32, packed, turned)
    return packed


def unpack_rest(packed, rest_ref, repeated=False):
    lanes = lane_ids(8)
    for group in range(4):
        turned = roll_lanes(packed, -group * 32)
        if repeated:
            turned = jnp.where(lanes < 32, turned, roll_lanes(turned, 32))
            turned = jnp.where(lanes < 64, turned, roll_lanes(turned, 64))
        rest_ref[group * 8 : (group + 1) * 8, :] = turned


def take_modes(plan, in_ref, modes_ref, rest_ref, beside_ref=None):
    pad, size = plan.plane_rows, plan.own_z
    for place_x in range(plan.size_x):
        block, part = divmod(place_x, plan.part_z)
        unpack_rest(in_ref[place_x, 4 * pad : 4 * pad + 8, :], rest_ref.at[place_x], True)
        for which in range(2):
            for inner in range(plan.own_c):
                channel = block * plan.own_c + inner
                row = which * pad + inner * size
                kz = slice(part * size, (part + 1) * size)
                for at in range(2):
                    begin = at * 2 * pad + row
                    modes_ref[channel, which, kz, at * LANES : (at + 1) * LANES] = in_ref[
                        place_x, begin : begin + size, :
                    ]
                modes_ref[channel, which, kz, 2 * LANES :] = rest_ref[place_x, row : row + size, :]
                if beside_ref is not None:
                    group, slot = divmod(channel, 4)
                    mine = slice(slot * 32, (slot + 1) * 32)
                    beside_ref[group, which, kz, mine] = rest_ref[place_x, row : row + size, mine]


def put_modes(plan, modes_ref, tail, out_ref, rest_ref):
    pad, size = plan.plane_rows, plan.own_z
    zeros = jnp.zeros((pad - plan.planes, LANES), jnp.float32)
    rest_ref[...] = jnp.zeros(rest_ref.shape, jnp.float32)
    for place_x in range(plan.size_x):
        block, part = divmod(place_x, plan.part_z)
        for which in range(2):
            for inner in range(plan.own_c):
                channel = block * plan.own_c + inner
                row = which * pad + inner * size
                kz = slice(part * size, (part + 1) * size)
                for at in range(2):
                    begin = at * 2 * pad + row
                    out_ref[place_x, begin : begin + size, :] = modes_ref[
                        channel, which, kz, at * LANES : (at + 1) * LANES
                    ]
                rest_ref[place_x, row : row + size, 0:32] = tail(channel, which)[kz, 0:32]
            for at in range(2):
                begin = at * 2 * pad + which * pad + plan.planes
                out_ref[place_x, begin : begin + pad - plan.planes, :] = zeros
        out_ref[place_x, 4 * pad : 4 * pad + 8, :] = pack_rest(rest_ref.at[place_x])


def bring_weights(plan, weight_hbm, weight_ref, beside_hbm, beside_ref, arrived, by_input):
    full = pl.ds(0, 2 * LANES)
    size = plan.channels // CHUNKS
    copies = [pltpu.make_async_copy(beside_hbm, beside_ref, arrived.at[CHUNKS])]
    for chunk in range(CHUNKS):
        mine = pl.ds(chunk * size, size)
        whole = slice(None)
        source = (whole, mine) if by_input else (whole, whole, mine)
        source = source + (whole,) * (4 - len(source)) + (full,)
        target = source[:4]
        copies.append(
            pltpu.make_async_copy(weight_hbm.at[source], weight_ref.at[target], arrived.at[chunk])
        )
    for copy in copies:
        copy.start()
    return copies


def add_product(sums, weight_re, weight_im, value_re, value_im, back):
    weight_re = weight_re.astype(jnp.float32)
    weight_im = weight_im.astype(jnp.float32)
    if back:
        return (
            sums[0] + (weight_re * value_re + weight_im * value_im),
            sums[1] + (weight_re * value_im - weight_im * value_re),
        )
    return (
        sums[0] + (weight_re * value_re - weight_im * value_im),
        sums[1] + (weight_re * value_im + weight_im * value_re),
    )


def mix_kernel(
    plan,
    in_ref,
    weight_hbm,
    beside_hbm,
    out_ref,
    spectrum_hbm,
    mixed_ref,
    rest_ref,
    tails_ref,
    weight_ref,
    beside_ref,
    arrived,
    spectrum_ref,
    sent,
):
    copies = bring_weights(plan, weight_hbm, weight_ref, beside_hbm, beside_ref, arrived, False)
    take_modes(plan, in_ref, spectrum_ref, rest_ref)
    leaving = pltpu.make_async_copy(spectrum_ref, spectrum_hbm, sent)
    leaving.start()
    full, end = slice(0, 2 * LANES), slice(2 * LANES, 3 * LANES)
    size = plan.channels // CHUNKS
    copies[0].wait()
    for chunk, copy in enumerate(copies[1:]):
        copy.wait()
        for out_channel in range(chunk * size, (chunk + 1) * size):
            zeros = jnp.zeros((plan.blocks_z, 2 * LANES), jnp.float32)
            sums = (zeros, zeros)
            for channel in range(plan.channels):
                sums = add_product(
                    sums,
                    weight_ref[0, channel, out_channel],
                    weight_ref[1, channel, out_channel],
                    spectrum_ref[channel, 0, :, full],
                    spectrum_ref[channel, 1, :, full],
                    False,
                )
            mixed_ref[out_channel, 0], mixed_ref[out_channel, 1] = sums
    for group in range(plan.channels // 4):
        zeros = jnp.zeros((plan.blocks_z, LANES), jnp.float32)
        sums = (zeros, zeros)
        for channel in range(plan.channels):
            sums = add_product(
                sums,
                beside_ref[0, channel, group],
                beside_ref[1, channel, group],
                spectrum_ref[channel, 0, :, end],
                spectrum_ref[channel, 1, :, end],
                False,
            )
        tails_ref[group, 0], tails_ref[group, 1] = sums

    def tail(channel, which):
        group, slot = divmod(channel, 4)
        return roll_lanes(tails_ref[group, which], -slot * 32)

    put_modes(plan, mixed_ref, tail, out_ref, rest_ref)
    leaving.wait()


def mix_back_kernel(
    plan,
    in_ref,
    weight_hbm,
    beside_hbm,
    out_ref,
    grad_hbm,
    sums_ref,
    mixed_ref,
    rest_ref,
    tails_ref,
    weight_ref,
    beside_ref,
    arrived,
    grad_beside_ref,
    grad_ref,
    sent,
):
    copies = bring_weights(plan, weight_hbm, weight_ref, beside_hbm, beside_ref, arrived, True)
    spare = jnp.zeros((1, LANES), jnp.float32)
    for place_x in range(plan.size_x):
        spare = spare + in_ref[place_x, plan.planes : plan.planes + 1, :]
    sums_ref[...] = jnp.broadcast_to(spare, (8, LANES))
    take_modes(plan, in_ref, grad_ref, rest_ref, grad_beside_ref)
    leaving = pltpu.make_async_copy(grad_ref, grad_hbm, sent)
    leaving.start()
    full = slice(0, 2 * LANES)
    size = plan.channels // CHUNKS
    copies[0].wait()
    for chunk, copy in enumerate(copies[1:]):
        copy.wait()
        for channel in range(chunk * size, (chunk + 1) * size):
            zeros = jnp.zeros((plan.blocks_z, 2 * LANES), jnp.float32)
            sums = (zeros, zeros)
            for out_channel in range(plan.channels):
                sums = add_product(
                    sums,
                    weight_ref[0, channel, out_channel],
                    weight_ref[1, channel, out_channel],
                    grad_ref[out_channel, 0, :, full],
                    grad_ref[out_channel, 1, :, full],
                    True,
                )
            mixed_ref[channel, 0], mixed_ref[channel, 1] = sums
            zeros = jnp.zeros((plan.blocks_z, LANES), jnp.float32)
            sums = (zeros, zeros)
            for group in range(plan.channels // 4):
                sums = add_product(
                    sums,
                    beside_ref[0, channel, group],
                    beside_ref[1, channel, group],
                    grad_beside_ref[group, 0],
                    grad_beside_ref[group, 1],
                    True,
                )
            for which in range(2):
                total = sums[which] + roll_lanes(sums[which], 64)
                tails_ref[channel, which] = total + roll_lanes(total, 32)

    def tail(channel, which):
        return tails_ref[channel, which]

    put_modes(plan, mixed_ref, tail, out_ref, rest_ref)
    leaving.wait()


def weight_grad_kernel(plan, spectrum_ref, grad_ref, before_ref, out_ref, after_ref):
    after_ref[...] = before_ref[...]
    kept = slice(0, plan.pair_rows)
    for channel in range(spectrum_ref.shape[0]):
        for out_channel in range(plan.channels):
            for kz in range(plan.blocks_z):
                row = slice(kz, kz + 1)
                value_re = spectrum_ref[channel, 0, row, kept]
                value_im = spectrum_ref[channel, 1, row, kept]
                grad_re = grad_ref[out_channel, 0, row, kept]
                grad_im = grad_ref[out_channel, 1, row, kept]
                out_ref[channel, out_channel, kz, 0:1, :] = value_re * grad_re + value_im * grad_im
                out_ref[channel, out_channel, kz, 1:2, :] = value_re * grad_im - value_im * grad_re


def weight_grad(plan, spectrum, grad, before):
    own = (plan.blocks_z, 2, plan.pair_rows)
    wide = (plan.blocks_z, 3 * LANES)
    step = 4
    rows, after = pl.pallas_call(
        functools.partial(weight_grad_kernel, plan),
        grid=(plan.channels // step,),
        out_shape=[
            pltpu.HBM((plan.channels, plan.channels) + own, jnp.float32),
            jax.ShapeDtypeStruct(before.shape, before.dtype),
        ],
        in_specs=[
            pl.BlockSpec((step, 2) + wide, lambda at: (at, 0, 0, 0)),
            pl.BlockSpec((plan.channels, 2) + wide, lambda at: (0, 0, 0, 0)),
            pl.BlockSpec(before.shape, lambda at: (0, 0)),
        ],
        out_specs=[
            pl.BlockSpec((step, plan.channels) + own, lambda at: (at, 0, 0, 0, 0)),
            pl.BlockSpec(before.shape, lambda at: (0, 0)),
        ],
        compiler_params=pltpu.CompilerParams(vmem_limit_bytes=VMEM_BYTES),
    )(spectrum, grad, before)
    return jnp.transpose(rows, (3, 0, 1, 2, 4)), after


def plane_synthesis_kernel(
    plan, in_ref, extra_ref, table_ref, out_ref, rows_ref, modes_ref, rest_ref
):
    y_table, x_table = plane_products(table_ref, 2 * plan.full_x, 3 * plan.width_x)
    pad, width = plan.plane_rows, plan.width_y
    lanes = lane_ids(pad)
    for place_x in range(plan.size_x):
        unpack_rest(in_ref[place_x, 4 * pad : 4 * pad + 8, :], rest_ref.at[place_x])
        tiles = []
        for which in range(2):
            row = which * pad
            tiles.append(
                [
                    in_ref[place_x, row : row + pad, :],
                    in_ref[place_x, 2 * pad + row : 3 * pad + row, :],
                    rest_ref[place_x, row : row + pad, :],
                ]
            )
        for inner in range(plan.own_kx):
            first = inner * width
            tile, offset = divmod(first, LANES)
            pieces = []
            for which in range(2):
                piece = roll_lanes(tiles[which][tile], which * HALF - offset)
                if offset + width > LANES:
                    later = roll_lanes(tiles[which][tile + 1], which * HALF - offset)
                    piece = jnp.where(lanes < which * HALF + LANES - offset, piece, later)
                pieces.append(piece)
            merged = jnp.where(lanes < HALF, pieces[0], pieces[1])
            used = jnp.bitwise_and(lanes, HALF - 1) < width
            at = (place_x * plan.own_kx + inner) * pad
            modes_ref[at : at + pad, :] = jnp.where(used, merged, 0.0)
    right = jnp.concatenate(
        [modes_ref[pl.ds(plane, plan.width_x, stride=pad), :] for plane in range(plan.planes)],
        axis=1,
    )
    high, low = split(right)
    both = product(x_table, jnp.concatenate([high, high, low], axis=0))
    sign = jnp.where(lane_ids(plan.full_x) < HALF, -1.0, 1.0)
    for plane in range(plan.planes):
        mine = slice(plane * LANES, (plane + 1) * LANES)
        turned = roll_lanes(both[plan.full_x :, mine], HALF)
        rows_ref[pl.ds(plane, plan.full_x, stride=pad), :] = (
            both[: plan.full_x, mine] + sign * turned
        )
    rows_ref[pl.ds(plan.planes, plan.full_x, stride=pad), :] = jnp.zeros(
        (plan.full_x, LANES), jnp.float32
    )
    cells = along_y(rows_ref[...], y_table)
    size = plan.size_x * pad
    cells = swap_blocks(
        [cells[row * size : (row + 1) * size] for row in range(plan.rows_x)], plan.rows_y
    )
    for place_y in range(plan.size_y):
        for which in range(2):
            out_ref[:, place_y, which] = cells[place_y * 2 + which].reshape(
                plan.size_x, pad, LANES
            )
    spare = extra_ref[0:1, :]
    for place_x in range(plan.size_x):
        for place_y in range(plan.size_y):
            out_ref[place_x, place_y, 0, plan.planes : plan.planes + 1, :] = spare


def widen_map(plan, small, transposed):
    rows = plan.channels * plan.rows_y
    row_ids = lax.broadcasted_iota(jnp.int32, (rows, plan.channels), 0)
    column_ids = lax.broadcasted_iota(jnp.int32, (rows, plan.channels), 1)
    spread = jnp.where(row_ids // plan.rows_y == column_ids, 1.0, 0.0).astype(jnp.bfloat16)
    wide = product(spread, small, ((1,), (0,)) if transposed else ((1,), (1,)))
    wide = product(wide.astype(jnp.bfloat16), spread, NT)
    return jnp.where(same_cell(plan), wide, 0.0).astype(jnp.bfloat16)


def same_cell(plan):
    rows = plan.channels * plan.rows_y
    row_ids = lax.broadcasted_iota(jnp.int32, (rows, rows), 0)
    column_ids = lax.broadcasted_iota(jnp.int32, (rows, rows), 1)
    return jnp.bitwise_and(row_ids, plan.rows_y - 1) == jnp.bitwise_and(
        column_ids, plan.rows_y - 1
    )


def depth_rows(plan, in_ref, rows_ref, channel):
    rows = take_spectrum(plan, in_ref, rows_ref, channel)
    high, low = split(rows)
    return jnp.concatenate([high, high, low], axis=0)


def pointwise_kernel(
    plan, field_ref, map_ref, bias_ref, weight_ref, out_ref, nothing_ref, beside_ref
):
    def beside(channel, carry):
        for which in range(2):
            for group in range(plan.channels // 4):
                parts = [
                    weight_ref[which, channel, group * 4 + slot, :, 2 * LANES :]
                    for slot in range(4)
                ]
                beside_ref[which, channel, group] = jnp.concatenate(
                    [part.astype(jnp.float32) for part in parts], axis=1
                ).astype(jnp.bfloat16)
        return carry

    lax.fori_loop(0, plan.channels, beside, 0)
    nothing_ref[...] = jnp.zeros((8, LANES), jnp.float32)
    rows, size = plan.channels * plan.rows_y, plan.rows_y
    wide = widen_map(plan, map_ref[...], False)

    def one(row, carry):
        here = pl.ds(row, 1)
        mapped = product(wide, field_ref[:, here].reshape(rows, plan.depth))
        for channel in range(plan.channels):
            part = mapped[channel * size : (channel + 1) * size] + bias_ref[channel]
            out_ref[channel, here] = part.reshape(1, size, plan.depth)
        return carry

    lax.fori_loop(0, plan.rows_x, one, 0)


def activation_kernel(
    plan,
    in_ref,
    pointwise_ref,
    cotangent_ref,
    inverse_ref,
    forward_ref,
    output_hbm,
    spectrum_hbm,
    high_hbm,
    low_hbm,
    rows_ref,
    output_ref,
    spectrum_ref,
    high_ref,
    low_ref,
    sent,
):
    pairs = (
        (spectrum_ref, spectrum_hbm, plan.part_z),
        (output_ref, output_hbm, plan.own_c),
        (high_ref, high_hbm, plan.own_c),
        (low_ref, low_hbm, plan.own_c),
    )
    copies = []
    clear_spare(plan, spectrum_ref)
    flat = (plan.cells, plan.depth)
    block = (plan.rows_x, plan.rows_y, plan.depth)
    inverse = inverse_ref[...]
    forward = forward_ref[...]
    scale = math.sqrt(2.0 / math.pi)
    for channel in range(plan.channels):
        if channel % plan.own_c == 0:
            left = [
                depth_rows(plan, in_ref, rows_ref, channel + inner)
                for inner in range(plan.own_c)
            ]
            conv = product(jnp.concatenate(left, axis=1), inverse, TN)
        first = channel % plan.own_c * plan.cells
        preact = conv[first : first + plan.cells] + pointwise_ref[channel].reshape(flat)
        square = preact * preact
        bend = jnp.tanh(preact * (scale + (scale * 0.044715) * square))
        half = 0.5 + 0.5 * bend
        active = preact * half
        output_ref[channel] = active.astype(jnp.bfloat16).reshape(block)
        slope = half + active * (1.0 - half) * (
            2.0 * scale + (6.0 * scale * 0.044715) * square
        )
        grad = cotangent_ref[channel].reshape(flat).astype(jnp.float32) * slope
        high, low = split(grad)
        high_ref[channel] = high.reshape(block)
        low_ref[channel] = low.reshape(block)
        both = product(forward, high, NT)
        more = product(forward[: 2 * MZ], low, NT)
        put_spectrum(plan, spectrum_ref, channel, both[: 2 * MZ] + both[2 * MZ :] + more)
        copies += send_block(plan, channel, pairs, sent)
    for copy in copies:
        copy.wait()


def send_block(plan, channel, pairs, sent):
    block, inner = divmod(channel, plan.own_c)
    if inner < plan.own_c - 1:
        return []
    copies = []
    for at, (held, target, size) in enumerate(pairs):
        mine = pl.ds(block * size, size)
        copies.append(pltpu.make_async_copy(held.at[mine], target.at[mine], sent.at[at, block]))
    for copy in copies:
        copy.start()
    return copies


def pointwise_grad_kernel(
    plan, field_ref, high_ref, low_ref, map_ref, back_ref, sums_ref, cross_ref
):
    rows = plan.channels * plan.rows_y
    wide = widen_map(plan, map_ref[...], True)
    cross_ref[...] = jnp.zeros((rows + 16, rows), jnp.float32)
    ones = jnp.ones((16, plan.depth), jnp.bfloat16)
    slab = (plan.channels, 1, plan.rows_y, plan.depth)

    def one(row, carry):
        here = pl.ds(row, 1)
        values = field_ref[:, here].reshape(rows, plan.depth)
        values = jnp.concatenate([values, ones], axis=0)
        high = high_ref[:, here].reshape(rows, plan.depth)
        low = low_ref[:, here].reshape(rows, plan.depth)
        back_ref[:, here] = (product(wide, high) + product(wide, low)).reshape(slab)
        cross_ref[...] += product(values, high, NT) + product(values, low, NT)
        return carry

    lax.fori_loop(0, plan.rows_x, one, 0)
    row_ids = lax.broadcasted_iota(jnp.int32, (rows, LANES), 0)
    gather = jnp.where(row_ids // plan.rows_y == lane_ids(rows), 1.0, 0.0)
    exact = lax.Precision.HIGHEST
    cross = jnp.where(same_cell(plan), cross_ref[:rows], 0.0)
    by_out = product(cross, gather, precision=exact)
    sums = product(gather, by_out, TN, precision=exact)
    bias_sums = product(cross_ref[rows : rows + 8], gather, precision=exact)
    lanes = lane_ids(1)
    per_row = LANES // SLOT
    for at in range(8):
        packed = jnp.zeros((1, LANES), jnp.float32)
        for slot in range(per_row):
            row = at * per_row + slot
            if row > plan.channels:
                continue
            line = sums[row : row + 1] if row < plan.channels else bias_sums[0:1]
            packed = jnp.where(lanes // SLOT == slot, roll_lanes(line, slot * SLOT), packed)
        sums_ref[at : at + 1, :] = packed


def last_kernel(
    plan,
    in_ref,
    back_ref,
    inverse_ref,
    grad_ref,
    map_grad_ref,
    bias_grad_ref,
    rows_ref,
):
    block = (plan.rows_x, plan.rows_y, plan.depth)
    flat = (plan.cells, plan.depth)
    inverse = inverse_ref[...]
    for channel in range(plan.channels):
        total = product(depth_rows(plan, in_ref, rows_ref, channel), inverse, TN)
        total = total + back_ref[channel].reshape(flat)
        grad_ref[channel] = total.astype(jnp.bfloat16).reshape(block)
    shrink = float(plan.full_x * plan.full_y * plan.depth) ** (-0.5)
    per_row = LANES // SLOT
    for at in range(plan.size_x):
        line = jnp.zeros((1, LANES), jnp.float32)
        for place_y in range(plan.size_y):
            line = line + in_ref[at, place_y, 0, plan.planes : plan.planes + 1, :]
        for slot in range(per_row):
            row = at * per_row + slot
            mine = shrink * roll_lanes(line, -slot * SLOT)[:, : plan.channels]
            if row < plan.channels:
                map_grad_ref[row : row + 1, :] = mine
            elif row == plan.channels:
                bias_grad_ref[...] = mine


def by_planes(plan, field, cotangent, spectral_weight, pointwise_weight, bias):
    pad = plan.plane_rows
    f32 = jnp.float32
    cell_shape = (plan.size_x, plan.size_y, 2, pad, LANES)
    mode_shape = (plan.size_x, 4 * pad + 8, LANES)
    own_shape = (plan.channels, 2, plan.blocks_z, 3 * LANES)
    groups = plan.channels // 4
    beside_shape = (2, plan.channels, groups, plan.blocks_z, LANES)
    grid_shape = field.shape

    def shape(dims, kind=f32):
        return jax.ShapeDtypeStruct(dims, kind)

    def cell_exchange(values):
        flat = values.reshape(plan.devices, 2 * pad, LANES)
        return lax.all_to_all(flat, ("gx", "gy"), 0, 0, tiled=True).reshape(cell_shape)

    def mode_exchange(values):
        return lax.all_to_all(values, "gx", 0, 0, tiled=True)

    z_high, z_low = split_table(plan.z_table(False))
    scaled_high, scaled_low = split_table(plan.z_table(True))
    z_forward = jnp.asarray(np.concatenate([z_high, z_low]))
    z_inverse = jnp.asarray(np.concatenate([z_high, z_low, z_high]))
    scaled_forward = jnp.asarray(np.concatenate([scaled_high, scaled_low]))
    scaled_inverse = jnp.asarray(np.concatenate([scaled_high, scaled_low, scaled_high]))
    forward_table, inverse_table = (jnp.asarray(table) for table in plan.plane_tables())

    lane_rows = pltpu.VMEM((plan.full_x * pad, LANES), f32)
    lane_modes = pltpu.VMEM((plan.width_x * pad, LANES), f32)
    rest = pltpu.VMEM((plan.size_x, 2 * pad, LANES), f32)
    own_full = pltpu.VMEM(own_shape[:3] + (2 * LANES,), f32)
    tails = pltpu.VMEM(own_shape[:3] + (LANES,), f32)
    group_tails = pltpu.VMEM((groups,) + own_shape[1:3] + (LANES,), f32)
    lines = pltpu.VMEM((plan.channels, 2 * MZ, LANES), f32)
    wide = plan.channels * plan.rows_y
    row_shape = shape((8, LANES))

    blocks_sent = pltpu.SemaphoreType.DMA((4, plan.part_c))

    held_weights = [
        pltpu.VMEM(spectral_weight.shape[:4] + (2 * LANES,), spectral_weight.dtype),
        pltpu.VMEM(beside_shape, jnp.bfloat16),
        pltpu.SemaphoreType.DMA((CHUNKS + 1,)),
    ]

    held_grid = pltpu.VMEM(grid_shape, jnp.bfloat16)

    def in_hbm(struct):
        return pltpu.HBM(struct.shape, struct.dtype)

    def with_plan(kernel):
        return functools.partial(kernel, plan)

    def plane_analysis(cells, extra):
        return call(
            with_plan(plane_analysis_kernel),
            shape(mode_shape),
            [lane_rows, lane_modes, rest],
            cells,
            extra,
            forward_table,
        )

    def plane_synthesis(modes, extra):
        return call(
            with_plan(plane_synthesis_kernel),
            shape(cell_shape),
            [lane_rows, lane_modes, rest],
            modes,
            extra,
            inverse_table,
        )

    with jax.named_scope("depth_analysis"):
        cells = call(
            with_plan(depth_analysis_kernel),
            in_hbm(shape(cell_shape)),
            [
                pltpu.VMEM(grid_shape, jnp.bfloat16),
                pltpu.VMEM(z_forward.shape, jnp.bfloat16),
                pltpu.VMEM(cell_shape, f32),
                pltpu.SemaphoreType.DMA((3,)),
                blocks_sent,
            ],
            field,
            z_forward,
            hbm=(0, 1),
            hbm_outs=(0,),
        )
    with jax.named_scope("cells_to_planes"):
        cells = cell_exchange(cells)
    with jax.named_scope("pointwise"):
        weights = with_layout_constraint(spectral_weight, Layout((0, 1, 2, 3, 4)))
        pointwise, nothing, beside = call(
            with_plan(pointwise_kernel),
            [in_hbm(shape(grid_shape)), row_shape, in_hbm(shape(beside_shape, jnp.bfloat16))],
            [],
            field,
            pointwise_weight,
            bias,
            weights,
            smem=(2,),
        )
    with jax.named_scope("plane_analysis"):
        modes = plane_analysis(cells, nothing)
    with jax.named_scope("planes_to_modes"):
        modes = mode_exchange(modes)
    with jax.named_scope("mix"):
        modes, spectrum = call(
            with_plan(mix_kernel),
            [shape(mode_shape), in_hbm(shape(own_shape))],
            [own_full, rest, group_tails]
            + held_weights
            + [pltpu.VMEM(own_shape, f32), pltpu.SemaphoreType.DMA],
            modes,
            weights,
            beside,
            hbm=(1, 2),
            hbm_outs=(1,),
        )
    with jax.named_scope("modes_to_planes"):
        modes = mode_exchange(modes)
    with jax.named_scope("plane_synthesis"):
        cells = plane_synthesis(modes, nothing)
    with jax.named_scope("planes_to_cells"):
        cells = cell_exchange(cells)
    with jax.named_scope("activation"):
        half_grid = shape(grid_shape, jnp.bfloat16)
        output, cells, grad_high, grad_low = call(
            with_plan(activation_kernel),
            [in_hbm(half_grid), in_hbm(shape(cell_shape)), in_hbm(half_grid), in_hbm(half_grid)],
            [lines, held_grid, pltpu.VMEM(cell_shape, f32), held_grid, held_grid, blocks_sent],
            cells,
            pointwise,
            cotangent,
            scaled_inverse,
            scaled_forward,
            hbm_outs=(0, 1, 2, 3),
        )
    with jax.named_scope("grad_cells_to_planes"):
        cells = cell_exchange(cells)
    with jax.named_scope("pointwise_grad"):
        back, sums = call(
            with_plan(pointwise_grad_kernel),
            [in_hbm(shape(grid_shape)), row_shape],
            [pltpu.VMEM((wide + 16, wide), f32)],
            field,
            grad_high,
            grad_low,
            pointwise_weight,
        )
    with jax.named_scope("grad_plane_analysis"):
        modes = plane_analysis(cells, sums)
    with jax.named_scope("grad_planes_to_modes"):
        modes = mode_exchange(modes)
    with jax.named_scope("grad_mix"):
        modes, grad_mix, sums = call(
            with_plan(mix_back_kernel),
            [in_hbm(shape(mode_shape)), in_hbm(shape(own_shape)), row_shape],
            [own_full, rest, tails]
            + held_weights
            + [group_tails, pltpu.VMEM(own_shape, f32), pltpu.SemaphoreType.DMA],
            modes,
            weights,
            beside,
            hbm=(1, 2),
            hbm_outs=(1,),
        )
    with jax.named_scope("grad_modes_to_planes"):
        modes = mode_exchange(modes)
    with jax.named_scope("grad_spectral"):
        grad_spectral, sums = weight_grad(plan, spectrum, grad_mix, sums)
    with jax.named_scope("grad_plane_synthesis"):
        cells = plane_synthesis(modes, sums)
    with jax.named_scope("grad_planes_to_cells"):
        cells = cell_exchange(cells)
    with jax.named_scope("grad_field"):
        channels = plan.channels
        grad_field, map_grad, bias_grad = call(
            with_plan(last_kernel),
            [half_grid, shape((channels, channels)), shape((1, channels))],
            [lines],
            cells,
            back,
            z_inverse,
        )
    return output, grad_field, grad_spectral, map_grad, bias_grad.reshape(channels)


def layer(field, cotangent, spectral_weight, pointwise_weight, bias):
    plan = Plan(
        field.shape, spectral_weight.shape, lax.axis_size("gx"), lax.axis_size("gy")
    )
    if plan.fits:
        return by_planes(plan, field, cotangent, spectral_weight, pointwise_weight, bias)
    return local(field, cotangent, spectral_weight, pointwise_weight, bias)


def solution(mesh):
    placed = (
        P(None, "gx", "gy", None),
        P(None, "gx", "gy", None),
        P(None, None, None, "gy", "gx"),
        P(),
        P(),
    )
    return jax.shard_map(
        layer,
        mesh=mesh,
        in_specs=placed,
        out_specs=(
            P(None, "gx", "gy", None),
            P(None, "gx", "gy", None),
            P(None, None, None, "gy", "gx"),
            P(),
            P(),
        ),
        check_vma=False,
    )
```

```python
import functools
import math

import jax
import jax.numpy as jnp
from jax import lax
import numpy as np
from jax.experimental import pallas as pl
from jax.experimental.layout import Layout, with_layout_constraint
from jax.experimental.pallas import tpu as pltpu
from jax.sharding import PartitionSpec as P

MX = 24
MY = 24
MZ = 24


PRECISE = lax.Precision.HIGHEST
TWO_PI = 2.0 * math.pi


def angles(frequencies, places, length):
    product = places[:, None] * frequencies[None, :] % length
    return product.astype(jnp.float32) * (TWO_PI / length)


def frequency(position, kept_modes, length):
    return jnp.where(position < kept_modes, position, position - 2 * kept_modes + length)


def forward_y(values, phases):
    cosine_table = jnp.cos(phases)
    sine_table = jnp.sin(phases)
    with_cos = jnp.einsum("brcxy,yj->brcxj", values, cosine_table, precision=PRECISE)
    with_sin = jnp.einsum("brcxy,yj->brcxj", values, sine_table, precision=PRECISE)
    real_part = with_cos[:, 0] + with_sin[:, 1]
    imag_part = with_cos[:, 1] - with_sin[:, 0]
    return jnp.stack([real_part, imag_part], axis=1)


def inverse_y(values, phases):
    cosine_table = jnp.cos(phases)
    sine_table = jnp.sin(phases)
    with_cos = jnp.einsum("brcxj,yj->brcxy", values, cosine_table, precision=PRECISE)
    with_sin = jnp.einsum("brcxj,yj->brcxy", values, sine_table, precision=PRECISE)
    real_part = with_cos[:, 0] - with_sin[:, 1]
    imag_part = with_sin[:, 0] + with_cos[:, 1]
    return jnp.stack([real_part, imag_part], axis=1)


def local(field, cotangent, spectral_weight, pointwise_weight, bias):
    channels, rows_x, rows_y, depth_cells = field.shape
    blocks_z = spectral_weight.shape[3]
    pair_rows = spectral_weight.shape[4]
    width_x = 2 * MX
    width_y = 2 * MY
    full_x = rows_x * lax.axis_size("gx")
    full_y = rows_y * lax.axis_size("gy")
    cell_count = float(full_x * full_y * depth_cells)
    place_x = lax.axis_index("gx")
    place_y = lax.axis_index("gy")
    own_x = place_x * rows_x + jnp.arange(rows_x, dtype=jnp.int32)
    freq_x = frequency(jnp.arange(width_x, dtype=jnp.int32), MX, full_x)
    freq_y = frequency(jnp.arange(width_y, dtype=jnp.int32), MY, full_y)
    phases_full_y = angles(freq_y, jnp.arange(full_y, dtype=jnp.int32), full_y)
    z_phases = angles(
        jnp.arange(MZ, dtype=jnp.int32), jnp.arange(depth_cells, dtype=jnp.int32), depth_cells
    )
    table_z = jnp.stack([jnp.cos(z_phases), -jnp.sin(z_phases)], axis=2).reshape(
        depth_cells, 2 * MZ
    )
    kz_own = place_y * blocks_z + jnp.arange(blocks_z, dtype=jnp.int32)
    weight_z = (jnp.where(kz_own == 0, 1.0, 2.0).astype(jnp.float32) / cell_count)[None, :, None]
    own_first = place_x * pair_rows
    flat_width = blocks_z * 2 * channels

    def kx_terms(values, places, first_pair, count):
        kx_count = min(count // width_y + 2, width_x)
        kx_first = jnp.minimum(first_pair // width_y, width_x - kx_count)
        kx_ids = kx_first + jnp.arange(kx_count, dtype=jnp.int32)
        phases = angles(frequency(kx_ids, MX, full_x), places, full_x)
        cosine_table = jnp.cos(phases)
        sine_table = jnp.sin(phases)
        real_part = jnp.einsum(
            "bcxj,xi->ijbc", values[:, 0], cosine_table, precision=PRECISE
        ) + jnp.einsum("bcxj,xi->ijbc", values[:, 1], sine_table, precision=PRECISE)
        imag_part = jnp.einsum(
            "bcxj,xi->ijbc", values[:, 1], cosine_table, precision=PRECISE
        ) - jnp.einsum("bcxj,xi->ijbc", values[:, 0], sine_table, precision=PRECISE)
        terms = jnp.stack([real_part, imag_part], axis=3).reshape(kx_count * width_y, flat_width)
        offset = first_pair - kx_first * width_y
        return lax.dynamic_slice_in_dim(terms, offset, count, 0)

    def analyze(values):
        flat = values.reshape(-1, depth_cells)
        spectra = jnp.einsum("zk,mz->km", table_z, flat, precision=PRECISE).reshape(
            2 * MZ, channels, rows_x, rows_y
        )
        columns = lax.all_to_all(spectra, "gy", split_axis=0, concat_axis=3, tiled=True)
        mode_data = forward_y(columns.reshape(blocks_z, 2, channels, rows_x, full_y), phases_full_y)
        portion = lax.all_gather(mode_data, "gx", axis=3, tiled=True)
        places = jnp.arange(portion.shape[3], dtype=jnp.int32)
        owned = kx_terms(portion, places, own_first, pair_rows)
        return jnp.transpose(owned.reshape(pair_rows, blocks_z, 2, channels), (2, 3, 1, 0))

    def synthesize(spectrum):
        portion = lax.all_gather(spectrum, "gx", axis=3, tiled=True)
        blocks = portion.reshape(2, channels, blocks_z, width_x, width_y)
        phases = angles(freq_x, own_x, full_x)
        cosine_table = jnp.cos(phases)
        sine_table = jnp.sin(phases)
        real_part = jnp.einsum(
            "cbij,xi->bcxj", blocks[0], cosine_table, precision=PRECISE
        ) - jnp.einsum("cbij,xi->bcxj", blocks[1], sine_table, precision=PRECISE)
        imag_part = jnp.einsum(
            "cbij,xi->bcxj", blocks[0], sine_table, precision=PRECISE
        ) + jnp.einsum("cbij,xi->bcxj", blocks[1], cosine_table, precision=PRECISE)
        mode_data = jnp.stack([real_part, imag_part], axis=1)
        fields = inverse_y(mode_data, phases_full_y)
        columns = lax.all_to_all(fields, "gy", split_axis=4, concat_axis=0, tiled=True)
        flat = columns.reshape(2 * MZ, -1)
        return jnp.einsum("km,zk->mz", flat, table_z, precision=PRECISE).reshape(
            channels, rows_x, rows_y, depth_cells
        )

    weights = spectral_weight.astype(jnp.float32)
    widened = field.astype(jnp.float32)
    spec_u = analyze(widened)
    mixed_re = jnp.einsum("cobp,cbp->obp", weights[0], spec_u[0], precision=PRECISE) - jnp.einsum(
        "cobp,cbp->obp", weights[1], spec_u[1], precision=PRECISE
    )
    mixed_im = jnp.einsum("cobp,cbp->obp", weights[0], spec_u[1], precision=PRECISE) + jnp.einsum(
        "cobp,cbp->obp", weights[1], spec_u[0], precision=PRECISE
    )
    mixed_modes = jnp.stack([mixed_re, mixed_im]) * weight_z
    conv = synthesize(mixed_modes)
    pointwise = jnp.dot(
        pointwise_weight.T, field.reshape(channels, -1), preferred_element_type=jnp.float32
    ).reshape(field.shape)
    preact = pointwise + bias[:, None, None, None] + conv
    activated, pullback = jax.vjp(jax.nn.gelu, preact)
    gradient = pullback(cotangent.astype(jnp.float32))[0]
    grad_mix = analyze(gradient) * weight_z
    spec_re = jnp.einsum("cobp,obp->cbp", weights[0], grad_mix[0], precision=PRECISE) + jnp.einsum(
        "cobp,obp->cbp", weights[1], grad_mix[1], precision=PRECISE
    )
    spec_im = jnp.einsum("cobp,obp->cbp", weights[0], grad_mix[1], precision=PRECISE) - jnp.einsum(
        "cobp,obp->cbp", weights[1], grad_mix[0], precision=PRECISE
    )
    grad_spec = jnp.stack([spec_re, spec_im])
    weight_re = jnp.einsum("cbp,obp->cobp", spec_u[0], grad_mix[0], precision=PRECISE) + jnp.einsum(
        "cbp,obp->cobp", spec_u[1], grad_mix[1], precision=PRECISE
    )
    weight_im = jnp.einsum("cbp,obp->cobp", spec_u[0], grad_mix[1], precision=PRECISE) - jnp.einsum(
        "cbp,obp->cobp", spec_u[1], grad_mix[0], precision=PRECISE
    )
    grad_spectral = jnp.stack([weight_re, weight_im])
    returned = synthesize(grad_spec)
    grad_flat = gradient.reshape(channels, -1)
    back_point = jnp.dot(
        pointwise_weight.astype(jnp.float32), grad_flat, precision=PRECISE
    ).reshape(field.shape)
    grad_field = (back_point + returned).astype(jnp.bfloat16)
    local_weight = jnp.dot(widened.reshape(channels, -1), grad_flat.T, precision=PRECISE)
    local_bias = jnp.sum(grad_flat, axis=1)
    summed_weight, summed_bias = lax.psum((local_weight, local_bias), ("gx", "gy"))
    shrink = cell_count ** (-0.5)
    return (
        activated.astype(jnp.bfloat16),
        grad_field,
        grad_spectral,
        summed_weight * shrink,
        summed_bias * shrink,
    )


LANES = 128
HALF = 64
SLOT = 32
CHUNKS = 5
VMEM_BYTES = 20 * 1024 * 1024


def split_table(table):
    high = table.astype(jnp.bfloat16)
    low = (table - high.astype(np.float64)).astype(jnp.bfloat16)
    return high, low


def frequency_table(kept_modes, length):
    position = np.arange(2 * kept_modes)
    return np.where(position < kept_modes, position, position - 2 * kept_modes + length)


def phase_table(frequencies, places, length):
    product = places[:, None] * frequencies[None, :] % length
    return product.astype(np.float64) * (TWO_PI / length)


def split(values):
    high = values.astype(jnp.bfloat16)
    low = (values - high.astype(jnp.float32)).astype(jnp.bfloat16)
    return high, low


def product(left, right, contract=((1,), (0,)), precision=None):
    return lax.dot_general(
        left, right, (contract, ((), ())), preferred_element_type=jnp.float32, precision=precision
    )


NT = ((1,), (1,))
TN = ((0,), (0,))


def lane_ids(rows):
    return lax.broadcasted_iota(jnp.int32, (rows, LANES), 1)


def roll_lanes(values, shift):
    shift = shift % LANES
    if shift == 0:
        return values
    return pltpu.roll(values, shift, 1)


class Plan:
    def __init__(self, field_shape, weight_shape, size_x, size_y):
        self.channels, self.rows_x, self.rows_y, self.depth = field_shape
        self.size_x, self.size_y = size_x, size_y
        self.blocks_z = weight_shape[3]
        self.pair_rows = weight_shape[4]
        self.full_x = self.rows_x * size_x
        self.full_y = self.rows_y * size_y
        self.width_x, self.width_y = 2 * MX, 2 * MY
        self.cells = self.rows_x * self.rows_y
        self.part_c, self.part_z = 0, 0
        for part_z in range(1, self.blocks_z + 1):
            part_c = size_x // part_z
            if size_x % part_z or self.blocks_z % part_z or self.channels % part_c:
                continue
            self.part_c, self.part_z = part_c, part_z
        self.fits = False
        if self.part_c == 0:
            return
        self.own_c = self.channels // self.part_c
        self.own_z = self.blocks_z // self.part_z
        self.planes = self.own_c * self.own_z
        self.plane_rows = 16
        self.own_kx = self.pair_rows // self.width_y
        self.devices = size_x * size_y
        self.fits = (
            self.cells == LANES
            and self.rows_y == 16
            and self.size_y * 2 == self.rows_x
            and self.depth % LANES == 0
            and self.planes < self.plane_rows
            and self.pair_rows % self.width_y == 0
            and self.pair_rows == 2 * LANES + 32
            and self.width_y <= HALF
            and 3 * max(self.full_x, self.width_x) <= 2 * LANES
            and size_x == 8
            and self.channels % CHUNKS == 0
            and self.channels % 4 == 0
            and self.channels <= SLOT
            and self.channels < size_x * (LANES // SLOT)
            and self.own_z * 2 * self.part_z * size_y == 2 * MZ
        )

    def z_table(self, scaled):
        kz = np.arange(MZ)
        phases = phase_table(kz, np.arange(self.depth), self.depth)
        both = np.stack([np.cos(phases), -np.sin(phases)])
        if scaled:
            cells = float(self.full_x * self.full_y * self.depth)
            both = both * (np.where(kz == 0, 1.0, 2.0) / cells)
        both = both.reshape(2, self.depth, self.size_y, self.part_z, self.own_z)
        return both.transpose(2, 3, 0, 4, 1).reshape(2 * MZ, self.depth)

    def y_tables(self):
        freq = frequency_table(MY, self.full_y)
        phases = phase_table(freq, np.arange(self.full_y), self.full_y)
        cosine, sine = np.cos(phases), np.sin(phases)
        one = np.zeros((self.size_y, 2, self.rows_y, 2, HALF))
        by_block = (self.size_y, self.rows_y, self.width_y)
        one[:, 0, :, 0, : self.width_y] = cosine.reshape(by_block)
        one[:, 1, :, 0, : self.width_y] = sine.reshape(by_block)
        one[:, 0, :, 1, : self.width_y] = -sine.reshape(by_block)
        one[:, 1, :, 1, : self.width_y] = cosine.reshape(by_block)
        one = one.reshape(LANES, LANES)
        tables = []
        for table in (one, one.T):
            high, low = split_table(table)
            top = np.concatenate([high, low], axis=1)
            bottom = np.concatenate([high, np.zeros_like(low)], axis=1)
            tables.append(np.concatenate([top, bottom], axis=0))
        return tables

    def x_tables(self):
        freq = frequency_table(MX, self.full_x)
        phases = phase_table(freq, np.arange(self.full_x), self.full_x)
        phases = phases.reshape(self.size_x, self.rows_x, self.width_x).transpose(1, 0, 2)
        phases = phases.reshape(self.full_x, self.width_x)
        cosine, sine = np.cos(phases), np.sin(phases)
        forward = np.concatenate([cosine.T, sine.T], axis=0)
        inverse = np.concatenate([cosine, sine], axis=0)
        tables = []
        for table in (forward, inverse):
            high, low = split_table(table)
            tables.append(np.concatenate([high, low, high], axis=1))
        return tables

    def plane_tables(self):
        tables = []
        for along_y, along_x in zip(self.y_tables(), self.x_tables()):
            rows, columns = along_x.shape
            spare = ((0, -rows % 16), (0, 2 * LANES - columns))
            tables.append(np.concatenate([along_y, np.pad(along_x, spare)], axis=0))
        return tables


def plane_products(table_ref, rows, columns):
    across = 2 * LANES
    return table_ref[:across], table_ref[across : across + rows, :columns]


def call(kernel, out_shape, scratch, *operands, smem=(), hbm=(), hbm_outs=()):
    operands = [
        pltpu.with_memory_space_constraint(operand, pltpu.HBM) if at in hbm else operand
        for at, operand in enumerate(operands)
    ]
    specs = []
    for at in range(len(operands)):
        space = pltpu.SMEM if at in smem else pltpu.HBM if at in hbm else pltpu.VMEM
        specs.append(pl.BlockSpec(memory_space=space))
    single = not isinstance(out_shape, (tuple, list))
    shapes = [out_shape] if single else out_shape
    outs = [
        pl.BlockSpec(memory_space=pltpu.HBM if at in hbm_outs else pltpu.VMEM)
        for at in range(len(shapes))
    ]
    return pl.pallas_call(
        kernel,
        out_shape=out_shape,
        in_specs=specs,
        out_specs=outs[0] if single else outs,
        scratch_shapes=scratch,
        compiler_params=pltpu.CompilerParams(vmem_limit_bytes=VMEM_BYTES),
    )(*operands)


def put_spectrum(plan, out_ref, channel, rows):
    block, inner = divmod(channel, plan.own_c)
    size = plan.own_z
    at = 0
    for place_y in range(plan.size_y):
        for part in range(plan.part_z):
            place_x = block * plan.part_z + part
            for which in range(2):
                out_ref[place_x, place_y, which, inner * size : (inner + 1) * size, :] = rows[
                    at : at + size
                ]
                at += size


def take_spectrum(plan, in_ref, rows_ref, channel):
    block, inner = divmod(channel, plan.own_c)
    size = plan.own_z
    at = 0
    for place_y in range(plan.size_y):
        for part in range(plan.part_z):
            place_x = block * plan.part_z + part
            for which in range(2):
                rows_ref[channel, at : at + size, :] = in_ref[
                    place_x, place_y, which, inner * size : (inner + 1) * size, :
                ]
                at += size
    return rows_ref[channel]


def clear_spare(plan, out_ref):
    zeros = jnp.zeros((plan.plane_rows - plan.planes, LANES), jnp.float32)
    for place_x in range(plan.size_x):
        for place_y in range(plan.size_y):
            for which in range(2):
                out_ref[place_x, place_y, which, plan.planes :, :] = zeros


def depth_analysis_kernel(
    plan, field_ref, table_ref, out_hbm, blocks_ref, held_ref, out_ref, arrived, sent
):
    copies = [pltpu.make_async_copy(table_ref, held_ref, arrived.at[2])]
    size = plan.channels // 2
    for part in range(2):
        mine = pl.ds(part * size, size)
        copies.append(
            pltpu.make_async_copy(field_ref.at[mine], blocks_ref.at[mine], arrived.at[part])
        )
    for copy in copies:
        copy.start()
    clear_spare(plan, out_ref)
    leaving = []
    copies[0].wait()
    table = held_ref[...]
    for channel in range(plan.channels):
        if channel % size == 0:
            copies[1 + channel // size].wait()
        block = blocks_ref[channel].reshape(plan.cells, plan.depth)
        both = product(table, block, NT)
        put_spectrum(plan, out_ref, channel, both[: 2 * MZ] + both[2 * MZ :])
        leaving += send_block(plan, channel, ((out_ref, out_hbm, plan.part_z),), sent)
    for copy in leaving:
        copy.wait()


def swap_blocks(values, block):
    values = list(values)
    lanes = lane_ids(values[0].shape[0])
    step = 1
    while step < len(values):
        low = jnp.bitwise_and(lanes, step * block) == 0
        for at in range(len(values)):
            if at & step:
                continue
            first, second = values[at], values[at + step]
            values[at] = jnp.where(low, first, roll_lanes(second, step * block))
            values[at + step] = jnp.where(low, roll_lanes(first, -step * block), second)
        step *= 2
    return values


def along_y(values, table):
    high, low = split(values)
    both = product(jnp.concatenate([high, low], axis=1), table)
    return both[:, :LANES] + both[:, LANES:]


def plane_analysis_kernel(
    plan, in_ref, extra_ref, table_ref, out_ref, rows_ref, modes_ref, rest_ref
):
    y_table, x_table = plane_products(table_ref, 2 * plan.width_x, 3 * plan.full_x)
    pad = plan.plane_rows
    left = [
        in_ref[:, place_y, which].reshape(plan.size_x * pad, LANES)
        for place_y in range(plan.size_y)
        for which in range(2)
    ]
    rows_ref[...] = along_y(
        jnp.concatenate(swap_blocks(left, plan.rows_y), axis=0), y_table
    )
    right = jnp.concatenate(
        [rows_ref[pl.ds(plane, plan.full_x, stride=pad), :] for plane in range(plan.planes)], axis=1
    )
    high, low = split(right)
    both = product(x_table, jnp.concatenate([high, high, low], axis=0))
    sign = jnp.where(lane_ids(plan.width_x) < HALF, 1.0, -1.0)
    for plane in range(plan.planes):
        mine = slice(plane * LANES, (plane + 1) * LANES)
        turned = roll_lanes(both[plan.width_x :, mine], HALF)
        modes_ref[pl.ds(plane, plan.width_x, stride=pad), :] = (
            both[: plan.width_x, mine] + sign * turned
        )
    modes_ref[pl.ds(plan.planes, plan.width_x, stride=pad), :] = jnp.zeros(
        (plan.width_x, LANES), jnp.float32
    )
    lanes = lane_ids(pad)
    width = plan.width_y
    for place_x in range(plan.size_x):
        for which in range(2):
            tiles = [None, None, None]
            for inner in range(plan.own_kx):
                kx = place_x * plan.own_kx + inner
                first = inner * width
                turned = roll_lanes(modes_ref[kx * pad : (kx + 1) * pad, :], first - which * HALF)
                tile, offset = divmod(first, LANES)
                for at in (tile, tile + 1):
                    begin = first - at * LANES
                    if begin >= LANES or begin + width <= 0:
                        continue
                    if tiles[at] is None:
                        tiles[at] = turned
                    else:
                        tiles[at] = jnp.where(lanes < begin, tiles[at], turned)
            for at in range(2):
                row = at * 2 * pad + which * pad
                out_ref[place_x, row : row + pad, :] = tiles[at]
            rest_ref[place_x, which * pad : (which + 1) * pad, :] = tiles[2]
        out_ref[place_x, 4 * pad : 4 * pad + 8, :] = pack_rest(rest_ref.at[place_x])
        out_ref[place_x, plan.planes : plan.planes + 1, :] = extra_ref[place_x : place_x + 1, :]


def pack_rest(rest_ref):
    lanes = lane_ids(8)
    packed = rest_ref[0:8, :]
    for group in range(1, 4):
        turned = roll_lanes(rest_ref[group * 8 : (group + 1) * 8, :], group * 32)
        packed = jnp.where(lanes < group * 32, packed, turned)
    return packed


def unpack_rest(packed, rest_ref, repeated=False):
    lanes = lane_ids(8)
    for group in range(4):
        turned = roll_lanes(packed, -group * 32)
        if repeated:
            turned = jnp.where(lanes < 32, turned, roll_lanes(turned, 32))
            turned = jnp.where(lanes < 64, turned, roll_lanes(turned, 64))
        rest_ref[group * 8 : (group + 1) * 8, :] = turned


def take_modes(plan, in_ref, modes_ref, rest_ref, beside_ref=None):
    pad, size = plan.plane_rows, plan.own_z
    for place_x in range(plan.size_x):
        block, part = divmod(place_x, plan.part_z)
        unpack_rest(in_ref[place_x, 4 * pad : 4 * pad + 8, :], rest_ref.at[place_x], True)
        for which in range(2):
            for inner in range(plan.own_c):
                channel = block * plan.own_c + inner
                row = which * pad + inner * size
                kz = slice(part * size, (part + 1) * size)
                for at in range(2):
                    begin = at * 2 * pad + row
                    modes_ref[channel, which, kz, at * LANES : (at + 1) * LANES] = in_ref[
                        place_x, begin : begin + size, :
                    ]
                modes_ref[channel, which, kz, 2 * LANES :] = rest_ref[place_x, row : row + size, :]
                if beside_ref is not None:
                    group, slot = divmod(channel, 4)
                    mine = slice(slot * 32, (slot + 1) * 32)
                    beside_ref[group, which, kz, mine] = rest_ref[place_x, row : row + size, mine]


def put_modes(plan, modes_ref, tail, out_ref, rest_ref):
    pad, size = plan.plane_rows, plan.own_z
    zeros = jnp.zeros((pad - plan.planes, LANES), jnp.float32)
    rest_ref[...] = jnp.zeros(rest_ref.shape, jnp.float32)
    for place_x in range(plan.size_x):
        block, part = divmod(place_x, plan.part_z)
        for which in range(2):
            for inner in range(plan.own_c):
                channel = block * plan.own_c + inner
                row = which * pad + inner * size
                kz = slice(part * size, (part + 1) * size)
                for at in range(2):
                    begin = at * 2 * pad + row
                    out_ref[place_x, begin : begin + size, :] = modes_ref[
                        channel, which, kz, at * LANES : (at + 1) * LANES
                    ]
                rest_ref[place_x, row : row + size, 0:32] = tail(channel, which)[kz, 0:32]
            for at in range(2):
                begin = at * 2 * pad + which * pad + plan.planes
                out_ref[place_x, begin : begin + pad - plan.planes, :] = zeros
        out_ref[place_x, 4 * pad : 4 * pad + 8, :] = pack_rest(rest_ref.at[place_x])


def bring_weights(plan, weight_hbm, weight_ref, beside_hbm, beside_ref, arrived, by_input):
    full = pl.ds(0, 2 * LANES)
    size = plan.channels // CHUNKS
    copies = [pltpu.make_async_copy(beside_hbm, beside_ref, arrived.at[CHUNKS])]
    for chunk in range(CHUNKS):
        mine = pl.ds(chunk * size, size)
        whole = slice(None)
        source = (whole, mine) if by_input else (whole, whole, mine)
        source = source + (whole,) * (4 - len(source)) + (full,)
        target = source[:4]
        copies.append(
            pltpu.make_async_copy(weight_hbm.at[source], weight_ref.at[target], arrived.at[chunk])
        )
    for copy in copies:
        copy.start()
    return copies


def add_product(sums, weight_re, weight_im, value_re, value_im, back):
    weight_re = weight_re.astype(jnp.float32)
    weight_im = weight_im.astype(jnp.float32)
    if back:
        return (
            sums[0] + (weight_re * value_re + weight_im * value_im),
            sums[1] + (weight_re * value_im - weight_im * value_re),
        )
    return (
        sums[0] + (weight_re * value_re - weight_im * value_im),
        sums[1] + (weight_re * value_im + weight_im * value_re),
    )


def mix_kernel(
    plan,
    in_ref,
    weight_hbm,
    beside_hbm,
    out_ref,
    spectrum_hbm,
    mixed_ref,
    rest_ref,
    tails_ref,
    weight_ref,
    beside_ref,
    arrived,
    spectrum_ref,
    sent,
):
    copies = bring_weights(plan, weight_hbm, weight_ref, beside_hbm, beside_ref, arrived, False)
    take_modes(plan, in_ref, spectrum_ref, rest_ref)
    leaving = pltpu.make_async_copy(spectrum_ref, spectrum_hbm, sent)
    leaving.start()
    full, end = slice(0, 2 * LANES), slice(2 * LANES, 3 * LANES)
    size = plan.channels // CHUNKS
    copies[0].wait()
    for chunk, copy in enumerate(copies[1:]):
        copy.wait()
        for out_channel in range(chunk * size, (chunk + 1) * size):
            zeros = jnp.zeros((plan.blocks_z, 2 * LANES), jnp.float32)
            sums = (zeros, zeros)
            for channel in range(plan.channels):
                sums = add_product(
                    sums,
                    weight_ref[0, channel, out_channel],
                    weight_ref[1, channel, out_channel],
                    spectrum_ref[channel, 0, :, full],
                    spectrum_ref[channel, 1, :, full],
                    False,
                )
            mixed_ref[out_channel, 0], mixed_ref[out_channel, 1] = sums
    for group in range(plan.channels // 4):
        zeros = jnp.zeros((plan.blocks_z, LANES), jnp.float32)
        sums = (zeros, zeros)
        for channel in range(plan.channels):
            sums = add_product(
                sums,
                beside_ref[0, channel, group],
                beside_ref[1, channel, group],
                spectrum_ref[channel, 0, :, end],
                spectrum_ref[channel, 1, :, end],
                False,
            )
        tails_ref[group, 0], tails_ref[group, 1] = sums

    def tail(channel, which):
        group, slot = divmod(channel, 4)
        return roll_lanes(tails_ref[group, which], -slot * 32)

    put_modes(plan, mixed_ref, tail, out_ref, rest_ref)
    leaving.wait()


def mix_back_kernel(
    plan,
    in_ref,
    weight_hbm,
    beside_hbm,
    out_ref,
    grad_hbm,
    sums_ref,
    mixed_ref,
    rest_ref,
    tails_ref,
    weight_ref,
    beside_ref,
    arrived,
    grad_beside_ref,
    grad_ref,
    sent,
):
    copies = bring_weights(plan, weight_hbm, weight_ref, beside_hbm, beside_ref, arrived, True)
    spare = jnp.zeros((1, LANES), jnp.float32)
    for place_x in range(plan.size_x):
        spare = spare + in_ref[place_x, plan.planes : plan.planes + 1, :]
    sums_ref[...] = jnp.broadcast_to(spare, (8, LANES))
    take_modes(plan, in_ref, grad_ref, rest_ref, grad_beside_ref)
    leaving = pltpu.make_async_copy(grad_ref, grad_hbm, sent)
    leaving.start()
    full = slice(0, 2 * LANES)
    size = plan.channels // CHUNKS
    copies[0].wait()
    for chunk, copy in enumerate(copies[1:]):
        copy.wait()
        for channel in range(chunk * size, (chunk + 1) * size):
            zeros = jnp.zeros((plan.blocks_z, 2 * LANES), jnp.float32)
            sums = (zeros, zeros)
            for out_channel in range(plan.channels):
                sums = add_product(
                    sums,
                    weight_ref[0, channel, out_channel],
                    weight_ref[1, channel, out_channel],
                    grad_ref[out_channel, 0, :, full],
                    grad_ref[out_channel, 1, :, full],
                    True,
                )
            mixed_ref[channel, 0], mixed_ref[channel, 1] = sums
            zeros = jnp.zeros((plan.blocks_z, LANES), jnp.float32)
            sums = (zeros, zeros)
            for group in range(plan.channels // 4):
                sums = add_product(
                    sums,
                    beside_ref[0, channel, group],
                    beside_ref[1, channel, group],
                    grad_beside_ref[group, 0],
                    grad_beside_ref[group, 1],
                    True,
                )
            for which in range(2):
                total = sums[which] + roll_lanes(sums[which], 64)
                tails_ref[channel, which] = total + roll_lanes(total, 32)

    def tail(channel, which):
        return tails_ref[channel, which]

    put_modes(plan, mixed_ref, tail, out_ref, rest_ref)
    leaving.wait()


def weight_grad_kernel(plan, spectrum_ref, grad_ref, before_ref, out_ref, after_ref):
    after_ref[...] = before_ref[...]
    kept = slice(0, plan.pair_rows)
    for channel in range(spectrum_ref.shape[0]):
        for out_channel in range(plan.channels):
            for kz in range(plan.blocks_z):
                row = slice(kz, kz + 1)
                value_re = spectrum_ref[channel, 0, row, kept]
                value_im = spectrum_ref[channel, 1, row, kept]
                grad_re = grad_ref[out_channel, 0, row, kept]
                grad_im = grad_ref[out_channel, 1, row, kept]
                out_ref[channel, out_channel, kz, 0:1, :] = value_re * grad_re + value_im * grad_im
                out_ref[channel, out_channel, kz, 1:2, :] = value_re * grad_im - value_im * grad_re


def weight_grad(plan, spectrum, grad, before):
    own = (plan.blocks_z, 2, plan.pair_rows)
    wide = (plan.blocks_z, 3 * LANES)
    step = 4
    rows, after = pl.pallas_call(
        functools.partial(weight_grad_kernel, plan),
        grid=(plan.channels // step,),
        out_shape=[
            pltpu.HBM((plan.channels, plan.channels) + own, jnp.float32),
            jax.ShapeDtypeStruct(before.shape, before.dtype),
        ],
        in_specs=[
            pl.BlockSpec((step, 2) + wide, lambda at: (at, 0, 0, 0)),
            pl.BlockSpec((plan.channels, 2) + wide, lambda at: (0, 0, 0, 0)),
            pl.BlockSpec(before.shape, lambda at: (0, 0)),
        ],
        out_specs=[
            pl.BlockSpec((step, plan.channels) + own, lambda at: (at, 0, 0, 0, 0)),
            pl.BlockSpec(before.shape, lambda at: (0, 0)),
        ],
        compiler_params=pltpu.CompilerParams(vmem_limit_bytes=VMEM_BYTES),
    )(
        pltpu.with_memory_space_constraint(spectrum, pltpu.HBM),
        pltpu.with_memory_space_constraint(grad, pltpu.HBM),
        before,
    )
    return jnp.transpose(rows, (3, 0, 1, 2, 4)), after


def plane_synthesis_kernel(
    plan, in_ref, extra_ref, table_ref, out_ref, rows_ref, modes_ref, rest_ref
):
    y_table, x_table = plane_products(table_ref, 2 * plan.full_x, 3 * plan.width_x)
    pad, width = plan.plane_rows, plan.width_y
    lanes = lane_ids(pad)
    for place_x in range(plan.size_x):
        unpack_rest(in_ref[place_x, 4 * pad : 4 * pad + 8, :], rest_ref.at[place_x])
        tiles = []
        for which in range(2):
            row = which * pad
            tiles.append(
                [
                    in_ref[place_x, row : row + pad, :],
                    in_ref[place_x, 2 * pad + row : 3 * pad + row, :],
                    rest_ref[place_x, row : row + pad, :],
                ]
            )
        for inner in range(plan.own_kx):
            first = inner * width
            tile, offset = divmod(first, LANES)
            pieces = []
            for which in range(2):
                piece = roll_lanes(tiles[which][tile], which * HALF - offset)
                if offset + width > LANES:
                    later = roll_lanes(tiles[which][tile + 1], which * HALF - offset)
                    piece = jnp.where(lanes < which * HALF + LANES - offset, piece, later)
                pieces.append(piece)
            merged = jnp.where(lanes < HALF, pieces[0], pieces[1])
            used = jnp.bitwise_and(lanes, HALF - 1) < width
            at = (place_x * plan.own_kx + inner) * pad
            modes_ref[at : at + pad, :] = jnp.where(used, merged, 0.0)
    right = jnp.concatenate(
        [modes_ref[pl.ds(plane, plan.width_x, stride=pad), :] for plane in range(plan.planes)],
        axis=1,
    )
    high, low = split(right)
    both = product(x_table, jnp.concatenate([high, high, low], axis=0))
    sign = jnp.where(lane_ids(plan.full_x) < HALF, -1.0, 1.0)
    for plane in range(plan.planes):
        mine = slice(plane * LANES, (plane + 1) * LANES)
        turned = roll_lanes(both[plan.full_x :, mine], HALF)
        rows_ref[pl.ds(plane, plan.full_x, stride=pad), :] = (
            both[: plan.full_x, mine] + sign * turned
        )
    rows_ref[pl.ds(plan.planes, plan.full_x, stride=pad), :] = jnp.zeros(
        (plan.full_x, LANES), jnp.float32
    )
    cells = along_y(rows_ref[...], y_table)
    size = plan.size_x * pad
    cells = swap_blocks(
        [cells[row * size : (row + 1) * size] for row in range(plan.rows_x)], plan.rows_y
    )
    for place_y in range(plan.size_y):
        for which in range(2):
            out_ref[:, place_y, which] = cells[place_y * 2 + which].reshape(
                plan.size_x, pad, LANES
            )
    spare = extra_ref[0:1, :]
    for place_x in range(plan.size_x):
        for place_y in range(plan.size_y):
            out_ref[place_x, place_y, 0, plan.planes : plan.planes + 1, :] = spare


def widen_map(plan, small, transposed):
    rows = plan.channels * plan.rows_y
    row_ids = lax.broadcasted_iota(jnp.int32, (rows, plan.channels), 0)
    column_ids = lax.broadcasted_iota(jnp.int32, (rows, plan.channels), 1)
    spread = jnp.where(row_ids // plan.rows_y == column_ids, 1.0, 0.0).astype(jnp.bfloat16)
    wide = product(spread, small, ((1,), (0,)) if transposed else ((1,), (1,)))
    wide = product(wide.astype(jnp.bfloat16), spread, NT)
    return jnp.where(same_cell(plan), wide, 0.0).astype(jnp.bfloat16)


def same_cell(plan):
    rows = plan.channels * plan.rows_y
    row_ids = lax.broadcasted_iota(jnp.int32, (rows, rows), 0)
    column_ids = lax.broadcasted_iota(jnp.int32, (rows, rows), 1)
    return jnp.bitwise_and(row_ids, plan.rows_y - 1) == jnp.bitwise_and(
        column_ids, plan.rows_y - 1
    )


def depth_rows(plan, in_ref, rows_ref, channel):
    rows = take_spectrum(plan, in_ref, rows_ref, channel)
    high, low = split(rows)
    return jnp.concatenate([high, high, low], axis=0)


def pointwise_kernel(
    plan, field_ref, map_ref, bias_ref, weight_ref, out_ref, nothing_ref, beside_ref
):
    def beside(channel, carry):
        for which in range(2):
            for group in range(plan.channels // 4):
                parts = [
                    weight_ref[which, channel, group * 4 + slot, :, 2 * LANES :]
                    for slot in range(4)
                ]
                beside_ref[which, channel, group] = jnp.concatenate(
                    [part.astype(jnp.float32) for part in parts], axis=1
                ).astype(jnp.bfloat16)
        return carry

    lax.fori_loop(0, plan.channels, beside, 0)
    nothing_ref[...] = jnp.zeros((8, LANES), jnp.float32)
    rows, size = plan.channels * plan.rows_y, plan.rows_y
    wide = widen_map(plan, map_ref[...], False)

    def one(row, carry):
        here = pl.ds(row, 1)
        mapped = product(wide, field_ref[:, here].reshape(rows, plan.depth))
        for channel in range(plan.channels):
            part = mapped[channel * size : (channel + 1) * size] + bias_ref[channel]
            out_ref[channel, here] = part.reshape(1, size, plan.depth)
        return carry

    lax.fori_loop(0, plan.rows_x, one, 0)


def activation_kernel(
    plan,
    in_ref,
    pointwise_ref,
    cotangent_ref,
    inverse_ref,
    forward_ref,
    output_hbm,
    spectrum_hbm,
    high_hbm,
    low_hbm,
    rows_ref,
    output_ref,
    spectrum_ref,
    high_ref,
    low_ref,
    sent,
):
    pairs = (
        (spectrum_ref, spectrum_hbm, plan.part_z),
        (output_ref, output_hbm, plan.own_c),
        (high_ref, high_hbm, plan.own_c),
        (low_ref, low_hbm, plan.own_c),
    )
    copies = []
    clear_spare(plan, spectrum_ref)
    flat = (plan.cells, plan.depth)
    block = (plan.rows_x, plan.rows_y, plan.depth)
    inverse = inverse_ref[...]
    forward = forward_ref[...]
    scale = math.sqrt(2.0 / math.pi)
    for channel in range(plan.channels):
        if channel % plan.own_c == 0:
            left = [
                depth_rows(plan, in_ref, rows_ref, channel + inner)
                for inner in range(plan.own_c)
            ]
            conv = product(jnp.concatenate(left, axis=1), inverse, TN)
        first = channel % plan.own_c * plan.cells
        preact = conv[first : first + plan.cells] + pointwise_ref[channel].reshape(flat)
        square = preact * preact
        bend = jnp.tanh(preact * (scale + (scale * 0.044715) * square))
        half = 0.5 + 0.5 * bend
        active = preact * half
        output_ref[channel] = active.astype(jnp.bfloat16).reshape(block)
        slope = half + active * (1.0 - half) * (
            2.0 * scale + (6.0 * scale * 0.044715) * square
        )
        grad = cotangent_ref[channel].reshape(flat).astype(jnp.float32) * slope
        high, low = split(grad)
        high_ref[channel] = high.reshape(block)
        low_ref[channel] = low.reshape(block)
        both = product(forward, high, NT)
        more = product(forward[: 2 * MZ], low, NT)
        put_spectrum(plan, spectrum_ref, channel, both[: 2 * MZ] + both[2 * MZ :] + more)
        copies += send_block(plan, channel, pairs, sent)
    for copy in copies:
        copy.wait()


def send_block(plan, channel, pairs, sent):
    block, inner = divmod(channel, plan.own_c)
    if inner < plan.own_c - 1:
        return []
    copies = []
    for at, (held, target, size) in enumerate(pairs):
        mine = pl.ds(block * size, size)
        copies.append(pltpu.make_async_copy(held.at[mine], target.at[mine], sent.at[at, block]))
    for copy in copies:
        copy.start()
    return copies


def pointwise_grad_kernel(
    plan, field_ref, high_ref, low_ref, map_ref, back_ref, sums_ref, cross_ref
):
    rows = plan.channels * plan.rows_y
    wide = widen_map(plan, map_ref[...], True)
    cross_ref[...] = jnp.zeros((rows + 16, rows), jnp.float32)
    ones = jnp.ones((16, plan.depth), jnp.bfloat16)
    slab = (plan.channels, 1, plan.rows_y, plan.depth)

    def one(row, carry):
        here = pl.ds(row, 1)
        values = field_ref[:, here].reshape(rows, plan.depth)
        values = jnp.concatenate([values, ones], axis=0)
        high = high_ref[:, here].reshape(rows, plan.depth)
        low = low_ref[:, here].reshape(rows, plan.depth)
        back_ref[:, here] = (product(wide, high) + product(wide, low)).reshape(slab)
        cross_ref[...] += product(values, high, NT) + product(values, low, NT)
        return carry

    lax.fori_loop(0, plan.rows_x, one, 0)
    row_ids = lax.broadcasted_iota(jnp.int32, (rows, LANES), 0)
    gather = jnp.where(row_ids // plan.rows_y == lane_ids(rows), 1.0, 0.0)
    exact = lax.Precision.HIGHEST
    cross = jnp.where(same_cell(plan), cross_ref[:rows], 0.0)
    by_out = product(cross, gather, precision=exact)
    sums = product(gather, by_out, TN, precision=exact)
    bias_sums = product(cross_ref[rows : rows + 8], gather, precision=exact)
    lanes = lane_ids(1)
    per_row = LANES // SLOT
    for at in range(8):
        packed = jnp.zeros((1, LANES), jnp.float32)
        for slot in range(per_row):
            row = at * per_row + slot
            if row > plan.channels:
                continue
            line = sums[row : row + 1] if row < plan.channels else bias_sums[0:1]
            packed = jnp.where(lanes // SLOT == slot, roll_lanes(line, slot * SLOT), packed)
        sums_ref[at : at + 1, :] = packed


def last_kernel(
    plan,
    in_ref,
    back_ref,
    inverse_ref,
    grad_ref,
    map_grad_ref,
    bias_grad_ref,
    rows_ref,
):
    block = (plan.rows_x, plan.rows_y, plan.depth)
    flat = (plan.cells, plan.depth)
    inverse = inverse_ref[...]
    for channel in range(plan.channels):
        total = product(depth_rows(plan, in_ref, rows_ref, channel), inverse, TN)
        total = total + back_ref[channel].reshape(flat)
        grad_ref[channel] = total.astype(jnp.bfloat16).reshape(block)
    shrink = float(plan.full_x * plan.full_y * plan.depth) ** (-0.5)
    per_row = LANES // SLOT
    for at in range(plan.size_x):
        line = jnp.zeros((1, LANES), jnp.float32)
        for place_y in range(plan.size_y):
            line = line + in_ref[at, place_y, 0, plan.planes : plan.planes + 1, :]
        for slot in range(per_row):
            row = at * per_row + slot
            mine = shrink * roll_lanes(line, -slot * SLOT)[:, : plan.channels]
            if row < plan.channels:
                map_grad_ref[row : row + 1, :] = mine
            elif row == plan.channels:
                bias_grad_ref[...] = mine


def by_planes(plan, field, cotangent, spectral_weight, pointwise_weight, bias):
    pad = plan.plane_rows
    f32 = jnp.float32
    cell_shape = (plan.size_x, plan.size_y, 2, pad, LANES)
    mode_shape = (plan.size_x, 4 * pad + 8, LANES)
    own_shape = (plan.channels, 2, plan.blocks_z, 3 * LANES)
    groups = plan.channels // 4
    beside_shape = (2, plan.channels, groups, plan.blocks_z, LANES)
    grid_shape = field.shape

    def shape(dims, kind=f32):
        return jax.ShapeDtypeStruct(dims, kind)

    def cell_exchange(values):
        flat = values.reshape(plan.devices, 2 * pad, LANES)
        return lax.all_to_all(flat, ("gx", "gy"), 0, 0, tiled=True).reshape(cell_shape)

    def mode_exchange(values):
        return lax.all_to_all(values, "gx", 0, 0, tiled=True)

    z_high, z_low = split_table(plan.z_table(False))
    scaled_high, scaled_low = split_table(plan.z_table(True))
    z_forward = jnp.asarray(np.concatenate([z_high, z_low]))
    z_inverse = jnp.asarray(np.concatenate([z_high, z_low, z_high]))
    scaled_forward = jnp.asarray(np.concatenate([scaled_high, scaled_low]))
    scaled_inverse = jnp.asarray(np.concatenate([scaled_high, scaled_low, scaled_high]))
    forward_table, inverse_table = (jnp.asarray(table) for table in plan.plane_tables())

    lane_rows = pltpu.VMEM((plan.full_x * pad, LANES), f32)
    lane_modes = pltpu.VMEM((plan.width_x * pad, LANES), f32)
    rest = pltpu.VMEM((plan.size_x, 2 * pad, LANES), f32)
    own_full = pltpu.VMEM(own_shape[:3] + (2 * LANES,), f32)
    tails = pltpu.VMEM(own_shape[:3] + (LANES,), f32)
    group_tails = pltpu.VMEM((groups,) + own_shape[1:3] + (LANES,), f32)
    lines = pltpu.VMEM((plan.channels, 2 * MZ, LANES), f32)
    wide = plan.channels * plan.rows_y
    row_shape = shape((8, LANES))

    blocks_sent = pltpu.SemaphoreType.DMA((4, plan.part_c))

    held_weights = [
        pltpu.VMEM(spectral_weight.shape[:4] + (2 * LANES,), spectral_weight.dtype),
        pltpu.VMEM(beside_shape, jnp.bfloat16),
        pltpu.SemaphoreType.DMA((CHUNKS + 1,)),
    ]

    held_grid = pltpu.VMEM(grid_shape, jnp.bfloat16)

    def in_hbm(struct):
        return pltpu.HBM(struct.shape, struct.dtype)

    def with_plan(kernel):
        return functools.partial(kernel, plan)

    def plane_analysis(cells, extra):
        return call(
            with_plan(plane_analysis_kernel),
            shape(mode_shape),
            [lane_rows, lane_modes, rest],
            cells,
            extra,
            forward_table,
        )

    def plane_synthesis(modes, extra):
        return call(
            with_plan(plane_synthesis_kernel),
            shape(cell_shape),
            [lane_rows, lane_modes, rest],
            modes,
            extra,
            inverse_table,
        )

    with jax.named_scope("depth_analysis"):
        cells = call(
            with_plan(depth_analysis_kernel),
            in_hbm(shape(cell_shape)),
            [
                pltpu.VMEM(grid_shape, jnp.bfloat16),
                pltpu.VMEM(z_forward.shape, jnp.bfloat16),
                pltpu.VMEM(cell_shape, f32),
                pltpu.SemaphoreType.DMA((3,)),
                blocks_sent,
            ],
            field,
            z_forward,
            hbm=(0, 1),
            hbm_outs=(0,),
        )
    with jax.named_scope("cells_to_planes"):
        cells = cell_exchange(cells)
    with jax.named_scope("pointwise"):
        weights = with_layout_constraint(spectral_weight, Layout((0, 1, 2, 3, 4)))
        pointwise, nothing, beside = call(
            with_plan(pointwise_kernel),
            [in_hbm(shape(grid_shape)), row_shape, in_hbm(shape(beside_shape, jnp.bfloat16))],
            [],
            field,
            pointwise_weight,
            bias,
            weights,
            smem=(2,),
        )
    with jax.named_scope("plane_analysis"):
        modes = plane_analysis(cells, nothing)
    with jax.named_scope("planes_to_modes"):
        modes = mode_exchange(modes)
    with jax.named_scope("mix"):
        modes, spectrum = call(
            with_plan(mix_kernel),
            [shape(mode_shape), in_hbm(shape(own_shape))],
            [own_full, rest, group_tails]
            + held_weights
            + [pltpu.VMEM(own_shape, f32), pltpu.SemaphoreType.DMA],
            modes,
            weights,
            beside,
            hbm=(1, 2),
            hbm_outs=(1,),
        )
    with jax.named_scope("modes_to_planes"):
        modes = mode_exchange(modes)
    with jax.named_scope("plane_synthesis"):
        cells = plane_synthesis(modes, nothing)
    with jax.named_scope("planes_to_cells"):
        cells = cell_exchange(cells)
    with jax.named_scope("activation"):
        half_grid = shape(grid_shape, jnp.bfloat16)
        output, cells, grad_high, grad_low = call(
            with_plan(activation_kernel),
            [in_hbm(half_grid), in_hbm(shape(cell_shape)), in_hbm(half_grid), in_hbm(half_grid)],
            [lines, held_grid, pltpu.VMEM(cell_shape, f32), held_grid, held_grid, blocks_sent],
            cells,
            pointwise,
            cotangent,
            scaled_inverse,
            scaled_forward,
            hbm_outs=(0, 1, 2, 3),
        )
    with jax.named_scope("grad_cells_to_planes"):
        cells = cell_exchange(cells)
    with jax.named_scope("pointwise_grad"):
        back, sums = call(
            with_plan(pointwise_grad_kernel),
            [in_hbm(shape(grid_shape)), row_shape],
            [pltpu.VMEM((wide + 16, wide), f32)],
            field,
            grad_high,
            grad_low,
            pointwise_weight,
        )
    with jax.named_scope("grad_plane_analysis"):
        modes = plane_analysis(cells, sums)
    with jax.named_scope("grad_planes_to_modes"):
        modes = mode_exchange(modes)
    with jax.named_scope("grad_mix"):
        modes, grad_mix, sums = call(
            with_plan(mix_back_kernel),
            [in_hbm(shape(mode_shape)), in_hbm(shape(own_shape)), row_shape],
            [own_full, rest, tails]
            + held_weights
            + [group_tails, pltpu.VMEM(own_shape, f32), pltpu.SemaphoreType.DMA],
            modes,
            weights,
            beside,
            hbm=(1, 2),
            hbm_outs=(1,),
        )
    with jax.named_scope("grad_modes_to_planes"):
        modes = mode_exchange(modes)
    with jax.named_scope("grad_spectral"):
        grad_spectral, sums = weight_grad(plan, spectrum, grad_mix, sums)
    with jax.named_scope("grad_plane_synthesis"):
        cells = plane_synthesis(modes, sums)
    with jax.named_scope("grad_planes_to_cells"):
        cells = cell_exchange(cells)
    with jax.named_scope("grad_field"):
        channels = plan.channels
        grad_field, map_grad, bias_grad = call(
            with_plan(last_kernel),
            [half_grid, shape((channels, channels)), shape((1, channels))],
            [lines],
            cells,
            back,
            z_inverse,
        )
    return output, grad_field, grad_spectral, map_grad, bias_grad.reshape(channels)


def layer(field, cotangent, spectral_weight, pointwise_weight, bias):
    plan = Plan(
        field.shape, spectral_weight.shape, lax.axis_size("gx"), lax.axis_size("gy")
    )
    if plan.fits:
        return by_planes(plan, field, cotangent, spectral_weight, pointwise_weight, bias)
    return local(field, cotangent, spectral_weight, pointwise_weight, bias)


def solution(mesh):
    placed = (
        P(None, "gx", "gy", None),
        P(None, "gx", "gy", None),
        P(None, None, None, "gy", "gx"),
        P(),
        P(),
    )
    return jax.shard_map(
        layer,
        mesh=mesh,
        in_specs=placed,
        out_specs=(
            P(None, "gx", "gy", None),
            P(None, "gx", "gy", None),
            P(None, None, None, "gy", "gx"),
            P(),
            P(),
        ),
        check_vma=False,
    )
```

```python
import functools
import math

import jax
import jax.numpy as jnp
from jax import lax
import numpy as np
from jax.experimental import pallas as pl
from jax.experimental.layout import Layout, with_layout_constraint
from jax.experimental.pallas import tpu as pltpu
from jax.sharding import PartitionSpec as P

MX = 24
MY = 24
MZ = 24


PRECISE = lax.Precision.HIGHEST
TWO_PI = 2.0 * math.pi


def angles(frequencies, places, length):
    product = places[:, None] * frequencies[None, :] % length
    return product.astype(jnp.float32) * (TWO_PI / length)


def frequency(position, kept_modes, length):
    return jnp.where(position < kept_modes, position, position - 2 * kept_modes + length)


def forward_y(values, phases):
    cosine_table = jnp.cos(phases)
    sine_table = jnp.sin(phases)
    with_cos = jnp.einsum("brcxy,yj->brcxj", values, cosine_table, precision=PRECISE)
    with_sin = jnp.einsum("brcxy,yj->brcxj", values, sine_table, precision=PRECISE)
    real_part = with_cos[:, 0] + with_sin[:, 1]
    imag_part = with_cos[:, 1] - with_sin[:, 0]
    return jnp.stack([real_part, imag_part], axis=1)


def inverse_y(values, phases):
    cosine_table = jnp.cos(phases)
    sine_table = jnp.sin(phases)
    with_cos = jnp.einsum("brcxj,yj->brcxy", values, cosine_table, precision=PRECISE)
    with_sin = jnp.einsum("brcxj,yj->brcxy", values, sine_table, precision=PRECISE)
    real_part = with_cos[:, 0] - with_sin[:, 1]
    imag_part = with_sin[:, 0] + with_cos[:, 1]
    return jnp.stack([real_part, imag_part], axis=1)


def local(field, cotangent, spectral_weight, pointwise_weight, bias):
    channels, rows_x, rows_y, depth_cells = field.shape
    blocks_z = spectral_weight.shape[3]
    pair_rows = spectral_weight.shape[4]
    width_x = 2 * MX
    width_y = 2 * MY
    full_x = rows_x * lax.axis_size("gx")
    full_y = rows_y * lax.axis_size("gy")
    cell_count = float(full_x * full_y * depth_cells)
    place_x = lax.axis_index("gx")
    place_y = lax.axis_index("gy")
    own_x = place_x * rows_x + jnp.arange(rows_x, dtype=jnp.int32)
    freq_x = frequency(jnp.arange(width_x, dtype=jnp.int32), MX, full_x)
    freq_y = frequency(jnp.arange(width_y, dtype=jnp.int32), MY, full_y)
    phases_full_y = angles(freq_y, jnp.arange(full_y, dtype=jnp.int32), full_y)
    z_phases = angles(
        jnp.arange(MZ, dtype=jnp.int32), jnp.arange(depth_cells, dtype=jnp.int32), depth_cells
    )
    table_z = jnp.stack([jnp.cos(z_phases), -jnp.sin(z_phases)], axis=2).reshape(
        depth_cells, 2 * MZ
    )
    kz_own = place_y * blocks_z + jnp.arange(blocks_z, dtype=jnp.int32)
    weight_z = (jnp.where(kz_own == 0, 1.0, 2.0).astype(jnp.float32) / cell_count)[None, :, None]
    own_first = place_x * pair_rows
    flat_width = blocks_z * 2 * channels

    def kx_terms(values, places, first_pair, count):
        kx_count = min(count // width_y + 2, width_x)
        kx_first = jnp.minimum(first_pair // width_y, width_x - kx_count)
        kx_ids = kx_first + jnp.arange(kx_count, dtype=jnp.int32)
        phases = angles(frequency(kx_ids, MX, full_x), places, full_x)
        cosine_table = jnp.cos(phases)
        sine_table = jnp.sin(phases)
        real_part = jnp.einsum(
            "bcxj,xi->ijbc", values[:, 0], cosine_table, precision=PRECISE
        ) + jnp.einsum("bcxj,xi->ijbc", values[:, 1], sine_table, precision=PRECISE)
        imag_part = jnp.einsum(
            "bcxj,xi->ijbc", values[:, 1], cosine_table, precision=PRECISE
        ) - jnp.einsum("bcxj,xi->ijbc", values[:, 0], sine_table, precision=PRECISE)
        terms = jnp.stack([real_part, imag_part], axis=3).reshape(kx_count * width_y, flat_width)
        offset = first_pair - kx_first * width_y
        return lax.dynamic_slice_in_dim(terms, offset, count, 0)

    def analyze(values):
        flat = values.reshape(-1, depth_cells)
        spectra = jnp.einsum("zk,mz->km", table_z, flat, precision=PRECISE).reshape(
            2 * MZ, channels, rows_x, rows_y
        )
        columns = lax.all_to_all(spectra, "gy", split_axis=0, concat_axis=3, tiled=True)
        mode_data = forward_y(columns.reshape(blocks_z, 2, channels, rows_x, full_y), phases_full_y)
        portion = lax.all_gather(mode_data, "gx", axis=3, tiled=True)
        places = jnp.arange(portion.shape[3], dtype=jnp.int32)
        owned = kx_terms(portion, places, own_first, pair_rows)
        return jnp.transpose(owned.reshape(pair_rows, blocks_z, 2, channels), (2, 3, 1, 0))

    def synthesize(spectrum):
        portion = lax.all_gather(spectrum, "gx", axis=3, tiled=True)
        blocks = portion.reshape(2, channels, blocks_z, width_x, width_y)
        phases = angles(freq_x, own_x, full_x)
        cosine_table = jnp.cos(phases)
        sine_table = jnp.sin(phases)
        real_part = jnp.einsum(
            "cbij,xi->bcxj", blocks[0], cosine_table, precision=PRECISE
        ) - jnp.einsum("cbij,xi->bcxj", blocks[1], sine_table, precision=PRECISE)
        imag_part = jnp.einsum(
            "cbij,xi->bcxj", blocks[0], sine_table, precision=PRECISE
        ) + jnp.einsum("cbij,xi->bcxj", blocks[1], cosine_table, precision=PRECISE)
        mode_data = jnp.stack([real_part, imag_part], axis=1)
        fields = inverse_y(mode_data, phases_full_y)
        columns = lax.all_to_all(fields, "gy", split_axis=4, concat_axis=0, tiled=True)
        flat = columns.reshape(2 * MZ, -1)
        return jnp.einsum("km,zk->mz", flat, table_z, precision=PRECISE).reshape(
            channels, rows_x, rows_y, depth_cells
        )

    weights = spectral_weight.astype(jnp.float32)
    widened = field.astype(jnp.float32)
    spec_u = analyze(widened)
    mixed_re = jnp.einsum("cobp,cbp->obp", weights[0], spec_u[0], precision=PRECISE) - jnp.einsum(
        "cobp,cbp->obp", weights[1], spec_u[1], precision=PRECISE
    )
    mixed_im = jnp.einsum("cobp,cbp->obp", weights[0], spec_u[1], precision=PRECISE) + jnp.einsum(
        "cobp,cbp->obp", weights[1], spec_u[0], precision=PRECISE
    )
    mixed_modes = jnp.stack([mixed_re, mixed_im]) * weight_z
    conv = synthesize(mixed_modes)
    pointwise = jnp.dot(
        pointwise_weight.T, field.reshape(channels, -1), preferred_element_type=jnp.float32
    ).reshape(field.shape)
    preact = pointwise + bias[:, None, None, None] + conv
    activated, pullback = jax.vjp(jax.nn.gelu, preact)
    gradient = pullback(cotangent.astype(jnp.float32))[0]
    grad_mix = analyze(gradient) * weight_z
    spec_re = jnp.einsum("cobp,obp->cbp", weights[0], grad_mix[0], precision=PRECISE) + jnp.einsum(
        "cobp,obp->cbp", weights[1], grad_mix[1], precision=PRECISE
    )
    spec_im = jnp.einsum("cobp,obp->cbp", weights[0], grad_mix[1], precision=PRECISE) - jnp.einsum(
        "cobp,obp->cbp", weights[1], grad_mix[0], precision=PRECISE
    )
    grad_spec = jnp.stack([spec_re, spec_im])
    weight_re = jnp.einsum("cbp,obp->cobp", spec_u[0], grad_mix[0], precision=PRECISE) + jnp.einsum(
        "cbp,obp->cobp", spec_u[1], grad_mix[1], precision=PRECISE
    )
    weight_im = jnp.einsum("cbp,obp->cobp", spec_u[0], grad_mix[1], precision=PRECISE) - jnp.einsum(
        "cbp,obp->cobp", spec_u[1], grad_mix[0], precision=PRECISE
    )
    grad_spectral = jnp.stack([weight_re, weight_im])
    returned = synthesize(grad_spec)
    grad_flat = gradient.reshape(channels, -1)
    back_point = jnp.dot(
        pointwise_weight.astype(jnp.float32), grad_flat, precision=PRECISE
    ).reshape(field.shape)
    grad_field = (back_point + returned).astype(jnp.bfloat16)
    local_weight = jnp.dot(widened.reshape(channels, -1), grad_flat.T, precision=PRECISE)
    local_bias = jnp.sum(grad_flat, axis=1)
    summed_weight, summed_bias = lax.psum((local_weight, local_bias), ("gx", "gy"))
    shrink = cell_count ** (-0.5)
    return (
        activated.astype(jnp.bfloat16),
        grad_field,
        grad_spectral,
        summed_weight * shrink,
        summed_bias * shrink,
    )


LANES = 128
HALF = 64
SLOT = 32
CHUNKS = 5
VMEM_BYTES = 20 * 1024 * 1024


def split_table(table):
    high = table.astype(jnp.bfloat16)
    low = (table - high.astype(np.float64)).astype(jnp.bfloat16)
    return high, low


def frequency_table(kept_modes, length):
    position = np.arange(2 * kept_modes)
    return np.where(position < kept_modes, position, position - 2 * kept_modes + length)


def phase_table(frequencies, places, length):
    product = places[:, None] * frequencies[None, :] % length
    return product.astype(np.float64) * (TWO_PI / length)


def split(values):
    high = values.astype(jnp.bfloat16)
    low = (values - high.astype(jnp.float32)).astype(jnp.bfloat16)
    return high, low


def product(left, right, contract=((1,), (0,)), precision=None):
    return lax.dot_general(
        left, right, (contract, ((), ())), preferred_element_type=jnp.float32, precision=precision
    )


NT = ((1,), (1,))
TN = ((0,), (0,))


def lane_ids(rows):
    return lax.broadcasted_iota(jnp.int32, (rows, LANES), 1)


def roll_lanes(values, shift):
    shift = shift % LANES
    if shift == 0:
        return values
    return pltpu.roll(values, shift, 1)


class Plan:
    def __init__(self, field_shape, weight_shape, size_x, size_y):
        self.channels, self.rows_x, self.rows_y, self.depth = field_shape
        self.size_x, self.size_y = size_x, size_y
        self.blocks_z = weight_shape[3]
        self.pair_rows = weight_shape[4]
        self.full_x = self.rows_x * size_x
        self.full_y = self.rows_y * size_y
        self.width_x, self.width_y = 2 * MX, 2 * MY
        self.cells = self.rows_x * self.rows_y
        self.part_c, self.part_z = 0, 0
        for part_z in range(1, self.blocks_z + 1):
            part_c = size_x // part_z
            if size_x % part_z or self.blocks_z % part_z or self.channels % part_c:
                continue
            self.part_c, self.part_z = part_c, part_z
        self.fits = False
        if self.part_c == 0:
            return
        self.own_c = self.channels // self.part_c
        self.own_z = self.blocks_z // self.part_z
        self.planes = self.own_c * self.own_z
        self.plane_rows = 16
        self.own_kx = self.pair_rows // self.width_y
        self.devices = size_x * size_y
        self.fits = (
            self.cells == LANES
            and self.rows_y == 16
            and self.size_y * 2 == self.rows_x
            and self.depth % LANES == 0
            and self.planes < self.plane_rows
            and self.pair_rows % self.width_y == 0
            and self.pair_rows == 2 * LANES + 32
            and self.width_y <= HALF
            and 3 * max(self.full_x, self.width_x) <= 2 * LANES
            and size_x == 8
            and self.channels % CHUNKS == 0
            and self.channels % 4 == 0
            and self.channels <= SLOT
            and self.channels < size_x * (LANES // SLOT)
            and self.own_z * 2 * self.part_z * size_y == 2 * MZ
        )

    def z_table(self, scaled):
        kz = np.arange(MZ)
        phases = phase_table(kz, np.arange(self.depth), self.depth)
        both = np.stack([np.cos(phases), -np.sin(phases)])
        if scaled:
            cells = float(self.full_x * self.full_y * self.depth)
            both = both * (np.where(kz == 0, 1.0, 2.0) / cells)
        both = both.reshape(2, self.depth, self.size_y, self.part_z, self.own_z)
        return both.transpose(2, 3, 0, 4, 1).reshape(2 * MZ, self.depth)

    def y_tables(self):
        freq = frequency_table(MY, self.full_y)
        phases = phase_table(freq, np.arange(self.full_y), self.full_y)
        cosine, sine = np.cos(phases), np.sin(phases)
        one = np.zeros((self.size_y, 2, self.rows_y, 2, HALF))
        by_block = (self.size_y, self.rows_y, self.width_y)
        one[:, 0, :, 0, : self.width_y] = cosine.reshape(by_block)
        one[:, 1, :, 0, : self.width_y] = sine.reshape(by_block)
        one[:, 0, :, 1, : self.width_y] = -sine.reshape(by_block)
        one[:, 1, :, 1, : self.width_y] = cosine.reshape(by_block)
        one = one.reshape(LANES, LANES)
        tables = []
        for table in (one, one.T):
            high, low = split_table(table)
            top = np.concatenate([high, low], axis=1)
            bottom = np.concatenate([high, np.zeros_like(low)], axis=1)
            tables.append(np.concatenate([top, bottom], axis=0))
        return tables

    def x_tables(self):
        freq = frequency_table(MX, self.full_x)
        phases = phase_table(freq, np.arange(self.full_x), self.full_x)
        phases = phases.reshape(self.size_x, self.rows_x, self.width_x).transpose(1, 0, 2)
        phases = phases.reshape(self.full_x, self.width_x)
        cosine, sine = np.cos(phases), np.sin(phases)
        forward = np.concatenate([cosine.T, sine.T], axis=0)
        inverse = np.concatenate([cosine, sine], axis=0)
        tables = []
        for table in (forward, inverse):
            high, low = split_table(table)
            tables.append(np.concatenate([high, low, high], axis=1))
        return tables

    def plane_tables(self):
        tables = []
        for along_y, along_x in zip(self.y_tables(), self.x_tables()):
            rows, columns = along_x.shape
            spare = ((0, -rows % 16), (0, 2 * LANES - columns))
            tables.append(np.concatenate([along_y, np.pad(along_x, spare)], axis=0))
        return tables


def plane_products(table_ref, rows, columns):
    across = 2 * LANES
    return table_ref[:across], table_ref[across : across + rows, :columns]


def call(kernel, out_shape, scratch, *operands, smem=(), hbm=(), hbm_outs=()):
    operands = [
        pltpu.with_memory_space_constraint(operand, pltpu.HBM) if at in hbm else operand
        for at, operand in enumerate(operands)
    ]
    specs = []
    for at in range(len(operands)):
        space = pltpu.SMEM if at in smem else pltpu.HBM if at in hbm else pltpu.VMEM
        specs.append(pl.BlockSpec(memory_space=space))
    single = not isinstance(out_shape, (tuple, list))
    shapes = [out_shape] if single else out_shape
    outs = [
        pl.BlockSpec(memory_space=pltpu.HBM if at in hbm_outs else pltpu.VMEM)
        for at in range(len(shapes))
    ]
    return pl.pallas_call(
        kernel,
        out_shape=out_shape,
        in_specs=specs,
        out_specs=outs[0] if single else outs,
        scratch_shapes=scratch,
        compiler_params=pltpu.CompilerParams(vmem_limit_bytes=VMEM_BYTES),
    )(*operands)


def put_spectrum(plan, out_ref, channel, rows):
    block, inner = divmod(channel, plan.own_c)
    size = plan.own_z
    at = 0
    for place_y in range(plan.size_y):
        for part in range(plan.part_z):
            place_x = block * plan.part_z + part
            for which in range(2):
                out_ref[place_x, place_y, which, inner * size : (inner + 1) * size, :] = rows[
                    at : at + size
                ]
                at += size


def take_spectrum(plan, in_ref, rows_ref, channel):
    block, inner = divmod(channel, plan.own_c)
    size = plan.own_z
    at = 0
    for place_y in range(plan.size_y):
        for part in range(plan.part_z):
            place_x = block * plan.part_z + part
            for which in range(2):
                rows_ref[channel, at : at + size, :] = in_ref[
                    place_x, place_y, which, inner * size : (inner + 1) * size, :
                ]
                at += size
    return rows_ref[channel]


def clear_spare(plan, out_ref):
    zeros = jnp.zeros((plan.plane_rows - plan.planes, LANES), jnp.float32)
    for place_x in range(plan.size_x):
        for place_y in range(plan.size_y):
            for which in range(2):
                out_ref[place_x, place_y, which, plan.planes :, :] = zeros


def depth_analysis_kernel(
    plan, field_ref, table_ref, out_hbm, blocks_ref, held_ref, out_ref, arrived, sent
):
    copies = [pltpu.make_async_copy(table_ref, held_ref, arrived.at[2])]
    size = plan.channels // 2
    for part in range(2):
        mine = pl.ds(part * size, size)
        copies.append(
            pltpu.make_async_copy(field_ref.at[mine], blocks_ref.at[mine], arrived.at[part])
        )
    for copy in copies:
        copy.start()
    clear_spare(plan, out_ref)
    leaving = []
    copies[0].wait()
    table = held_ref[...]
    for channel in range(plan.channels):
        if channel % size == 0:
            copies[1 + channel // size].wait()
        block = blocks_ref[channel].reshape(plan.cells, plan.depth)
        both = product(table, block, NT)
        put_spectrum(plan, out_ref, channel, both[: 2 * MZ] + both[2 * MZ :])
        leaving += send_block(plan, channel, ((out_ref, out_hbm, plan.part_z),), sent)
    for copy in leaving:
        copy.wait()


def swap_blocks(values, block):
    values = list(values)
    lanes = lane_ids(values[0].shape[0])
    step = 1
    while step < len(values):
        low = jnp.bitwise_and(lanes, step * block) == 0
        for at in range(len(values)):
            if at & step:
                continue
            first, second = values[at], values[at + step]
            values[at] = jnp.where(low, first, roll_lanes(second, step * block))
            values[at + step] = jnp.where(low, roll_lanes(first, -step * block), second)
        step *= 2
    return values


def along_y(values, table):
    high, low = split(values)
    both = product(jnp.concatenate([high, low], axis=1), table)
    return both[:, :LANES] + both[:, LANES:]


def plane_analysis_kernel(
    plan, in_ref, extra_ref, table_ref, out_ref, rows_ref, modes_ref, rest_ref
):
    y_table, x_table = plane_products(table_ref, 2 * plan.width_x, 3 * plan.full_x)
    pad = plan.plane_rows
    left = [
        in_ref[:, place_y, which].reshape(plan.size_x * pad, LANES)
        for place_y in range(plan.size_y)
        for which in range(2)
    ]
    rows_ref[: plan.full_x * pad, :] = along_y(
        jnp.concatenate(swap_blocks(left, plan.rows_y), axis=0), y_table
    )
    right = jnp.concatenate(
        [rows_ref[pl.ds(plane, plan.full_x, stride=pad), :] for plane in range(plan.planes)], axis=1
    )
    high, low = split(right)
    both = product(x_table, jnp.concatenate([high, high, low], axis=0))
    sign = jnp.where(lane_ids(plan.width_x) < HALF, 1.0, -1.0)
    for plane in range(plan.planes):
        mine = slice(plane * LANES, (plane + 1) * LANES)
        turned = roll_lanes(both[plan.width_x :, mine], HALF)
        modes_ref[pl.ds(plane, plan.width_x, stride=pad), :] = (
            both[: plan.width_x, mine] + sign * turned
        )
    modes_ref[pl.ds(plan.planes, plan.width_x, stride=pad), :] = jnp.zeros(
        (plan.width_x, LANES), jnp.float32
    )
    lanes = lane_ids(pad)
    width = plan.width_y
    for place_x in range(plan.size_x):
        for which in range(2):
            tiles = [None, None, None]
            for inner in range(plan.own_kx):
                kx = place_x * plan.own_kx + inner
                first = inner * width
                turned = roll_lanes(modes_ref[kx * pad : (kx + 1) * pad, :], first - which * HALF)
                tile, offset = divmod(first, LANES)
                for at in (tile, tile + 1):
                    begin = first - at * LANES
                    if begin >= LANES or begin + width <= 0:
                        continue
                    if tiles[at] is None:
                        tiles[at] = turned
                    else:
                        tiles[at] = jnp.where(lanes < begin, tiles[at], turned)
            for at in range(2):
                row = at * 2 * pad + which * pad
                out_ref[place_x, row : row + pad, :] = tiles[at]
            rest_ref[place_x, which * pad : (which + 1) * pad, :] = tiles[2]
        out_ref[place_x, 4 * pad : 4 * pad + 8, :] = pack_rest(rest_ref.at[place_x])
        out_ref[place_x, plan.planes : plan.planes + 1, :] = extra_ref[place_x : place_x + 1, :]


def pack_rest(rest_ref):
    lanes = lane_ids(8)
    packed = rest_ref[0:8, :]
    for group in range(1, 4):
        turned = roll_lanes(rest_ref[group * 8 : (group + 1) * 8, :], group * 32)
        packed = jnp.where(lanes < group * 32, packed, turned)
    return packed


def unpack_rest(packed, rest_ref, repeated=False):
    lanes = lane_ids(8)
    for group in range(4):
        turned = roll_lanes(packed, -group * 32)
        if repeated:
            turned = jnp.where(lanes < 32, turned, roll_lanes(turned, 32))
            turned = jnp.where(lanes < 64, turned, roll_lanes(turned, 64))
        rest_ref[group * 8 : (group + 1) * 8, :] = turned


def take_modes(plan, in_ref, modes_ref, rest_ref, beside_ref=None):
    pad, size = plan.plane_rows, plan.own_z
    for place_x in range(plan.size_x):
        block, part = divmod(place_x, plan.part_z)
        unpack_rest(in_ref[place_x, 4 * pad : 4 * pad + 8, :], rest_ref.at[place_x], True)
        for which in range(2):
            for inner in range(plan.own_c):
                channel = block * plan.own_c + inner
                row = which * pad + inner * size
                kz = slice(part * size, (part + 1) * size)
                for at in range(2):
                    begin = at * 2 * pad + row
                    modes_ref[channel, which, kz, at * LANES : (at + 1) * LANES] = in_ref[
                        place_x, begin : begin + size, :
                    ]
                modes_ref[channel, which, kz, 2 * LANES :] = rest_ref[place_x, row : row + size, :]
                if beside_ref is not None:
                    group, slot = divmod(channel, 4)
                    mine = slice(slot * 32, (slot + 1) * 32)
                    beside_ref[group, which, kz, mine] = rest_ref[place_x, row : row + size, mine]


def put_modes(plan, modes_ref, tail, out_ref, rest_ref):
    pad, size = plan.plane_rows, plan.own_z
    zeros = jnp.zeros((pad - plan.planes, LANES), jnp.float32)
    rest_ref[...] = jnp.zeros(rest_ref.shape, jnp.float32)
    for place_x in range(plan.size_x):
        block, part = divmod(place_x, plan.part_z)
        for which in range(2):
            for inner in range(plan.own_c):
                channel = block * plan.own_c + inner
                row = which * pad + inner * size
                kz = slice(part * size, (part + 1) * size)
                for at in range(2):
                    begin = at * 2 * pad + row
                    out_ref[place_x, begin : begin + size, :] = modes_ref[
                        channel, which, kz, at * LANES : (at + 1) * LANES
                    ]
                rest_ref[place_x, row : row + size, 0:32] = tail(channel, which)[kz, 0:32]
            for at in range(2):
                begin = at * 2 * pad + which * pad + plan.planes
                out_ref[place_x, begin : begin + pad - plan.planes, :] = zeros
        out_ref[place_x, 4 * pad : 4 * pad + 8, :] = pack_rest(rest_ref.at[place_x])


def bring_weights(plan, weight_hbm, weight_ref, beside_hbm, beside_ref, arrived, by_input):
    full = pl.ds(0, 2 * LANES)
    size = plan.channels // CHUNKS
    copies = [pltpu.make_async_copy(beside_hbm, beside_ref, arrived.at[CHUNKS])]
    for chunk in range(CHUNKS):
        mine = pl.ds(chunk * size, size)
        whole = slice(None)
        source = (whole, mine) if by_input else (whole, whole, mine)
        source = source + (whole,) * (4 - len(source)) + (full,)
        target = source[:4]
        copies.append(
            pltpu.make_async_copy(weight_hbm.at[source], weight_ref.at[target], arrived.at[chunk])
        )
    for copy in copies:
        copy.start()
    return copies


def add_product(sums, weight_re, weight_im, value_re, value_im, back):
    weight_re = weight_re.astype(jnp.float32)
    weight_im = weight_im.astype(jnp.float32)
    if back:
        return (
            sums[0] + (weight_re * value_re + weight_im * value_im),
            sums[1] + (weight_re * value_im - weight_im * value_re),
        )
    return (
        sums[0] + (weight_re * value_re - weight_im * value_im),
        sums[1] + (weight_re * value_im + weight_im * value_re),
    )


def mix_kernel(
    plan,
    in_ref,
    weight_hbm,
    beside_hbm,
    out_ref,
    spectrum_hbm,
    mixed_ref,
    rest_ref,
    tails_ref,
    weight_ref,
    beside_ref,
    arrived,
    spectrum_ref,
    sent,
):
    copies = bring_weights(plan, weight_hbm, weight_ref, beside_hbm, beside_ref, arrived, False)
    take_modes(plan, in_ref, spectrum_ref, rest_ref)
    leaving = pltpu.make_async_copy(spectrum_ref, spectrum_hbm, sent)
    leaving.start()
    full, end = slice(0, 2 * LANES), slice(2 * LANES, 3 * LANES)
    size = plan.channels // CHUNKS
    copies[0].wait()
    for chunk, copy in enumerate(copies[1:]):
        copy.wait()
        for out_channel in range(chunk * size, (chunk + 1) * size):
            zeros = jnp.zeros((plan.blocks_z, 2 * LANES), jnp.float32)
            sums = (zeros, zeros)
            for channel in range(plan.channels):
                sums = add_product(
                    sums,
                    weight_ref[0, channel, out_channel],
                    weight_ref[1, channel, out_channel],
                    spectrum_ref[channel, 0, :, full],
                    spectrum_ref[channel, 1, :, full],
                    False,
                )
            mixed_ref[out_channel, 0], mixed_ref[out_channel, 1] = sums
    for group in range(plan.channels // 4):
        zeros = jnp.zeros((plan.blocks_z, LANES), jnp.float32)
        sums = (zeros, zeros)
        for channel in range(plan.channels):
            sums = add_product(
                sums,
                beside_ref[0, channel, group],
                beside_ref[1, channel, group],
                spectrum_ref[channel, 0, :, end],
                spectrum_ref[channel, 1, :, end],
                False,
            )
        tails_ref[group, 0], tails_ref[group, 1] = sums

    def tail(channel, which):
        group, slot = divmod(channel, 4)
        return roll_lanes(tails_ref[group, which], -slot * 32)

    put_modes(plan, mixed_ref, tail, out_ref, rest_ref)
    leaving.wait()


def mix_back_kernel(
    plan,
    in_ref,
    weight_hbm,
    beside_hbm,
    out_ref,
    grad_hbm,
    sums_ref,
    mixed_ref,
    rest_ref,
    tails_ref,
    weight_ref,
    beside_ref,
    arrived,
    grad_beside_ref,
    grad_ref,
    sent,
):
    copies = bring_weights(plan, weight_hbm, weight_ref, beside_hbm, beside_ref, arrived, True)
    spare = jnp.zeros((1, LANES), jnp.float32)
    for place_x in range(plan.size_x):
        spare = spare + in_ref[place_x, plan.planes : plan.planes + 1, :]
    sums_ref[...] = jnp.broadcast_to(spare, (8, LANES))
    take_modes(plan, in_ref, grad_ref, rest_ref, grad_beside_ref)
    leaving = pltpu.make_async_copy(grad_ref, grad_hbm, sent)
    leaving.start()
    full = slice(0, 2 * LANES)
    size = plan.channels // CHUNKS
    copies[0].wait()
    for chunk, copy in enumerate(copies[1:]):
        copy.wait()
        for channel in range(chunk * size, (chunk + 1) * size):
            zeros = jnp.zeros((plan.blocks_z, 2 * LANES), jnp.float32)
            sums = (zeros, zeros)
            for out_channel in range(plan.channels):
                sums = add_product(
                    sums,
                    weight_ref[0, channel, out_channel],
                    weight_ref[1, channel, out_channel],
                    grad_ref[out_channel, 0, :, full],
                    grad_ref[out_channel, 1, :, full],
                    True,
                )
            mixed_ref[channel, 0], mixed_ref[channel, 1] = sums
            zeros = jnp.zeros((plan.blocks_z, LANES), jnp.float32)
            sums = (zeros, zeros)
            for group in range(plan.channels // 4):
                sums = add_product(
                    sums,
                    beside_ref[0, channel, group],
                    beside_ref[1, channel, group],
                    grad_beside_ref[group, 0],
                    grad_beside_ref[group, 1],
                    True,
                )
            for which in range(2):
                total = sums[which] + roll_lanes(sums[which], 64)
                tails_ref[channel, which] = total + roll_lanes(total, 32)

    def tail(channel, which):
        return tails_ref[channel, which]

    put_modes(plan, mixed_ref, tail, out_ref, rest_ref)
    leaving.wait()


def weight_grad_kernel(plan, spectrum_ref, grad_ref, before_ref, out_ref, after_ref):
    after_ref[...] = before_ref[...]
    kept = slice(0, plan.pair_rows)
    for channel in range(spectrum_ref.shape[0]):
        for out_channel in range(plan.channels):
            for kz in range(plan.blocks_z):
                row = slice(kz, kz + 1)
                value_re = spectrum_ref[channel, 0, row, kept]
                value_im = spectrum_ref[channel, 1, row, kept]
                grad_re = grad_ref[out_channel, 0, row, kept]
                grad_im = grad_ref[out_channel, 1, row, kept]
                out_ref[channel, out_channel, kz, 0:1, :] = value_re * grad_re + value_im * grad_im
                out_ref[channel, out_channel, kz, 1:2, :] = value_re * grad_im - value_im * grad_re


def weight_grad(plan, spectrum, grad, before):
    own = (plan.blocks_z, 2, plan.pair_rows)
    wide = (plan.blocks_z, 3 * LANES)
    step = 4
    rows, after = pl.pallas_call(
        functools.partial(weight_grad_kernel, plan),
        grid=(plan.channels // step,),
        out_shape=[
            pltpu.HBM((plan.channels, plan.channels) + own, jnp.float32),
            jax.ShapeDtypeStruct(before.shape, before.dtype),
        ],
        in_specs=[
            pl.BlockSpec((step, 2) + wide, lambda at: (at, 0, 0, 0)),
            pl.BlockSpec((plan.channels, 2) + wide, lambda at: (0, 0, 0, 0)),
            pl.BlockSpec(before.shape, lambda at: (0, 0)),
        ],
        out_specs=[
            pl.BlockSpec((step, plan.channels) + own, lambda at: (at, 0, 0, 0, 0)),
            pl.BlockSpec(before.shape, lambda at: (0, 0)),
        ],
        compiler_params=pltpu.CompilerParams(vmem_limit_bytes=VMEM_BYTES),
    )(
        pltpu.with_memory_space_constraint(spectrum, pltpu.HBM),
        pltpu.with_memory_space_constraint(grad, pltpu.HBM),
        before,
    )
    return jnp.transpose(rows, (3, 0, 1, 2, 4)), after


def plane_synthesis_kernel(
    plan, in_ref, extra_ref, table_ref, out_ref, rows_ref, modes_ref, rest_ref
):
    y_table, x_table = plane_products(table_ref, 2 * plan.full_x, 3 * plan.width_x)
    pad, width = plan.plane_rows, plan.width_y
    lanes = lane_ids(pad)
    for place_x in range(plan.size_x):
        unpack_rest(in_ref[place_x, 4 * pad : 4 * pad + 8, :], rest_ref.at[place_x])
        tiles = []
        for which in range(2):
            row = which * pad
            tiles.append(
                [
                    in_ref[place_x, row : row + pad, :],
                    in_ref[place_x, 2 * pad + row : 3 * pad + row, :],
                    rest_ref[place_x, row : row + pad, :],
                ]
            )
        for inner in range(plan.own_kx):
            first = inner * width
            tile, offset = divmod(first, LANES)
            pieces = []
            for which in range(2):
                piece = roll_lanes(tiles[which][tile], which * HALF - offset)
                if offset + width > LANES:
                    later = roll_lanes(tiles[which][tile + 1], which * HALF - offset)
                    piece = jnp.where(lanes < which * HALF + LANES - offset, piece, later)
                pieces.append(piece)
            merged = jnp.where(lanes < HALF, pieces[0], pieces[1])
            used = jnp.bitwise_and(lanes, HALF - 1) < width
            at = (place_x * plan.own_kx + inner) * pad
            modes_ref[at : at + pad, :] = jnp.where(used, merged, 0.0)
    right = jnp.concatenate(
        [modes_ref[pl.ds(plane, plan.width_x, stride=pad), :] for plane in range(plan.planes)],
        axis=1,
    )
    high, low = split(right)
    both = product(x_table, jnp.concatenate([high, high, low], axis=0))
    sign = jnp.where(lane_ids(plan.full_x) < HALF, -1.0, 1.0)
    for plane in range(plan.planes):
        mine = slice(plane * LANES, (plane + 1) * LANES)
        turned = roll_lanes(both[plan.full_x :, mine], HALF)
        rows_ref[pl.ds(plane, plan.full_x, stride=pad), :] = (
            both[: plan.full_x, mine] + sign * turned
        )
    rows_ref[pl.ds(plan.planes, plan.full_x, stride=pad), :] = jnp.zeros(
        (plan.full_x, LANES), jnp.float32
    )
    cells = along_y(rows_ref[: plan.full_x * pad, :], y_table)
    size = plan.size_x * pad
    cells = swap_blocks(
        [cells[row * size : (row + 1) * size] for row in range(plan.rows_x)], plan.rows_y
    )
    for place_y in range(plan.size_y):
        for which in range(2):
            out_ref[:, place_y, which] = cells[place_y * 2 + which].reshape(
                plan.size_x, pad, LANES
            )
    spare = extra_ref[0:1, :]
    for place_x in range(plan.size_x):
        for place_y in range(plan.size_y):
            out_ref[place_x, place_y, 0, plan.planes : plan.planes + 1, :] = spare


def widen_map(plan, small, transposed):
    rows = plan.channels * plan.rows_y
    row_ids = lax.broadcasted_iota(jnp.int32, (rows, plan.channels), 0)
    column_ids = lax.broadcasted_iota(jnp.int32, (rows, plan.channels), 1)
    spread = jnp.where(row_ids // plan.rows_y == column_ids, 1.0, 0.0).astype(jnp.bfloat16)
    wide = product(spread, small, ((1,), (0,)) if transposed else ((1,), (1,)))
    wide = product(wide.astype(jnp.bfloat16), spread, NT)
    return jnp.where(same_cell(plan), wide, 0.0).astype(jnp.bfloat16)


def same_cell(plan):
    rows = plan.channels * plan.rows_y
    row_ids = lax.broadcasted_iota(jnp.int32, (rows, rows), 0)
    column_ids = lax.broadcasted_iota(jnp.int32, (rows, rows), 1)
    return jnp.bitwise_and(row_ids, plan.rows_y - 1) == jnp.bitwise_and(
        column_ids, plan.rows_y - 1
    )


def depth_rows(plan, in_ref, rows_ref, channel):
    rows = take_spectrum(plan, in_ref, rows_ref, channel)
    high, low = split(rows)
    return jnp.concatenate([high, high, low], axis=0)


def pointwise_kernel(
    plan, field_ref, map_ref, bias_ref, weight_ref, out_ref, nothing_ref, beside_ref
):
    def beside(channel, carry):
        for which in range(2):
            for group in range(plan.channels // 4):
                parts = [
                    weight_ref[which, channel, group * 4 + slot, :, 2 * LANES :]
                    for slot in range(4)
                ]
                beside_ref[which, channel, group] = jnp.concatenate(
                    [part.astype(jnp.float32) for part in parts], axis=1
                ).astype(jnp.bfloat16)
        return carry

    lax.fori_loop(0, plan.channels, beside, 0)
    nothing_ref[...] = jnp.zeros((8, LANES), jnp.float32)
    rows, size = plan.channels * plan.rows_y, plan.rows_y
    wide = widen_map(plan, map_ref[...], False)

    def one(row, carry):
        here = pl.ds(row, 1)
        mapped = product(wide, field_ref[:, here].reshape(rows, plan.depth))
        for channel in range(plan.channels):
            part = mapped[channel * size : (channel + 1) * size] + bias_ref[channel]
            out_ref[channel, here] = part.reshape(1, size, plan.depth)
        return carry

    lax.fori_loop(0, plan.rows_x, one, 0)


def activation_kernel(
    plan,
    in_ref,
    pointwise_ref,
    cotangent_ref,
    inverse_ref,
    forward_ref,
    output_hbm,
    spectrum_hbm,
    high_hbm,
    low_hbm,
    rows_ref,
    output_ref,
    spectrum_ref,
    high_ref,
    low_ref,
    sent,
):
    pairs = (
        (spectrum_ref, spectrum_hbm, plan.part_z),
        (output_ref, output_hbm, plan.own_c),
        (high_ref, high_hbm, plan.own_c),
        (low_ref, low_hbm, plan.own_c),
    )
    copies = []
    clear_spare(plan, spectrum_ref)
    flat = (plan.cells, plan.depth)
    block = (plan.rows_x, plan.rows_y, plan.depth)
    inverse = inverse_ref[...]
    forward = forward_ref[...]
    scale = math.sqrt(2.0 / math.pi)
    for channel in range(plan.channels):
        if channel % plan.own_c == 0:
            left = [
                depth_rows(plan, in_ref, rows_ref, channel + inner)
                for inner in range(plan.own_c)
            ]
            conv = product(jnp.concatenate(left, axis=1), inverse, TN)
        first = channel % plan.own_c * plan.cells
        preact = conv[first : first + plan.cells] + pointwise_ref[channel].reshape(flat)
        square = preact * preact
        bend = jnp.tanh(preact * (scale + (scale * 0.044715) * square))
        half = 0.5 + 0.5 * bend
        active = preact * half
        output_ref[channel] = active.astype(jnp.bfloat16).reshape(block)
        slope = half + active * (1.0 - half) * (
            2.0 * scale + (6.0 * scale * 0.044715) * square
        )
        grad = cotangent_ref[channel].reshape(flat).astype(jnp.float32) * slope
        high, low = split(grad)
        high_ref[channel] = high.reshape(block)
        low_ref[channel] = low.reshape(block)
        both = product(forward, high, NT)
        more = product(forward[: 2 * MZ], low, NT)
        put_spectrum(plan, spectrum_ref, channel, both[: 2 * MZ] + both[2 * MZ :] + more)
        copies += send_block(plan, channel, pairs, sent)
    for copy in copies:
        copy.wait()


def send_block(plan, channel, pairs, sent):
    block, inner = divmod(channel, plan.own_c)
    if inner < plan.own_c - 1:
        return []
    copies = []
    for at, (held, target, size) in enumerate(pairs):
        mine = pl.ds(block * size, size)
        copies.append(pltpu.make_async_copy(held.at[mine], target.at[mine], sent.at[at, block]))
    for copy in copies:
        copy.start()
    return copies


def pointwise_grad_kernel(
    plan, field_ref, high_ref, low_ref, map_ref, back_ref, sums_ref, cross_ref
):
    rows = plan.channels * plan.rows_y
    wide = widen_map(plan, map_ref[...], True)
    cross_ref[...] = jnp.zeros((rows + 16, rows), jnp.float32)
    ones = jnp.ones((16, plan.depth), jnp.bfloat16)
    slab = (plan.channels, 1, plan.rows_y, plan.depth)

    def one(row, carry):
        here = pl.ds(row, 1)
        values = field_ref[:, here].reshape(rows, plan.depth)
        values = jnp.concatenate([values, ones], axis=0)
        high = high_ref[:, here].reshape(rows, plan.depth)
        low = low_ref[:, here].reshape(rows, plan.depth)
        back_ref[:, here] = (product(wide, high) + product(wide, low)).reshape(slab)
        cross_ref[...] += product(values, high, NT) + product(values, low, NT)
        return carry

    lax.fori_loop(0, plan.rows_x, one, 0)
    row_ids = lax.broadcasted_iota(jnp.int32, (rows, LANES), 0)
    gather = jnp.where(row_ids // plan.rows_y == lane_ids(rows), 1.0, 0.0)
    exact = lax.Precision.HIGHEST
    cross = jnp.where(same_cell(plan), cross_ref[:rows], 0.0)
    by_out = product(cross, gather, precision=exact)
    sums = product(gather, by_out, TN, precision=exact)
    bias_sums = product(cross_ref[rows : rows + 8], gather, precision=exact)
    lanes = lane_ids(1)
    per_row = LANES // SLOT
    for at in range(8):
        packed = jnp.zeros((1, LANES), jnp.float32)
        for slot in range(per_row):
            row = at * per_row + slot
            if row > plan.channels:
                continue
            line = sums[row : row + 1] if row < plan.channels else bias_sums[0:1]
            packed = jnp.where(lanes // SLOT == slot, roll_lanes(line, slot * SLOT), packed)
        sums_ref[at : at + 1, :] = packed


def last_kernel(
    plan,
    in_ref,
    back_ref,
    inverse_ref,
    grad_ref,
    map_grad_ref,
    bias_grad_ref,
    rows_ref,
):
    block = (plan.rows_x, plan.rows_y, plan.depth)
    flat = (plan.cells, plan.depth)
    inverse = inverse_ref[...]
    for channel in range(plan.channels):
        total = product(depth_rows(plan, in_ref, rows_ref, channel), inverse, TN)
        total = total + back_ref[channel].reshape(flat)
        grad_ref[channel] = total.astype(jnp.bfloat16).reshape(block)
    shrink = float(plan.full_x * plan.full_y * plan.depth) ** (-0.5)
    per_row = LANES // SLOT
    for at in range(plan.size_x):
        line = jnp.zeros((1, LANES), jnp.float32)
        for place_y in range(plan.size_y):
            line = line + in_ref[at, place_y, 0, plan.planes : plan.planes + 1, :]
        for slot in range(per_row):
            row = at * per_row + slot
            mine = shrink * roll_lanes(line, -slot * SLOT)[:, : plan.channels]
            if row < plan.channels:
                map_grad_ref[row : row + 1, :] = mine
            elif row == plan.channels:
                bias_grad_ref[...] = mine


def by_planes(plan, field, cotangent, spectral_weight, pointwise_weight, bias):
    pad = plan.plane_rows
    f32 = jnp.float32
    cell_shape = (plan.size_x, plan.size_y, 2, pad, LANES)
    mode_shape = (plan.size_x, 4 * pad + 8, LANES)
    own_shape = (plan.channels, 2, plan.blocks_z, 3 * LANES)
    groups = plan.channels // 4
    beside_shape = (2, plan.channels, groups, plan.blocks_z, LANES)
    grid_shape = field.shape

    def shape(dims, kind=f32):
        return jax.ShapeDtypeStruct(dims, kind)

    def cell_exchange(values):
        flat = values.reshape(plan.devices, 2 * pad, LANES)
        return lax.all_to_all(flat, ("gx", "gy"), 0, 0, tiled=True).reshape(cell_shape)

    def mode_exchange(values):
        return lax.all_to_all(values, "gx", 0, 0, tiled=True)

    z_high, z_low = split_table(plan.z_table(False))
    scaled_high, scaled_low = split_table(plan.z_table(True))
    z_forward = jnp.asarray(np.concatenate([z_high, z_low]))
    z_inverse = jnp.asarray(np.concatenate([z_high, z_low, z_high]))
    scaled_forward = jnp.asarray(np.concatenate([scaled_high, scaled_low]))
    scaled_inverse = jnp.asarray(np.concatenate([scaled_high, scaled_low, scaled_high]))
    forward_table, inverse_table = (jnp.asarray(table) for table in plan.plane_tables())

    lane_rows = pltpu.VMEM(((plan.full_x + 1) * pad, LANES), f32)
    lane_modes = pltpu.VMEM(((plan.width_x + 1) * pad, LANES), f32)
    rest = pltpu.VMEM((plan.size_x, 2 * pad, LANES), f32)
    own_full = pltpu.VMEM(own_shape[:3] + (2 * LANES,), f32)
    tails = pltpu.VMEM(own_shape[:3] + (LANES,), f32)
    group_tails = pltpu.VMEM((groups,) + own_shape[1:3] + (LANES,), f32)
    lines = pltpu.VMEM((plan.channels, 2 * MZ, LANES), f32)
    wide = plan.channels * plan.rows_y
    row_shape = shape((8, LANES))

    blocks_sent = pltpu.SemaphoreType.DMA((4, plan.part_c))

    held_weights = [
        pltpu.VMEM(spectral_weight.shape[:4] + (2 * LANES,), spectral_weight.dtype),
        pltpu.VMEM(beside_shape, jnp.bfloat16),
        pltpu.SemaphoreType.DMA((CHUNKS + 1,)),
    ]

    held_grid = pltpu.VMEM(grid_shape, jnp.bfloat16)

    def in_hbm(struct):
        return pltpu.HBM(struct.shape, struct.dtype)

    def with_plan(kernel):
        return functools.partial(kernel, plan)

    def plane_analysis(cells, extra):
        return call(
            with_plan(plane_analysis_kernel),
            shape(mode_shape),
            [lane_rows, lane_modes, rest],
            cells,
            extra,
            forward_table,
        )

    def plane_synthesis(modes, extra):
        return call(
            with_plan(plane_synthesis_kernel),
            shape(cell_shape),
            [lane_rows, lane_modes, rest],
            modes,
            extra,
            inverse_table,
        )

    with jax.named_scope("depth_analysis"):
        cells = call(
            with_plan(depth_analysis_kernel),
            in_hbm(shape(cell_shape)),
            [
                pltpu.VMEM(grid_shape, jnp.bfloat16),
                pltpu.VMEM(z_forward.shape, jnp.bfloat16),
                pltpu.VMEM(cell_shape, f32),
                pltpu.SemaphoreType.DMA((3,)),
                blocks_sent,
            ],
            field,
            z_forward,
            hbm=(0, 1),
            hbm_outs=(0,),
        )
    with jax.named_scope("cells_to_planes"):
        cells = cell_exchange(cells)
    with jax.named_scope("pointwise"):
        weights = with_layout_constraint(spectral_weight, Layout((0, 1, 2, 3, 4)))
        pointwise, nothing, beside = call(
            with_plan(pointwise_kernel),
            [in_hbm(shape(grid_shape)), row_shape, in_hbm(shape(beside_shape, jnp.bfloat16))],
            [],
            field,
            pointwise_weight,
            bias,
            weights,
            smem=(2,),
        )
    with jax.named_scope("plane_analysis"):
        modes = plane_analysis(cells, nothing)
    with jax.named_scope("planes_to_modes"):
        modes = mode_exchange(modes)
    with jax.named_scope("mix"):
        modes, spectrum = call(
            with_plan(mix_kernel),
            [shape(mode_shape), in_hbm(shape(own_shape))],
            [own_full, rest, group_tails]
            + held_weights
            + [pltpu.VMEM(own_shape, f32), pltpu.SemaphoreType.DMA],
            modes,
            weights,
            beside,
            hbm=(1, 2),
            hbm_outs=(1,),
        )
    with jax.named_scope("modes_to_planes"):
        modes = mode_exchange(modes)
    with jax.named_scope("plane_synthesis"):
        cells = plane_synthesis(modes, nothing)
    with jax.named_scope("planes_to_cells"):
        cells = cell_exchange(cells)
    with jax.named_scope("activation"):
        half_grid = shape(grid_shape, jnp.bfloat16)
        output, cells, grad_high, grad_low = call(
            with_plan(activation_kernel),
            [in_hbm(half_grid), in_hbm(shape(cell_shape)), in_hbm(half_grid), in_hbm(half_grid)],
            [lines, held_grid, pltpu.VMEM(cell_shape, f32), held_grid, held_grid, blocks_sent],
            cells,
            pointwise,
            cotangent,
            scaled_inverse,
            scaled_forward,
            hbm_outs=(0, 1, 2, 3),
        )
    with jax.named_scope("grad_cells_to_planes"):
        cells = cell_exchange(cells)
    with jax.named_scope("pointwise_grad"):
        back, sums = call(
            with_plan(pointwise_grad_kernel),
            [in_hbm(shape(grid_shape)), row_shape],
            [pltpu.VMEM((wide + 16, wide), f32)],
            field,
            grad_high,
            grad_low,
            pointwise_weight,
        )
    with jax.named_scope("grad_plane_analysis"):
        modes = plane_analysis(cells, sums)
    with jax.named_scope("grad_planes_to_modes"):
        modes = mode_exchange(modes)
    with jax.named_scope("grad_mix"):
        modes, grad_mix, sums = call(
            with_plan(mix_back_kernel),
            [in_hbm(shape(mode_shape)), in_hbm(shape(own_shape)), row_shape],
            [own_full, rest, tails]
            + held_weights
            + [group_tails, pltpu.VMEM(own_shape, f32), pltpu.SemaphoreType.DMA],
            modes,
            weights,
            beside,
            hbm=(1, 2),
            hbm_outs=(1,),
        )
    with jax.named_scope("grad_modes_to_planes"):
        modes = mode_exchange(modes)
    with jax.named_scope("grad_spectral"):
        grad_spectral, sums = weight_grad(plan, spectrum, grad_mix, sums)
    with jax.named_scope("grad_plane_synthesis"):
        cells = plane_synthesis(modes, sums)
    with jax.named_scope("grad_planes_to_cells"):
        cells = cell_exchange(cells)
    with jax.named_scope("grad_field"):
        channels = plan.channels
        grad_field, map_grad, bias_grad = call(
            with_plan(last_kernel),
            [half_grid, shape((channels, channels)), shape((1, channels))],
            [lines],
            cells,
            back,
            z_inverse,
        )
    return output, grad_field, grad_spectral, map_grad, bias_grad.reshape(channels)


def layer(field, cotangent, spectral_weight, pointwise_weight, bias):
    plan = Plan(
        field.shape, spectral_weight.shape, lax.axis_size("gx"), lax.axis_size("gy")
    )
    if plan.fits:
        return by_planes(plan, field, cotangent, spectral_weight, pointwise_weight, bias)
    return local(field, cotangent, spectral_weight, pointwise_weight, bias)


def solution(mesh):
    placed = (
        P(None, "gx", "gy", None),
        P(None, "gx", "gy", None),
        P(None, None, None, "gy", "gx"),
        P(),
        P(),
    )
    return jax.shard_map(
        layer,
        mesh=mesh,
        in_specs=placed,
        out_specs=(
            P(None, "gx", "gy", None),
            P(None, "gx", "gy", None),
            P(None, None, None, "gy", "gx"),
            P(),
            P(),
        ),
        check_vma=False,
    )
```
